128 devices in a mesh: member: 32 (over z, y_hi, x), tensor: 4 (over y_lo, core).
Axes of the slice: x: 4, y: 4 (y_hi: 2, y_lo: 2; y = y_hi * 2 + y_lo), z: 4, core: 2. Of those that a mesh axis runs over, the one named last changes fastest.
Arguments:
- series: float32 [16384], replicated, may hold values from -8 to 8
- starts: int32 [128], replicated, may hold values from 0 to 16216
- counts: int32 [32, 128], P(None, 'member'), may hold values from 0 to 3
- segment_lifting_matrix: float32 [32, 16, 2048], P('member', None, 'tensor')
- location_vector: float32 [32, 8, 2048], P('member', None, 'tensor'), may hold values from -8 to 8
- prelude_scaling_factor: float32 [32, 2048], P('member', 'tensor'), may hold values from 0.1 to 1.9
- expanding_matrix: bfloat16 [32, 2048, 8192], P('member', None, 'tensor'), may hold values from -0.125 to 0.125
- contracting_matrix: bfloat16 [32, 8192, 2048], P('member', 'tensor'), may hold values from -0.125 to 0.125
- final_scaling_factor: float32 [32, 2048], P('member', 'tensor'), may hold values from 0.1 to 1.9
- readout_matrix: bfloat16 [32, 8, 2048, 96], P('member', None, 'tensor'), may hold values from -0.1875 to 0.1875
Outputs:
- resampled_average_prediction: float32 [128, 96], P('member', 'tensor')
- error_percentiles: float32 [4, 96], P(None, 'tensor')
The draws below stay inside these ranges and needn't reach their ends.
All inputs are finite; a program needn't handle non-finite values.
Results may differ from the reference program's by a relative error of at most 0.012.
Values may be sent and summed in bfloat16 or wider, within the bound.
No kernel may reach another device: no remote copies, remote signals or barrier semaphores. Data moves between devices by JAX's collectives and lax.ppermute only.
A program may use at most 128 MiB of HBM per device.

```python
import math
import jax
import jax.numpy as jnp
from jax import lax

D = 2048
FF = 8192
H = 96
P_SIZE = 8
PLEN = 16
STRIDE = 8
SERIES = 16384
MEMBERS = 32
WINDOWS = 128
LOOK = 72


def draw_segment_lifting_matrix(key, part):
    key = jax.random.fold_in(key, 11)
    base_key, scale_key = jax.random.split(key)
    ramp = jnp.exp(math.log(3.0) * jnp.arange(D, dtype=jnp.float32) / D)
    base = jax.random.normal(base_key, (MEMBERS, PLEN, D), jnp.float32)
    column = jnp.exp(jax.random.uniform(scale_key, (D,), jnp.float32, 0.0, math.log(3.5)))
    return base * (ramp * column)[None, None, :] * PLEN ** (-0.5)


def place_ends(entries, stream_key, low, top_value):
    dims = entries.shape
    index_at = [jax.random.randint(jax.random.fold_in(stream_key, axis), (), 0, dims[axis]) for axis in range(len(dims))]
    entries = entries.at[tuple(index_at)].set(low)
    longest = dims.index(max(dims))
    index_at[longest] = (index_at[longest] + 1) % dims[longest]
    return entries.at[tuple(index_at)].set(top_value)


def steps_of(stream_key, extent, cuts, low, top_value):
    def one(dim, blocks):
        steps = jax.random.uniform(jax.random.fold_in(jax.random.fold_in(stream_key, 6), dim), (blocks,), jnp.float32, low / len(cuts), top_value / len(cuts))
        return jnp.repeat(jnp.exp(steps), extent[dim] // blocks).reshape((-1,) + (1,) * (len(extent) - dim - 1))

    factor_of = one(*cuts[0])
    for cut in cuts[1:]:
        factor_of = factor_of * one(*cut)
    return factor_of


def normal_values(own_key, shape, scale, most, cuts=(), held_as=jnp.bfloat16):
    entries = scale * jax.random.normal(own_key, shape, jnp.float32)
    if cuts:
        entries = entries * steps_of(own_key, shape, cuts, -0.22, 0.18)
    return jnp.clip(entries, -most, most).astype(held_as)


def setup_inputs(seed: int = 0) -> dict:
    seeds = jax.random.split(jax.random.key(seed), 11)
    return {
        "series": normal_values(seeds[0], (SERIES,), 2.0, 8.0, (), jnp.float32),
        "starts": place_ends(jax.random.randint(seeds[1], (WINDOWS,), 0, SERIES - LOOK - H + 1), jax.random.fold_in(seeds[1], 1), 0, SERIES - LOOK - H).astype(jnp.int32),
        "counts": place_ends(jax.random.randint(seeds[2], (MEMBERS, WINDOWS), 0, 4), jax.random.fold_in(seeds[2], 1), 0, 3).astype(jnp.int32),
        "segment_lifting_matrix": draw_segment_lifting_matrix(jax.random.fold_in(seeds[10], 71), 0),
        "location_vector": normal_values(seeds[4], (MEMBERS, P_SIZE, D), 2.0, 8.0, ((0, 32), (2, 4)), jnp.float32),
        "prelude_scaling_factor": jnp.clip(1.0 + 0.18 * jax.random.normal(seeds[5], (MEMBERS, D), jnp.float32), 0.1, 1.9),
        "expanding_matrix": normal_values(seeds[6], (MEMBERS, D, FF), D ** -0.5, 0.125, ((0, 32), (2, 4))),
        "contracting_matrix": normal_values(seeds[7], (MEMBERS, FF, D), (FF // 4) ** -0.5, 0.125, ((0, 32), (1, 4))),
        "final_scaling_factor": jnp.clip(1.0 + 0.18 * jax.random.normal(seeds[8], (MEMBERS, D), jnp.float32), 0.1, 1.9),
        "readout_matrix": normal_values(seeds[9], (MEMBERS, P_SIZE, D, H), (P_SIZE * D // 16) ** -0.5, 0.1875, ((0, 32), (2, 4))),
    }


def layer_norm(values, gain):
    middle_location = lax.optimization_barrier(jnp.mean(values, axis=-1, keepdims=True))
    deviation = values - middle_location
    variance = lax.optimization_barrier(jnp.mean(deviation * deviation, axis=-1, keepdims=True))
    return deviation * lax.rsqrt(variance + 1e-05) * gain

def reference(series, starts, counts, segment_lifting_matrix, location_vector, prelude_scaling_factor, expanding_matrix, contracting_matrix, final_scaling_factor, readout_matrix):
    windows = starts.shape[0]
    offsets = jnp.arange(LOOK, dtype=jnp.int32)
    look = series[starts[:, None] + offsets[None, :]]
    middle_location = lax.optimization_barrier(jnp.mean(look, axis=1))
    deviation = look - middle_location[:, None]
    error_dispersion = jnp.sqrt(lax.optimization_barrier(jnp.mean(deviation * deviation, axis=1)) + 1e-05)
    normed_look = deviation / error_dispersion[:, None]
    patch_index = jnp.arange(P_SIZE, dtype=jnp.int32)[:, None] * STRIDE + jnp.arange(PLEN, dtype=jnp.int32)[None, :]
    patches = normed_look[:, patch_index].reshape(windows * P_SIZE, PLEN)

    def learner_number(weights):
        embed, place, gain_one, up_one, down_one, gain_two, head_one = weights
        lifted = jnp.dot(patches, embed, precision=lax.Precision.HIGHEST, preferred_element_type=jnp.float32)
        lifted = lifted.reshape(windows, P_SIZE, D) + place[None]
        embedded = lifted.reshape(windows * P_SIZE, D).astype(jnp.bfloat16)
        normed = layer_norm(embedded.astype(jnp.float32), gain_one).astype(jnp.bfloat16)
        hidden = jnp.dot(normed, up_one, preferred_element_type=jnp.float32)
        activation = jax.nn.gelu(hidden, approximate=True).astype(jnp.bfloat16)
        state = embedded.astype(jnp.float32) + jnp.dot(activation, down_one, preferred_element_type=jnp.float32)
        final = layer_norm(state, gain_two).astype(jnp.bfloat16)
        unprocessed_signal = jnp.dot(final.reshape(windows, P_SIZE * D), head_one.reshape(P_SIZE * D, H), preferred_element_type=jnp.float32)
        return unprocessed_signal * error_dispersion[:, None] + middle_location[:, None]
    learner_prediction = lax.map(learner_number, (segment_lifting_matrix, location_vector, prelude_scaling_factor, expanding_matrix, contracting_matrix, final_scaling_factor, readout_matrix))
    learner_fraction = 1.0 / (1.0 + counts.astype(jnp.float32))
    resampled_average_prediction = lax.optimization_barrier(jnp.sum(learner_fraction[:, :, None] * learner_prediction, axis=0)) / lax.optimization_barrier(jnp.sum(learner_fraction, axis=0))[:, None]
    target_outcomes = series[starts[:, None] + LOOK + jnp.arange(H, dtype=jnp.int32)[None, :]]
    prediction_error = jnp.abs(target_outcomes - resampled_average_prediction)
    ascending_list = jnp.sort(prediction_error, axis=0)
    ranks = [windows * level // 100 for level in (50, 80, 90, 95)]
    error_percentiles = jnp.stack([ascending_list[rank] for rank in ranks], axis=0)
    return (resampled_average_prediction, error_percentiles)
```

```python
import functools
import math

import jax
import jax.numpy as jnp
from jax import lax
from jax.experimental import pallas as pl
from jax.experimental.pallas import tpu as pltpu
from jax.sharding import PartitionSpec as P

BF, F32 = jnp.bfloat16, jnp.float32
PATCHES, PLEN, STRIDE, LOOK = 8, 16, 8, 72
WIN, D, SHARD, HIDDEN, HORIZONS = 128, 2048, 512, 2048, 96
CHIPF = 2 * SHARD
KCAT = 256
MIB = 1 << 20
GROUPS = ((0,), (1,), (2,), (3,))


def split3(x):
    a = x.astype(BF)
    rest = x - a.astype(F32)
    b = rest.astype(BF)
    c = (rest - b.astype(F32)).astype(BF)
    return a, b, c


def dot(a, b):
    return jnp.dot(a, b, preferred_element_type=F32)


def roll_left(x, by):
    lanes = x.shape[1]
    by = by % lanes
    return x if by == 0 else pltpu.roll(x, lanes - by, 1)


def position():
    t = lax.axis_index("tensor")
    return t, t // 2, t % 2


def call(body, out_shape, in_specs, args, flops, nbytes, scratch=(), limit=24 * MIB):
    return pl.pallas_call(
        body,
        out_shape=out_shape,
        in_specs=in_specs,
        out_specs=jax.tree.map(lambda _: pl.BlockSpec(memory_space=pltpu.VMEM), out_shape),
        scratch_shapes=list(scratch),
        compiler_params=pltpu.CompilerParams(vmem_limit_bytes=limit),
        cost_estimate=pl.CostEstimate(flops=flops, bytes_accessed=nbytes, transcendentals=0),
    )(*args)


V = pl.BlockSpec(memory_space=pltpu.VMEM)
ANY = pl.BlockSpec(memory_space=pl.ANY)


def windows_kernel(series, starts, up, down, up_v, down_v, q, info, target, sem):
    loads = [
        pltpu.make_async_copy(up.at[0], up_v, sem.at[0]),
        pltpu.make_async_copy(down.at[0], down_v, sem.at[1]),
    ]
    for load in loads:
        load.start()
    lane = lax.broadcasted_iota(jnp.int32, (WIN, WIN), 1)
    first = jnp.broadcast_to(starts[...].astype(F32), (WIN, WIN)).T.astype(jnp.int32)
    row, offset = first >> 7, first & 127
    picks = [(row + k == lane).astype(F32).astype(BF) for k in range(3)]
    parts = split3(series[...])
    rows = [sum(dot(pick, part) for part in parts) for pick in picks]
    x = jnp.concatenate(rows, axis=1)
    offset = jnp.concatenate([offset] * 3, axis=1)
    for bit in range(7):
        x = jnp.where((offset >> bit) & 1 == 1, roll_left(x, 1 << bit), x)
    target[...] = roll_left(x, LOOK)[:, :WIN].T
    look = x[:, :WIN]
    center = jnp.sum(jnp.where(lane < LOOK, look, 0.0), axis=1, keepdims=True) * (1.0 / LOOK)
    dev = jnp.where(lane < LOOK, look - center, 0.0)
    spread = jnp.sqrt(jnp.sum(dev * dev, axis=1, keepdims=True) * (1.0 / LOOK) + 1e-05)
    normed = dev / spread
    pair = jnp.where(lane == 0, center, jnp.where(lane == 1, spread, 0.0)).T
    info[...] = pair[:8]
    block = lane // 32
    for p in range(PATCHES):
        one = jnp.where(lane < PLEN, roll_left(normed, STRIDE * p), 0.0)
        one = jnp.where(lane == PLEN + p, 1.0, one)
        two = one + pltpu.roll(one, 32, 1)
        four = two + pltpu.roll(two, 64, 1)
        a, b, c = (v.astype(F32) for v in split3(four))
        q[p, :, :WIN] = jnp.where(block < 2, a, b).astype(BF)
        q[p, :, WIN:] = jnp.where(block == 0, a, jnp.where(block == 1, c, 0.0)).astype(BF)
    for load in loads:
        load.wait()


def cat_rows(x):
    b1, b2, b3 = split3(x)
    zero = jnp.zeros_like(b1)
    return [b1, b2, b1, b2, b3, b1, zero, zero]


def lift_body(up, q, shards, mcat, rstd, dev_own, lhs, ecat):
    t, _, core = position()
    total = sum(jnp.sum(s[...], axis=1, keepdims=True) for s in shards) * (1.0 / D)
    keep = lax.broadcasted_iota(jnp.int32, (32, SHARD), 0) < PLEN + PATCHES
    for k, shard in enumerate(shards):
        gain = shard[PLEN + PATCHES : PLEN + PATCHES + 1, :]
        centred = jnp.where(keep, shard[...] - total, 0.0)
        at = pl.multiple_of(SHARD * (t ^ k), SHARD)
        for i, part in enumerate(split3(centred * gain)):
            lhs[32 * i : 32 * i + 32, pl.ds(at, SHARD)] = part
        for i, part in enumerate(cat_rows(centred)):
            ecat[k, 32 * i : 32 * i + 32, :] = part
    for j in range(HIDDEN // 512):
        cols = slice(512 * j, 512 * j + 512)
        m = dot(lhs[...], up[:, cols])
        m = m[:32] + m[32:64] + m[64:96]
        for i, part in enumerate(cat_rows(m)):
            mcat[32 * i : 32 * i + 32, cols] = part
    for p in range(PATCHES):
        square = jnp.zeros((WIN, 128), F32)
        for k in range(4):
            dev = dot(q[p], ecat[k])
            for c in range(SHARD // 128):
                piece = dev[:, 128 * c : 128 * c + 128]
                square = square + piece * piece
            if k < 2:
                side = pl.multiple_of(SHARD * (core ^ k), SHARD)

                @pl.when(p // 4 == core)
                def _():
                    dev_own[p % 4, :, pl.ds(side, SHARD)] = dev

        var = jnp.sum(square, axis=1, keepdims=True) * (1.0 / D)
        rstd[p] = jnp.broadcast_to(lax.rsqrt(var + 1e-05), (WIN, 128))


def gelu(h):
    c = math.sqrt(2.0 / math.pi)
    half = 0.5 * h
    return half + half * jnp.tanh(h * (c + (c * 0.044715) * (h * h)))


def feed_body(ks, q, rstd, mcat, down, send, keep_x, keep_y, act):
    _, chip, core = position()
    n = len(ks)
    for side in range(2):
        base = 4 * (1 - core) if side == 0 else 4 * core
        for i, k in enumerate(ks):
            p = base + k
            scale = rstd[p][:, :1]
            at = (side * n + i) * WIN
            for j in range(HIDDEN // 512):
                cols = slice(512 * j, 512 * j + 512)
                act[at : at + WIN, cols] = gelu(dot(q[p], mcat[:, cols]) * scale).astype(BF)
    rows = n * WIN
    for half, where in ((0, 1 - chip), (1, chip)):
        for j in range(2):
            cols = pl.ds(pl.multiple_of(CHIPF * where + 512 * j, 512), 512)
            out = dot(act[...], down[:, cols])
            send[:, CHIPF * half + 512 * j : CHIPF * half + 512 * (j + 1)] = out[:rows].astype(BF)
            kept = keep_x if half == 0 else keep_y
            kept[:, 512 * j : 512 * (j + 1)] = out[rows:]


def first_kernel(ks, up, q, s0, s1, s2, s3, down, mcat, rstd, dev_own, send, keep_x, keep_y, lhs, ecat, act):
    lift_body(up, q, (s0, s1, s2, s3), mcat, rstd, dev_own, lhs, ecat)
    feed_body(ks, q, rstd, mcat, down, send, keep_x, keep_y, act)


def feed_kernel(ks, q, rstd, mcat, down, send, keep_x, keep_y, act):
    feed_body(ks, q, rstd, mcat, down, send, keep_x, keep_y, act)


def state_kernel(groups, *refs):
    n = len(groups)
    prev, dev_own = refs[0], refs[1]
    ins = refs[2 : 2 + 3 * n]
    stats, states = refs[2 + 3 * n], refs[3 + 3 * n :]
    lane = lax.broadcasted_iota(jnp.int32, (WIN, WIN), 1)
    table = jnp.zeros((WIN, WIN), F32)
    for g, ks in enumerate(groups):
        keep_y, recv, cross = ins[3 * g : 3 * g + 3]
        for i, k in enumerate(ks):
            rows = slice(i * WIN, i * WIN + WIN)
            x = keep_y[rows, :] + recv[rows, CHIPF:].astype(F32)
            x = x + dev_own[k] + cross[rows, :].astype(F32)
            states[g][rows, :] = x
            mean = jnp.sum(x, axis=1, keepdims=True) * (1.0 / CHIPF)
            off = x - mean
            square = jnp.sum(off * off, axis=1, keepdims=True)
            table = jnp.where(lane == k, mean, jnp.where(lane == 4 + k, square, table))
    stats[...] = prev[...] + table.T[:8]


def head_kernel(groups, mine, theirs, w_own, w_peer, g_own, g_peer, info, counts, *refs):
    n = len(groups)
    states, outs, scr = refs[:n], refs[n : n + 4], refs[n + 4]
    t, _, core = position()
    slot = lax.axis_index("member")
    a, b = mine[...], theirs[...]
    mean = 0.5 * (a[:4] + b[:4])
    gap = a[:4] - b[:4]
    square = a[4:] + b[4:] + (0.5 * CHIPF) * (gap * gap)
    scale = lax.rsqrt(square * (1.0 / D) + 1e-05)
    table = jnp.concatenate([mean, scale, jnp.zeros((WIN - 8, WIN), F32)], axis=0).T
    total = jnp.zeros((WIN, HORIZONS), F32)
    for g, ks in enumerate(groups):
        for i, k in enumerate(ks):
            rows = slice(i * WIN, i * WIN + WIN)
            for gain, w in ((g_own, w_own), (g_peer, w_peer)):
                own = w is w_own
                at = pl.multiple_of(SHARD * (core if own else 1 - core), SHARD)
                x = states[g][rows, pl.ds(at, SHARD)]
                y = (x - table[:, k : k + 1]) * table[:, 4 + k : 5 + k] * gain[...]
                total = total + dot(y.astype(BF), w[4 * core + k])
    share = 1.0 / (1.0 + counts[...])
    members = share.shape[0]
    here = lax.broadcasted_iota(jnp.int32, (members, WIN), 0) == slot
    mine_share = jnp.sum(jnp.where(here, share, 0.0), axis=0, keepdims=True)
    factor = info[1:2, :] * mine_share / jnp.sum(share, axis=0, keepdims=True)
    scr[:, :HORIZONS] = total
    scr[:, HORIZONS:] = jnp.zeros((WIN, WIN - HORIZONS), F32)
    scr[...] = scr[...].T * factor
    for k in range(4):
        outs[k][...] = scr[pl.ds(pl.multiple_of(24 * (t ^ k), 8), 24), :]


def rank_kernel(levels, own, total, info, target, average, levels_out, scr, res, ranks):
    t, _, _ = position()
    slot = lax.axis_index("member")
    per = total.shape[0]
    pred = total[...] + info[0:1, :]
    wanted = target[pl.ds(pl.multiple_of(24 * t, 8), per), :]
    resid = jnp.abs(wanted - pred)
    scr[...] = jnp.zeros((WIN, WIN), F32)
    scr[:per, :] = pred
    scr[...] = scr[...].T
    if own % 8 == 0:
        average[...] = scr[pl.ds(pl.multiple_of(own * slot, 8), own), :per]
    else:
        at = own * slot
        rows = scr[pl.ds(pl.multiple_of((at // 8) * 8, 8), 8), :per]
        pick = rows[:own]
        for s in range(1, 8 // own):
            pick = jnp.where(at % 8 == s * own, rows[s * own : (s + 1) * own], pick)
        average[...] = pick
    res[...] = jnp.zeros((WIN, WIN), F32)
    res[:per, :] = resid
    across = res[...].T
    j = lax.broadcasted_iota(jnp.int32, (WIN, WIN), 0)
    i = lax.broadcasted_iota(jnp.int32, (WIN, WIN), 1)
    earlier = j < i
    for h in range(per):
        row, col = resid[h : h + 1, :], across[:, h : h + 1]
        before = (col < row) | ((col == row) & earlier)
        ranks[h : h + 1, :] = jnp.sum(before.astype(F32), axis=0, keepdims=True)
    order = ranks[...]
    lane = lax.broadcasted_iota(jnp.int32, (per, WIN), 1)
    table = jnp.zeros((per, WIN), F32)
    for n, level in enumerate(levels):
        value = jnp.sum(jnp.where(order == float(level), resid, 0.0), axis=1, keepdims=True)
        table = jnp.where(lane == n, value, table)
    res[:per, :] = table
    levels_out[...] = res[...].T[: len(levels), :per]


def per_device(series, starts, counts, lifting, location, gain_one, up, down, gain_two, readout):
    members = lax.axis_size("member")
    slot = lax.axis_index("member")
    own = counts.shape[1]
    sds = jax.ShapeDtypeStruct

    def over_tensor(x, k):
        return lax.ppermute(x, "tensor", [(i, i ^ k) for i in range(4)])

    def over_member(x, k):
        return lax.ppermute(x, "member", [(i, i ^ k) for i in range(members)])

    hops = [k for k in (1, 3, 8, 24, 4) if k < members]

    packed = jnp.concatenate([lifting[0], location[0], gain_one, jnp.zeros((7, SHARD), F32)], axis=0)
    shards = [packed] + [over_tensor(packed, k) for k in (1, 2, 3)]
    w_peer = over_tensor(readout[0], 1)
    g_peer = over_tensor(gain_two, 1)

    up_v, down_v, q, info, target = call(
        windows_kernel,
        (
            pltpu.VMEM((D, HIDDEN), BF),
            pltpu.VMEM((HIDDEN, D), BF),
            pltpu.VMEM((PATCHES, WIN, KCAT), BF),
            pltpu.VMEM((8, WIN), F32),
            pltpu.VMEM((WIN, WIN), F32),
        ),
        [V, V, ANY, ANY],
        (series.reshape(WIN, WIN), starts.reshape(1, WIN), up, down),
        10**8,
        16 * MIB,
        [pltpu.SemaphoreType.DMA((2,))],
    )

    place = lax.broadcasted_iota(jnp.int32, (members, WIN), 1) // own == slot
    every = jnp.where(place, jnp.tile(counts.astype(F32), (1, WIN // own)), 0.0)
    for k in hops:
        every = every + over_member(every, k)

    def feed_out(n):
        return (
            pltpu.VMEM((n * WIN, D), BF),
            pltpu.VMEM((n * WIN, CHIPF), F32),
            pltpu.VMEM((n * WIN, CHIPF), F32),
        )

    def feed_cost(n):
        return 2 * 2 * n * WIN * HIDDEN * (D + KCAT)

    sent, kept, crossed, received = [], [], [], []
    for g, ks in enumerate(GROUPS):
        n = len(ks)
        act = pltpu.VMEM((2 * n * WIN, HIDDEN), BF)
        if g == 0:
            mcat, rstd, dev_own, send, keep_x, keep_y = call(
                functools.partial(first_kernel, ks),
                (
                    pltpu.VMEM((KCAT, HIDDEN), BF),
                    pltpu.VMEM((PATCHES, WIN, 128), F32),
                    pltpu.VMEM((4, WIN, CHIPF), F32),
                )
                + feed_out(n),
                [V] * 7,
                (up_v, q, *shards, down_v),
                feed_cost(n) + 4 * 10**9,
                MIB,
                [pltpu.VMEM((96, D), BF), pltpu.VMEM((4, KCAT, SHARD), BF), act],
            )
        else:
            send, keep_x, keep_y = call(
                functools.partial(feed_kernel, ks),
                feed_out(n),
                [V] * 4,
                (q, rstd, mcat, down_v),
                feed_cost(n),
                MIB,
                [act],
            )
        recv = over_tensor(send, 1)
        total = (keep_x + recv[:, :CHIPF].astype(F32)).astype(BF)
        kept.append(keep_y)
        received.append(recv)
        crossed.append(over_tensor(total, 2))

    stats = jnp.zeros((8, WIN), F32)
    states = []
    for part in (range(0, len(GROUPS) - 1), range(len(GROUPS) - 1, len(GROUPS))):
        groups = tuple(GROUPS[g] for g in part)
        ins = []
        for g in part:
            ins += [kept[g], received[g], crossed[g]]
        outs = call(
            functools.partial(state_kernel, groups),
            (pltpu.VMEM((8, WIN), F32),) + tuple(pltpu.VMEM((len(ks) * WIN, CHIPF), F32) for ks in groups),
            [V] * (2 + len(ins)),
            (stats, dev_own, *ins),
            10**6 * len(groups),
            MIB,
        )
        stats = outs[0]
        states += list(outs[1:])

    peer = over_tensor(stats, 2)
    parts = call(
        functools.partial(head_kernel, GROUPS),
        tuple(sds((24, WIN), F32) for _ in range(4)),
        [V] * (8 + len(states)),
        (stats, peer, readout[0], w_peer, gain_two, g_peer, info, every, *states),
        10**8,
        MIB,
        [pltpu.VMEM((WIN, WIN), F32)],
    )
    total = parts[0] + over_tensor(parts[1], 1) + over_tensor(parts[2], 2) + over_tensor(parts[3], 3)
    for k in hops:
        total = total + over_member(total, k)

    levels = tuple(WIN * n // 100 for n in (50, 80, 90, 95))
    return call(
        functools.partial(rank_kernel, levels, own),
        (sds((own, 24), F32), sds((4, 24), F32)),
        [V] * 3,
        (total, info, target),
        10**6,
        MIB,
        [pltpu.VMEM((WIN, WIN), F32), pltpu.VMEM((WIN, WIN), F32), pltpu.VMEM((24, WIN), F32)],
    )


def solution(mesh):
    placed = (
        P(),
        P(),
        P(None, "member"),
        P("member", None, "tensor"),
        P("member", None, "tensor"),
        P("member", "tensor"),
        P("member", None, "tensor"),
        P("member", "tensor", None),
        P("member", "tensor"),
        P("member", None, "tensor", None),
    )
    return jax.shard_map(
        per_device,
        mesh=mesh,
        in_specs=placed,
        out_specs=(P("member", "tensor"), P(None, "tensor")),
        check_vma=False,
    )
```

```python
import functools
import math

import jax
import jax.numpy as jnp
from jax import lax
from jax.experimental import pallas as pl
from jax.experimental.pallas import tpu as pltpu
from jax.sharding import PartitionSpec as P

BF, F32 = jnp.bfloat16, jnp.float32
PATCHES, PLEN, STRIDE, LOOK = 8, 16, 8, 72
WIN, D, SHARD, HIDDEN, HORIZONS = 128, 2048, 512, 2048, 96
KCAT = 256
MIB = 1 << 20
US = 10**9


def split3(x):
    a = x.astype(BF)
    rest = x - a.astype(F32)
    b = rest.astype(BF)
    c = (rest - b.astype(F32)).astype(BF)
    return a, b, c


def dot(a, b):
    return jnp.dot(a, b, preferred_element_type=F32)


def roll_left(x, by):
    lanes = x.shape[1]
    by = by % lanes
    return x if by == 0 else pltpu.roll(x, lanes - by, 1)


def shard_cols(t):
    return pl.ds(pl.multiple_of(SHARD * t, SHARD), SHARD)


def call(body, out_shape, in_specs, args, flops, nbytes, scratch=(), limit=24 * MIB, after=()):
    taken, held = len(in_specs), len(after)

    def run(*refs):
        body(*refs[:taken], *refs[taken + held :])

    args = tuple(
        pltpu.with_memory_space_constraint(x, pltpu.HBM if spec is HBM else pltpu.VMEM)
        for x, spec in zip(args, in_specs)
    ) + tuple(after)
    in_specs = list(in_specs) + [ANY] * held
    return pl.pallas_call(
        run,
        out_shape=out_shape,
        in_specs=in_specs,
        out_specs=jax.tree.map(lambda _: pl.BlockSpec(memory_space=pltpu.VMEM), out_shape),
        scratch_shapes=list(scratch),
        compiler_params=pltpu.CompilerParams(vmem_limit_bytes=limit),
        cost_estimate=pl.CostEstimate(flops=flops, bytes_accessed=nbytes, transcendentals=0),
    )(*args)


V = pl.BlockSpec(memory_space=pltpu.VMEM)
ANY = pl.BlockSpec(memory_space=pl.ANY)
HBM = pl.BlockSpec(memory_space=pltpu.HBM)


def pack_kernel(lifting, location, gain_one, gain_two, counts_h, down, packed, every, give, g1, g2, counts, scr, sem):
    t = lax.axis_index("tensor")
    loads = [
        pltpu.make_async_copy(lifting.at[0], packed.at[0:PLEN, :], sem.at[0]),
        pltpu.make_async_copy(location.at[0], packed.at[PLEN : PLEN + PATCHES, :], sem.at[1]),
        pltpu.make_async_copy(gain_one, g1, sem.at[2]),
        pltpu.make_async_copy(gain_two, g2, sem.at[3]),
        pltpu.make_async_copy(counts_h, counts, sem.at[4]),
        pltpu.make_async_copy(down.at[0, :, shard_cols(t ^ 3)], give, sem.at[5]),
    ]
    for load in loads:
        load.start()
    own, members = counts.shape
    scr[...] = jnp.zeros((WIN, WIN), F32)
    for load in loads[:5]:
        load.wait()
    row = lax.broadcasted_iota(jnp.int32, (8, SHARD), 0)
    packed[PLEN + PATCHES :, :] = jnp.where(row == 0, g1[...], jnp.where(row == 1, g2[...], 0.0))
    scr[:own, :members] = counts[...].astype(F32)
    columns = scr[...].T[:members]
    at = own * lax.axis_index("member")
    place = lax.broadcasted_iota(jnp.int32, (members, WIN), 1) - at
    placed = jnp.zeros((members, WIN), F32)
    for j in range(own):
        placed = jnp.where(place == j, columns[:, j : j + 1], placed)
    every[...] = placed
    loads[5].wait()


def windows_kernel(series_h, starts_h, up, readout, up_v, head_v, q, info, target, series, starts, sem):
    small = [
        pltpu.make_async_copy(series_h, series, sem.at[0]),
        pltpu.make_async_copy(starts_h, starts, sem.at[1]),
    ]
    loads = [
        pltpu.make_async_copy(up.at[0], up_v, sem.at[2]),
        pltpu.make_async_copy(readout, head_v, sem.at[3]),
    ]
    for load in small + loads:
        load.start()
    for load in small:
        load.wait()
    lane = lax.broadcasted_iota(jnp.int32, (WIN, WIN), 1)
    first = jnp.broadcast_to(starts[...].astype(F32), (WIN, WIN)).T.astype(jnp.int32)
    row, offset = first >> 7, first & 127
    picks = [(row + k == lane).astype(F32).astype(BF) for k in range(3)]
    parts = split3(series[...])
    rows = [sum(dot(pick, part) for part in parts) for pick in picks]
    x = jnp.concatenate(rows, axis=1)
    offset = jnp.concatenate([offset] * 3, axis=1)
    for bit in range(7):
        x = jnp.where((offset >> bit) & 1 == 1, roll_left(x, 1 << bit), x)
    target[...] = roll_left(x, LOOK)[:, :WIN].T
    look = x[:, :WIN]
    center = jnp.sum(jnp.where(lane < LOOK, look, 0.0), axis=1, keepdims=True) * (1.0 / LOOK)
    dev = jnp.where(lane < LOOK, look - center, 0.0)
    spread = jnp.sqrt(jnp.sum(dev * dev, axis=1, keepdims=True) * (1.0 / LOOK) + 1e-05)
    normed = dev / spread
    pair = jnp.where(lane == 0, center, jnp.where(lane == 1, spread, 0.0)).T
    info[...] = pair[:8]
    block = lane // 32
    for p in range(PATCHES):
        one = jnp.where(lane < PLEN, roll_left(normed, STRIDE * p), 0.0)
        one = jnp.where(lane == PLEN + p, 1.0, one)
        two = one + pltpu.roll(one, 32, 1)
        four = two + pltpu.roll(two, 64, 1)
        a, b, c = (v.astype(F32) for v in split3(four))
        q[p, :, :WIN] = jnp.where(block < 2, a, b).astype(BF)
        q[p, :, WIN:] = jnp.where(block == 0, a, jnp.where(block == 1, c, 0.0)).astype(BF)
    for load in loads:
        load.wait()


def cat_rows(x):
    b1, b2, b3 = split3(x)
    zero = jnp.zeros_like(b1)
    return [b1, b2, b1, b2, b3, b1, zero, zero]


def lift_kernel(up, s0, s1, s2, s3, down, m24, ecat, own_x, own_y, give, lhs, sem):
    t = lax.axis_index("tensor")
    loads = [
        pltpu.make_async_copy(down.at[0, :, shard_cols(t ^ 2)], own_x, sem.at[0]),
        pltpu.make_async_copy(down.at[0, :, shard_cols(t)], own_y, sem.at[1]),
        pltpu.make_async_copy(down.at[0, :, shard_cols(t ^ 1)], give, sem.at[2]),
    ]
    for load in loads:
        load.start()
    shards = (s0, s1, s2, s3)
    total = sum(jnp.sum(s[...], axis=1, keepdims=True) for s in shards) * (1.0 / D)
    keep = lax.broadcasted_iota(jnp.int32, (32, SHARD), 0) < PLEN + PATCHES
    for k, shard in enumerate(shards):
        gain = shard[PLEN + PATCHES : PLEN + PATCHES + 1, :]
        centred = jnp.where(keep, shard[...] - total, 0.0)
        for i, part in enumerate(split3(centred * gain)):
            lhs[32 * i : 32 * i + 32, shard_cols(t ^ k)] = part
        for i, part in enumerate(cat_rows(centred)):
            ecat[k, 32 * i : 32 * i + 32, :] = part
    for j in range(HIDDEN // 512):
        cols = slice(512 * j, 512 * j + 512)
        m = dot(lhs[...], up[:, cols])
        m24[:, cols] = m[:32] + m[32:64] + m[64:96]
    for load in loads:
        load.wait()


def spread_rows(m24, mcat):
    for j in range(HIDDEN // 512):
        cols = slice(512 * j, 512 * j + 512)
        for i, part in enumerate(cat_rows(m24[:, cols])):
            mcat[32 * i : 32 * i + 32, cols] = part


def scale_kernel(q, ecat, m24, rstd, mcat):
    spread_rows(m24, mcat)
    for p in range(0, PATCHES, 2):
        square = jnp.zeros((2 * WIN, 128), F32)
        for k in range(4):
            dev = dot(q[p : p + 2].reshape(2 * WIN, KCAT), ecat[k])
            for c in range(SHARD // 128):
                piece = dev[:, 128 * c : 128 * c + 128]
                square = square + piece * piece
        var = jnp.sum(square, axis=1, keepdims=True) * (1.0 / D)
        rstd[p : p + 2] = jnp.broadcast_to(lax.rsqrt(var + 1e-05), (2 * WIN, 128)).reshape(2, WIN, 128)


def gelu(h):
    c = math.sqrt(2.0 / math.pi)
    half = 0.5 * h
    return half + half * jnp.tanh(h * (c + (c * 0.044715) * (h * h)))


def away_body(g, q, rstd, mcats, downs, act, send):
    rows = q[2 * g : 2 * g + 2].reshape(2 * WIN, KCAT)
    scale = rstd[2 * g : 2 * g + 2].reshape(2 * WIN, 128)[:, :1]
    total = jnp.zeros((2 * WIN, SHARD), F32)
    for side in range(2):
        for j in range(HIDDEN // 512):
            cols = slice(512 * j, 512 * j + 512)
            at = slice(HIDDEN * side + 512 * j, HIDDEN * side + 512 * (j + 1))
            act[:, at] = gelu(dot(rows, mcats[side][:, cols]) * scale).astype(BF)
    for side in range(2):
        total = total + dot(act[:, HIDDEN * side : HIDDEN * (side + 1)], downs[side][...])
    send[...] = total.astype(BF)


def first_away_kernel(q, rstd, m_own, m24_peer, d_own, d_peer, m_peer, act, send):
    spread_rows(m24_peer, m_peer)
    away_body(0, q, rstd, (m_own, m_peer), (d_own, d_peer), act, send)


def away_kernel(g, q, rstd, m_own, m_peer, d_own, d_peer, act, send):
    away_body(g, q, rstd, (m_own, m_peer), (d_own, d_peer), act, send)


def add_stats(table, p, x):
    lane = lax.broadcasted_iota(jnp.int32, (WIN, WIN), 1)
    mean = jnp.sum(x, axis=1, keepdims=True) * (1.0 / SHARD)
    off = x - mean
    square = jnp.sum(off * off, axis=1, keepdims=True)
    return jnp.where(lane == p, mean, jnp.where(lane == PATCHES + p, square, table))


def home_kernel(q, ecat, d_own, d_peer, a0, a1, a2, a3, c0, c1, c2, state, last, stats):
    table = jnp.zeros((WIN, WIN), F32)
    for g, act in enumerate((a0, a1, a2, a3)):
        x = dot(act[:, :HIDDEN], d_own[...]) + dot(act[:, HIDDEN:], d_peer[...])
        x = x + dot(q[2 * g : 2 * g + 2].reshape(2 * WIN, KCAT), ecat[0])
        if g == 3:
            last[...] = x
            continue
        x = x + (c0, c1, c2)[g][...].astype(F32)
        state[2 * WIN * g : 2 * WIN * (g + 1), :] = x
        table = add_stats(table, 2 * g, x[:WIN])
        table = add_stats(table, 2 * g + 1, x[WIN:])
    stats[...] = table.T[: 2 * PATCHES]


def last_state_kernel(last, cross, prev, state, stats):
    x = last[...] + cross[...].astype(F32)
    state[...] = x
    table = add_stats(jnp.zeros((WIN, WIN), F32), 6, x[:WIN])
    table = add_stats(table, 7, x[WIN:])
    stats[...] = prev[...] + table.T[: 2 * PATCHES]


def head_kernel(stats, state, last, heads, shard, info, counts, send, keep, scr):
    core = lax.axis_index("tensor") & 1
    slot = lax.axis_index("member")
    scale = lax.rsqrt(stats[PATCHES:, :] * (1.0 / D) + 1e-05)
    table = jnp.concatenate([stats[:PATCHES, :], scale, jnp.zeros((WIN - 2 * PATCHES, WIN), F32)], axis=0).T
    total = jnp.zeros((WIN, HORIZONS), F32)
    for p in range(PATCHES):
        x = state[p * WIN : (p + 1) * WIN, :] if p < 6 else last[(p - 6) * WIN : (p - 5) * WIN, :]
        y = (x - table[:, p : p + 1]) * table[:, PATCHES + p : PATCHES + p + 1] * shard[25:26, :]
        total = total + lax.dot_general(
            y.astype(BF), heads[p], (((1,), (1,)), ((), ())), preferred_element_type=F32
        )
    share = 1.0 / (1.0 + counts[...])
    members = share.shape[0]
    here = lax.broadcasted_iota(jnp.int32, (members, WIN), 0) == slot
    mine_share = jnp.sum(jnp.where(here, share, 0.0), axis=0, keepdims=True)
    factor = info[1:2, :] * mine_share / jnp.sum(share, axis=0, keepdims=True)
    scr[:, :HORIZONS] = total
    scr[:, HORIZONS:] = jnp.zeros((WIN, WIN - HORIZONS), F32)
    scr[...] = scr[...].T * factor
    for c in range(2):
        for out, side in ((keep, core), (send, 1 - core)):
            out[24 * c : 24 * c + 24, :] = scr[pl.ds(pl.multiple_of(48 * c + 24 * side, 8), 24), :]


def rank_kernel(levels, own, total, info, target, average, levels_out, scr, res, ranks):
    t = lax.axis_index("tensor")
    slot = lax.axis_index("member")
    per = total.shape[0]
    pred = total[...] + info[0:1, :]
    wanted = target[pl.ds(pl.multiple_of(24 * t, 8), per), :]
    resid = jnp.abs(wanted - pred)
    scr[...] = jnp.zeros((WIN, WIN), F32)
    scr[:per, :] = pred
    scr[...] = scr[...].T
    if own % 8 == 0:
        average[...] = scr[pl.ds(pl.multiple_of(own * slot, 8), own), :per]
    else:
        at = own * slot
        rows = scr[pl.ds(pl.multiple_of((at // 8) * 8, 8), 8), :per]
        pick = rows[:own]
        for s in range(1, 8 // own):
            pick = jnp.where(at % 8 == s * own, rows[s * own : (s + 1) * own], pick)
        average[...] = pick
    res[...] = jnp.zeros((WIN, WIN), F32)
    res[:per, :] = resid
    across = res[...].T
    j = lax.broadcasted_iota(jnp.int32, (WIN, WIN), 0)
    i = lax.broadcasted_iota(jnp.int32, (WIN, WIN), 1)
    earlier = j < i
    for h in range(per):
        row, col = resid[h : h + 1, :], across[:, h : h + 1]
        before = (col < row) | ((col == row) & earlier)
        ranks[h : h + 1, :] = jnp.sum(before.astype(F32), axis=0, keepdims=True)
    order = ranks[...]
    lane = lax.broadcasted_iota(jnp.int32, (per, WIN), 1)
    table = jnp.zeros((per, WIN), F32)
    for n, level in enumerate(levels):
        value = jnp.sum(jnp.where(order == float(level), resid, 0.0), axis=1, keepdims=True)
        table = jnp.where(lane == n, value, table)
    res[:per, :] = table
    levels_out[...] = res[...].T[: len(levels), :per]


def per_device(series, starts, counts, lifting, location, gain_one, up, down, gain_two, readout):
    members = lax.axis_size("member")
    own = counts.shape[1]
    sds = jax.ShapeDtypeStruct

    def over_tensor(x, k):
        return lax.ppermute(x, "tensor", [(i, i ^ k) for i in range(4)])

    def over_member(x, k):
        return lax.ppermute(x, "member", [(i, i ^ k) for i in range(members)])

    shard_bf = pltpu.VMEM((D, SHARD), BF)
    packed, every, give_x = call(
        pack_kernel,
        (pltpu.VMEM((32, SHARD), F32), pltpu.VMEM((members, WIN), F32), shard_bf),
        [HBM] * 6,
        (lifting, location, gain_one, gain_two, counts.T, down),
        2 * US,
        1000,
        [
            pltpu.VMEM((1, SHARD), F32),
            pltpu.VMEM((1, SHARD), F32),
            pltpu.VMEM((own, members), jnp.int32),
            pltpu.VMEM((WIN, WIN), F32),
            pltpu.SemaphoreType.DMA((6,)),
        ],
    )
    shards = [packed] + [over_tensor(packed, k) for k in (1, 2, 3)]
    peer_x = over_tensor(give_x, 1)

    heads = jnp.swapaxes(readout[0], 1, 2)
    up_v, heads_v, q, info, target = call(
        windows_kernel,
        (
            pltpu.VMEM((D, HIDDEN), BF),
            pltpu.VMEM((PATCHES, HORIZONS, SHARD), BF),
            pltpu.VMEM((PATCHES, WIN, KCAT), BF),
            pltpu.VMEM((8, WIN), F32),
            pltpu.VMEM((WIN, WIN), F32),
        ),
        [HBM] * 4,
        (series.reshape(WIN, WIN), starts.reshape(1, WIN), up, heads),
        5 * US,
        1000,
        [pltpu.VMEM((WIN, WIN), F32), pltpu.VMEM((1, WIN), jnp.int32), pltpu.SemaphoreType.DMA((4,))],
        after=(packed,),
    )

    hops = [k for k in (1, 3, 8, 24) if k < members]
    steps = iter(hops + [4] * (members > 4))

    def hop(value, after=None):
        k = next(steps, None)
        if after is not None:
            value = lax.optimization_barrier((value, after))[0]
        return value if k is None else value + over_member(value, k)

    every = hop(every)
    m24, ecat, own_x, own_y, give_y = call(
        lift_kernel,
        (pltpu.VMEM((32, HIDDEN), F32), pltpu.VMEM((4, KCAT, SHARD), BF), shard_bf, shard_bf, shard_bf),
        [V] * 5 + [HBM],
        (up_v, *shards, down),
        3 * US,
        1000,
        [pltpu.VMEM((96, D), BF), pltpu.SemaphoreType.DMA((3,))],
        after=(every,),
    )
    m24_peer = over_tensor(m24, 1)
    mcat_shape = pltpu.VMEM((KCAT, HIDDEN), BF)
    rstd, m_own = call(
        scale_kernel,
        (pltpu.VMEM((PATCHES, WIN, 128), F32), mcat_shape),
        [V] * 3,
        (q, ecat, m24),
        2 * US,
        1000,
    )
    sums = (pltpu.VMEM((2 * WIN, 2 * HIDDEN), BF), pltpu.VMEM((2 * WIN, SHARD), BF))
    m_peer, act, send = call(
        first_away_kernel,
        (mcat_shape,) + sums,
        [V] * 6,
        (q, rstd, m_own, m24_peer, own_x, peer_x),
        4 * US,
        1000,
    )
    acts, crossed = [act], [over_tensor(send, 2)]
    peer_y = over_tensor(lax.optimization_barrier((give_y, send))[0], 1)
    for g in range(1, 4):
        act, send = call(
            functools.partial(away_kernel, g),
            sums,
            [V] * 6,
            (q, rstd, m_own, m_peer, own_x, peer_x),
            4 * US,
            1000,
            after=(every, crossed[g - 2]) if g > 1 else (),
        )
        acts.append(act)
        crossed.append(over_tensor(send, 2))
        every = hop(every, send)
    state, last, stats = call(
        home_kernel,
        (
            pltpu.VMEM((6 * WIN, SHARD), F32),
            pltpu.VMEM((2 * WIN, SHARD), F32),
            pltpu.VMEM((2 * PATCHES, WIN), F32),
        ),
        [V] * 11,
        (q, ecat, own_y, peer_y, *acts, *crossed[:3]),
        5 * US,
        1000,
        after=(every,),
    )
    last, stats = call(
        last_state_kernel,
        (pltpu.VMEM((2 * WIN, SHARD), F32), pltpu.VMEM((2 * PATCHES, WIN), F32)),
        [V] * 3,
        (last, crossed[3], stats),
        US,
        1000,
    )
    every = hop(every, stats)
    features = SHARD
    for k in (1, 2):
        other = over_tensor(stats, k)
        gap = stats[:PATCHES] - other[:PATCHES]
        square = stats[PATCHES:] + other[PATCHES:] + (0.5 * features) * (gap * gap)
        stats = jnp.concatenate([0.5 * (stats[:PATCHES] + other[:PATCHES]), square], axis=0)
        features *= 2
    sent, held = call(
        head_kernel,
        (pltpu.VMEM((48, WIN), F32),) * 2,
        [V] * 7,
        (stats, state, last, heads_v, packed, info, every),
        US,
        1000,
        [pltpu.VMEM((WIN, WIN), F32)],
    )
    total = held + over_tensor(sent, 1)
    total = total + over_tensor(total, 2)
    if members > 4:
        pairs = [(4 * m + t, 4 * (m ^ 4) + (t ^ 2)) for m in range(members) for t in range(4)]
        total = total + lax.ppermute(total, ("member", "tensor"), pairs)
    total = lax.dynamic_slice_in_dim(total, 24 * ((lax.axis_index("tensor") >> 1)), 24, 0)
    for k in hops:
        total = total + over_member(total, k)

    levels = tuple(WIN * n // 100 for n in (50, 80, 90, 95))
    return call(
        functools.partial(rank_kernel, levels, own),
        (sds((own, 24), F32), sds((4, 24), F32)),
        [V] * 3,
        (total, info, target),
        US,
        1000,
        [pltpu.VMEM((WIN, WIN), F32), pltpu.VMEM((WIN, WIN), F32), pltpu.VMEM((24, WIN), F32)],
    )


def solution(mesh):
    placed = (
        P(),
        P(),
        P(None, "member"),
        P("member", None, "tensor"),
        P("member", None, "tensor"),
        P("member", "tensor"),
        P("member", None, "tensor"),
        P("member", "tensor", None),
        P("member", "tensor"),
        P("member", None, "tensor", None),
    )
    return jax.shard_map(
        per_device,
        mesh=mesh,
        in_specs=placed,
        out_specs=(P("member", "tensor"), P(None, "tensor")),
        check_vma=False,
    )
```

```python
import functools
import math

import jax
import jax.numpy as jnp
from jax import lax
from jax.experimental import pallas as pl
from jax.experimental.pallas import tpu as pltpu
from jax.sharding import PartitionSpec as P

BF, F32 = jnp.bfloat16, jnp.float32
PATCHES, PLEN, STRIDE, LOOK = 8, 16, 8, 72
WIN, D, SHARD, HIDDEN, HORIZONS = 128, 2048, 512, 2048, 96
KCAT = 256
MIB = 1 << 20
US = 10**9


def split3(x):
    a = x.astype(BF)
    rest = x - a.astype(F32)
    b = rest.astype(BF)
    c = (rest - b.astype(F32)).astype(BF)
    return a, b, c


def dot(a, b):
    return jnp.dot(a, b, preferred_element_type=F32)


def roll_left(x, by):
    lanes = x.shape[1]
    by = by % lanes
    return x if by == 0 else pltpu.roll(x, lanes - by, 1)


def shard_cols(t):
    return pl.ds(pl.multiple_of(SHARD * t, SHARD), SHARD)


def call(body, out_shape, in_specs, args, flops, nbytes, scratch=(), limit=24 * MIB, after=()):
    taken, held = len(in_specs), len(after)

    def run(*refs):
        body(*refs[:taken], *refs[taken + held :])

    args = tuple(
        pltpu.with_memory_space_constraint(x, pltpu.HBM if spec is HBM else pltpu.VMEM)
        for x, spec in zip(args, in_specs)
    ) + tuple(after)
    in_specs = list(in_specs) + [ANY] * held
    return pl.pallas_call(
        run,
        out_shape=out_shape,
        in_specs=in_specs,
        out_specs=jax.tree.map(lambda _: pl.BlockSpec(memory_space=pltpu.VMEM), out_shape),
        scratch_shapes=list(scratch),
        compiler_params=pltpu.CompilerParams(vmem_limit_bytes=limit),
        cost_estimate=pl.CostEstimate(flops=flops, bytes_accessed=nbytes, transcendentals=0),
    )(*args)


V = pl.BlockSpec(memory_space=pltpu.VMEM)
ANY = pl.BlockSpec(memory_space=pl.ANY)
HBM = pl.BlockSpec(memory_space=pltpu.HBM)


def pack_kernel(lifting, location, gain_one, gain_two, counts_h, down, packed, every, give, g1, g2, counts, scr, sem):
    t = lax.axis_index("tensor")
    loads = [
        pltpu.make_async_copy(lifting.at[0], packed.at[0:PLEN, :], sem.at[0]),
        pltpu.make_async_copy(location.at[0], packed.at[PLEN : PLEN + PATCHES, :], sem.at[1]),
        pltpu.make_async_copy(gain_one, g1, sem.at[2]),
        pltpu.make_async_copy(gain_two, g2, sem.at[3]),
        pltpu.make_async_copy(counts_h, counts, sem.at[4]),
        pltpu.make_async_copy(down.at[0, :, shard_cols(t ^ 3)], give, sem.at[5]),
    ]
    for load in loads:
        load.start()
    own, members = counts.shape
    scr[...] = jnp.zeros((WIN, WIN), F32)
    for load in loads[:5]:
        load.wait()
    row = lax.broadcasted_iota(jnp.int32, (8, SHARD), 0)
    packed[PLEN + PATCHES :, :] = jnp.where(row == 0, g1[...], jnp.where(row == 1, g2[...], 0.0))
    scr[:own, :members] = counts[...].astype(F32)
    columns = scr[...].T[:members]
    at = own * lax.axis_index("member")
    place = lax.broadcasted_iota(jnp.int32, (members, WIN), 1) - at
    placed = jnp.zeros((members, WIN), F32)
    for j in range(own):
        placed = jnp.where(place == j, columns[:, j : j + 1], placed)
    every[...] = placed
    loads[5].wait()


def lift_parts(t, shards, up, lhs):
    for n, (k, shard) in enumerate(shards):
        gain = shard[PLEN + PATCHES : PLEN + PATCHES + 1, :]
        row = lax.broadcasted_iota(jnp.int32, (32, SHARD), 0)
        rows = jnp.where(row < PLEN + PATCHES, shard[...] * gain, jnp.where(row == PLEN + PATCHES, gain, 0.0))
        for i, part in enumerate(split3(rows)):
            lhs[n, 32 * i : 32 * i + 32, :] = part
    for j in range(HIDDEN // 512):
        cols = slice(512 * j, 512 * j + 512)
        m = sum(dot(lhs[n], up[shard_cols(t ^ k), cols]) for n, (k, _) in enumerate(shards))
        yield cols, m[:32] + m[32:64] + m[64:96]


def windows_kernel(
    series_h, starts_h, down, heads_h, up, s0, s1,
    own_x, own_y, give_y, heads, q, info, target, half, series, starts, lhs, sem,
):
    t = lax.axis_index("tensor")
    small = [
        pltpu.make_async_copy(series_h, series, sem.at[0]),
        pltpu.make_async_copy(starts_h, starts, sem.at[1]),
    ]
    loads = [
        pltpu.make_async_copy(down.at[0, :, shard_cols(t ^ 2)], own_x, sem.at[2]),
        pltpu.make_async_copy(heads_h, heads, sem.at[3]),
        pltpu.make_async_copy(down.at[0, :, shard_cols(t ^ 1)], give_y, sem.at[4]),
        pltpu.make_async_copy(down.at[0, :, shard_cols(t)], own_y, sem.at[5]),
    ]
    for load in small + loads:
        load.start()
    for cols, m in lift_parts(t, ((0, s0), (1, s1)), up, lhs):
        half[:, cols] = m
    for load in small:
        load.wait()
    lane = lax.broadcasted_iota(jnp.int32, (WIN, WIN), 1)
    first = jnp.broadcast_to(starts[...].astype(F32), (WIN, WIN)).T.astype(jnp.int32)
    row, offset = first >> 7, first & 127
    picks = [(row + k == lane).astype(F32).astype(BF) for k in range(3)]
    parts = split3(series[...])
    rows = [sum(dot(pick, part) for part in parts) for pick in picks]
    x = jnp.concatenate(rows, axis=1)
    offset = jnp.concatenate([offset] * 3, axis=1)
    for bit in range(7):
        x = jnp.where((offset >> bit) & 1 == 1, roll_left(x, 1 << bit), x)
    target[...] = roll_left(x, LOOK)[:, :WIN].T
    look = x[:, :WIN]
    center = jnp.sum(jnp.where(lane < LOOK, look, 0.0), axis=1, keepdims=True) * (1.0 / LOOK)
    dev = jnp.where(lane < LOOK, look - center, 0.0)
    spread = jnp.sqrt(jnp.sum(dev * dev, axis=1, keepdims=True) * (1.0 / LOOK) + 1e-05)
    normed = dev / spread
    pair = jnp.where(lane == 0, center, jnp.where(lane == 1, spread, 0.0)).T
    info[...] = pair[:8]
    block = lane // 32
    for p in range(PATCHES):
        one = jnp.where(lane < PLEN, roll_left(normed, STRIDE * p), 0.0)
        one = jnp.where(lane == PLEN + p, 1.0, one)
        two = one + pltpu.roll(one, 32, 1)
        four = two + pltpu.roll(two, 64, 1)
        a, b, c = (v.astype(F32) for v in split3(four))
        q[p, :, :WIN] = jnp.where(block < 2, a, b).astype(BF)
        q[p, :, WIN:] = jnp.where(block == 0, a, jnp.where(block == 1, c, 0.0)).astype(BF)
    for load in loads:
        load.wait()


def cat_rows(x):
    b1, b2, b3 = split3(x)
    zero = jnp.zeros_like(b1)
    return [b1, b2, b1, b2, b3, b1, zero, zero]


def lift_kernel(up, s0, s1, s2, s3, half, m24, ecat, lhs):
    t = lax.axis_index("tensor")
    shards = (s0, s1, s2, s3)
    mean = sum(jnp.sum(s[...], axis=1, keepdims=True) for s in shards) * (1.0 / D)
    keep = lax.broadcasted_iota(jnp.int32, (32, SHARD), 0) < PLEN + PATCHES
    for cols, m in lift_parts(t, ((2, s2), (3, s3)), up, lhs):
        m = m + half[:, cols]
        m24[:, cols] = m - mean * m[PLEN + PATCHES : PLEN + PATCHES + 1, :]
    for k, shard in enumerate(shards):
        centred = jnp.where(keep, shard[...] - mean, 0.0)
        for i, part in enumerate(cat_rows(centred)):
            ecat[k, 32 * i : 32 * i + 32, :] = part


def spread_rows(m24, mcat):
    for j in range(HIDDEN // 512):
        cols = slice(512 * j, 512 * j + 512)
        row = lax.broadcasted_iota(jnp.int32, (32, 512), 0)
        for i, part in enumerate(cat_rows(jnp.where(row < PLEN + PATCHES, m24[:, cols], 0.0))):
            mcat[32 * i : 32 * i + 32, cols] = part


def scale_kernel(q, ecat, m24, rstd, mcat):
    spread_rows(m24, mcat)
    for p in range(0, PATCHES, 2):
        square = jnp.zeros((2 * WIN, 128), F32)
        for k in range(4):
            dev = dot(q[p : p + 2].reshape(2 * WIN, KCAT), ecat[k])
            for c in range(SHARD // 128):
                piece = dev[:, 128 * c : 128 * c + 128]
                square = square + piece * piece
        var = jnp.sum(square, axis=1, keepdims=True) * (1.0 / D)
        rstd[p : p + 2] = jnp.broadcast_to(lax.rsqrt(var + 1e-05), (2 * WIN, 128)).reshape(2, WIN, 128)


def gelu(h):
    c = math.sqrt(2.0 / math.pi)
    half = 0.5 * h
    return half + half * jnp.tanh(h * (c + (c * 0.044715) * (h * h)))


def away_body(g, q, rstd, mcats, downs, act, send):
    rows = q[2 * g : 2 * g + 2].reshape(2 * WIN, KCAT)
    scale = rstd[2 * g : 2 * g + 2].reshape(2 * WIN, 128)[:, :1]
    total = jnp.zeros((2 * WIN, SHARD), F32)
    for side in range(2):
        for j in range(HIDDEN // 512):
            cols = slice(512 * j, 512 * j + 512)
            at = slice(HIDDEN * side + 512 * j, HIDDEN * side + 512 * (j + 1))
            act[:, at] = gelu(dot(rows, mcats[side][:, cols]) * scale).astype(BF)
    for side in range(2):
        total = total + dot(act[:, HIDDEN * side : HIDDEN * (side + 1)], downs[side][...])
    send[...] = total.astype(BF)


def first_away_kernel(q, rstd, m_own, m24_peer, d_own, d_peer, m_peer, act, send):
    spread_rows(m24_peer, m_peer)
    away_body(0, q, rstd, (m_own, m_peer), (d_own, d_peer), act, send)


def away_kernel(g, q, rstd, m_own, m_peer, d_own, d_peer, act, send):
    away_body(g, q, rstd, (m_own, m_peer), (d_own, d_peer), act, send)


def add_stats(table, p, x):
    lane = lax.broadcasted_iota(jnp.int32, (WIN, WIN), 1)
    mean = jnp.sum(x, axis=1, keepdims=True) * (1.0 / SHARD)
    off = x - mean
    square = jnp.sum(off * off, axis=1, keepdims=True)
    return jnp.where(lane == p, mean, jnp.where(lane == PATCHES + p, square, table))


def home_rows(g, q, ecat, d_own, d_peer, act):
    x = dot(act[:, :HIDDEN], d_own[...]) + dot(act[:, HIDDEN:], d_peer[...])
    return x + dot(q[2 * g : 2 * g + 2].reshape(2 * WIN, KCAT), ecat[0])


def home_kernel(q, ecat, d_own, d_peer, a0, a1, part):
    for g, act in enumerate((a0, a1)):
        part[2 * WIN * g : 2 * WIN * (g + 1), :] = home_rows(g, q, ecat, d_own, d_peer, act)


def state_kernel(q, ecat, d_own, d_peer, a2, a3, part, c0, c1, c2, state, last, stats):
    last[...] = home_rows(3, q, ecat, d_own, d_peer, a3)
    table = jnp.zeros((WIN, WIN), F32)
    for g, cross in enumerate((c0, c1, c2)):
        rows = slice(2 * WIN * g, 2 * WIN * (g + 1))
        x = part[rows, :] if g < 2 else home_rows(2, q, ecat, d_own, d_peer, a2)
        x = x + cross[...].astype(F32)
        state[rows, :] = x
        table = add_stats(table, 2 * g, x[:WIN])
        table = add_stats(table, 2 * g + 1, x[WIN:])
    stats[...] = table.T[: 2 * PATCHES]


def last_state_kernel(last, cross, prev, state, stats):
    x = last[...] + cross[...].astype(F32)
    state[...] = x
    table = add_stats(jnp.zeros((WIN, WIN), F32), 6, x[:WIN])
    table = add_stats(table, 7, x[WIN:])
    stats[...] = prev[...] + table.T[: 2 * PATCHES]


def head_kernel(stats, state, last, heads, shard, info, counts, send, keep, scr):
    core = lax.axis_index("tensor") & 1
    slot = lax.axis_index("member")
    scale = lax.rsqrt(stats[PATCHES:, :] * (1.0 / D) + 1e-05)
    table = jnp.concatenate([stats[:PATCHES, :], scale, jnp.zeros((WIN - 2 * PATCHES, WIN), F32)], axis=0).T
    total = jnp.zeros((WIN, HORIZONS), F32)
    for p in range(PATCHES):
        x = state[p * WIN : (p + 1) * WIN, :] if p < 6 else last[(p - 6) * WIN : (p - 5) * WIN, :]
        y = (x - table[:, p : p + 1]) * table[:, PATCHES + p : PATCHES + p + 1] * shard[25:26, :]
        total = total + lax.dot_general(
            y.astype(BF), heads[p], (((1,), (1,)), ((), ())), preferred_element_type=F32
        )
    share = 1.0 / (1.0 + counts[...])
    members = share.shape[0]
    here = lax.broadcasted_iota(jnp.int32, (members, WIN), 0) == slot
    mine_share = jnp.sum(jnp.where(here, share, 0.0), axis=0, keepdims=True)
    factor = info[1:2, :] * mine_share / jnp.sum(share, axis=0, keepdims=True)
    scr[:, :HORIZONS] = total
    scr[:, HORIZONS:] = jnp.zeros((WIN, WIN - HORIZONS), F32)
    scr[...] = scr[...].T * factor
    for c in range(2):
        for out, side in ((keep, core), (send, 1 - core)):
            out[24 * c : 24 * c + 24, :] = scr[pl.ds(pl.multiple_of(48 * c + 24 * side, 8), 24), :]


def rank_kernel(levels, own, total, info, target, average, levels_out, scr, res, ranks):
    t = lax.axis_index("tensor")
    slot = lax.axis_index("member")
    per = total.shape[0]
    pred = total[...] + info[0:1, :]
    wanted = target[pl.ds(pl.multiple_of(24 * t, 8), per), :]
    resid = jnp.abs(wanted - pred)
    scr[...] = jnp.zeros((WIN, WIN), F32)
    scr[:per, :] = pred
    scr[...] = scr[...].T
    if own % 8 == 0:
        average[...] = scr[pl.ds(pl.multiple_of(own * slot, 8), own), :per]
    else:
        at = own * slot
        rows = scr[pl.ds(pl.multiple_of((at // 8) * 8, 8), 8), :per]
        pick = rows[:own]
        for s in range(1, 8 // own):
            pick = jnp.where(at % 8 == s * own, rows[s * own : (s + 1) * own], pick)
        average[...] = pick
    res[...] = jnp.zeros((WIN, WIN), F32)
    res[:per, :] = resid
    across = res[...].T
    j = lax.broadcasted_iota(jnp.int32, (WIN, WIN), 0)
    i = lax.broadcasted_iota(jnp.int32, (WIN, WIN), 1)
    earlier = j < i
    for h in range(per):
        row, col = resid[h : h + 1, :], across[:, h : h + 1]
        before = (col < row) | ((col == row) & earlier)
        ranks[h : h + 1, :] = jnp.sum(before.astype(F32), axis=0, keepdims=True)
    order = ranks[...]
    lane = lax.broadcasted_iota(jnp.int32, (per, WIN), 1)
    table = jnp.zeros((per, WIN), F32)
    for n, level in enumerate(levels):
        value = jnp.sum(jnp.where(order == float(level), resid, 0.0), axis=1, keepdims=True)
        table = jnp.where(lane == n, value, table)
    res[:per, :] = table
    levels_out[...] = res[...].T[: len(levels), :per]


def per_device(series, starts, counts, lifting, location, gain_one, up, down, gain_two, readout):
    members = lax.axis_size("member")
    own = counts.shape[1]
    sds = jax.ShapeDtypeStruct

    def over_tensor(x, k):
        return lax.ppermute(x, "tensor", [(i, i ^ k) for i in range(4)])

    def over_member(x, k):
        return lax.ppermute(x, "member", [(i, i ^ k) for i in range(members)])

    shard_bf = pltpu.VMEM((D, SHARD), BF)
    packed, every, give_x = call(
        pack_kernel,
        (pltpu.VMEM((32, SHARD), F32), pltpu.VMEM((members, WIN), F32), shard_bf),
        [HBM] * 6,
        (lifting, location, gain_one, gain_two, counts.T, down),
        2 * US,
        1000,
        [
            pltpu.VMEM((1, SHARD), F32),
            pltpu.VMEM((1, SHARD), F32),
            pltpu.VMEM((own, members), jnp.int32),
            pltpu.VMEM((WIN, WIN), F32),
            pltpu.SemaphoreType.DMA((6,)),
        ],
    )
    shards = [packed] + [over_tensor(packed, k) for k in (1, 2, 3)]
    peer_x = over_tensor(give_x, 1)

    heads = jnp.swapaxes(readout[0], 1, 2)
    up = up[0]
    own_x, own_y, give_y, heads_v, q, info, target, half = call(
        windows_kernel,
        (
            shard_bf,
            shard_bf,
            shard_bf,
            pltpu.VMEM((PATCHES, HORIZONS, SHARD), BF),
            pltpu.VMEM((PATCHES, WIN, KCAT), BF),
            pltpu.VMEM((8, WIN), F32),
            pltpu.VMEM((WIN, WIN), F32),
            pltpu.VMEM((32, HIDDEN), F32),
        ),
        [HBM] * 4 + [V] * 3,
        (series.reshape(WIN, WIN), starts.reshape(1, WIN), down, heads, up, packed, shards[1]),
        5 * US,
        1000,
        [
            pltpu.VMEM((WIN, WIN), F32),
            pltpu.VMEM((1, WIN), jnp.int32),
            pltpu.VMEM((2, 96, SHARD), BF),
            pltpu.SemaphoreType.DMA((6,)),
        ],
    )

    hops = [k for k in (1, 3, 8, 24) if k < members]
    steps = iter(hops + [4] * (members > 4))

    def hop(value, after=None):
        k = next(steps, None)
        if after is not None:
            value = lax.optimization_barrier((value, after))[0]
        return value if k is None else value + over_member(value, k)

    every = hop(every)
    m24, ecat = call(
        lift_kernel,
        (pltpu.VMEM((32, HIDDEN), F32), pltpu.VMEM((4, KCAT, SHARD), BF)),
        [V] * 6,
        (up, *shards, half),
        3 * US,
        1000,
        [pltpu.VMEM((2, 96, SHARD), BF)],
        after=(every,),
    )
    m24_peer = over_tensor(m24, 1)
    mcat_shape = pltpu.VMEM((KCAT, HIDDEN), BF)
    rstd, m_own = call(
        scale_kernel,
        (pltpu.VMEM((PATCHES, WIN, 128), F32), mcat_shape),
        [V] * 3,
        (q, ecat, m24),
        2 * US,
        1000,
    )
    sums = (pltpu.VMEM((2 * WIN, 2 * HIDDEN), BF), pltpu.VMEM((2 * WIN, SHARD), BF))
    m_peer, act, send = call(
        first_away_kernel,
        (mcat_shape,) + sums,
        [V] * 6,
        (q, rstd, m_own, m24_peer, own_x, peer_x),
        4 * US,
        1000,
    )
    acts, crossed = [act], [over_tensor(send, 2)]
    fed = (q, rstd, m_own, m_peer, own_x, peer_x)
    peer_y = over_tensor(lax.optimization_barrier((give_y, send))[0], 1)
    for g in range(1, 4):
        act, send = call(
            functools.partial(away_kernel, g),
            sums,
            [V] * 6,
            fed,
            4 * US,
            1000,
            after=(every, crossed[g - 2]) if g > 1 else (),
        )
        acts.append(act)
        crossed.append(over_tensor(send, 2))
        every = hop(every, send)
    homes = (q, ecat, own_y, peer_y)
    (part,) = call(
        home_kernel,
        (pltpu.VMEM((4 * WIN, SHARD), F32),),
        [V] * 6,
        (*homes, *acts[:2]),
        US // 10,
        1000,
        after=(send,),
    )
    state, last, stats = call(
        state_kernel,
        (
            pltpu.VMEM((6 * WIN, SHARD), F32),
            pltpu.VMEM((2 * WIN, SHARD), F32),
            pltpu.VMEM((2 * PATCHES, WIN), F32),
        ),
        [V] * 10,
        (*homes, *acts[2:], part, *crossed[:3]),
        5 * US,
        1000,
        after=(every,),
    )
    every = hop(every, part)
    last, stats = call(
        last_state_kernel,
        (pltpu.VMEM((2 * WIN, SHARD), F32), pltpu.VMEM((2 * PATCHES, WIN), F32)),
        [V] * 3,
        (last, crossed[3], stats),
        US,
        1000,
        after=(every,),
    )
    features = SHARD
    for k in (1, 2):
        other = over_tensor(stats, k)
        gap = stats[:PATCHES] - other[:PATCHES]
        square = stats[PATCHES:] + other[PATCHES:] + (0.5 * features) * (gap * gap)
        stats = jnp.concatenate([0.5 * (stats[:PATCHES] + other[:PATCHES]), square], axis=0)
        features *= 2
    sent, held = call(
        head_kernel,
        (pltpu.VMEM((48, WIN), F32),) * 2,
        [V] * 7,
        (stats, state, last, heads_v, packed, info, every),
        US,
        1000,
        [pltpu.VMEM((WIN, WIN), F32)],
    )
    total = held + over_tensor(sent, 1)
    total = total + over_tensor(total, 2)
    if members > 4:
        pairs = [(4 * m + t, 4 * (m ^ 4) + (t ^ 2)) for m in range(members) for t in range(4)]
        total = total + lax.ppermute(total, ("member", "tensor"), pairs)
    total = lax.dynamic_slice_in_dim(total, 24 * ((lax.axis_index("tensor") >> 1)), 24, 0)
    for k in hops:
        total = total + over_member(total, k)

    levels = tuple(WIN * n // 100 for n in (50, 80, 90, 95))
    return call(
        functools.partial(rank_kernel, levels, own),
        (sds((own, 24), F32), sds((4, 24), F32)),
        [V] * 3,
        (total, info, target),
        US,
        1000,
        [pltpu.VMEM((WIN, WIN), F32), pltpu.VMEM((WIN, WIN), F32), pltpu.VMEM((24, WIN), F32)],
    )


def solution(mesh):
    placed = (
        P(),
        P(),
        P(None, "member"),
        P("member", None, "tensor"),
        P("member", None, "tensor"),
        P("member", "tensor"),
        P("member", None, "tensor"),
        P("member", "tensor", None),
        P("member", "tensor"),
        P("member", None, "tensor", None),
    )
    return jax.shard_map(
        per_device,
        mesh=mesh,
        in_specs=placed,
        out_specs=(P("member", "tensor"), P(None, "tensor")),
        check_vma=False,
    )
```

```python
import functools
import math

import jax
import jax.numpy as jnp
from jax import lax
from jax.experimental import pallas as pl
from jax.experimental.pallas import tpu as pltpu
from jax.sharding import PartitionSpec as P

BF, F32 = jnp.bfloat16, jnp.float32
PATCHES, PLEN, STRIDE, LOOK = 8, 16, 8, 72
WIN, D, SHARD, HIDDEN, HORIZONS = 128, 2048, 512, 2048, 96
KCAT = 256
MIB = 1 << 20
US = 10**9


def split3(x):
    a = x.astype(BF)
    rest = x - a.astype(F32)
    b = rest.astype(BF)
    c = (rest - b.astype(F32)).astype(BF)
    return a, b, c


def dot(a, b):
    return jnp.dot(a, b, preferred_element_type=F32)


def roll_left(x, by):
    lanes = x.shape[1]
    by = by % lanes
    return x if by == 0 else pltpu.roll(x, lanes - by, 1)


def shard_cols(t):
    return pl.ds(pl.multiple_of(SHARD * t, SHARD), SHARD)


def call(body, out_shape, in_specs, args, flops, nbytes, scratch=(), limit=24 * MIB, after=()):
    taken, held = len(in_specs), len(after)

    def run(*refs):
        body(*refs[:taken], *refs[taken + held :])

    args = tuple(
        pltpu.with_memory_space_constraint(x, pltpu.HBM if spec is HBM else pltpu.VMEM)
        for x, spec in zip(args, in_specs)
    ) + tuple(after)
    in_specs = list(in_specs) + [ANY] * held
    return pl.pallas_call(
        run,
        out_shape=out_shape,
        in_specs=in_specs,
        out_specs=jax.tree.map(lambda _: pl.BlockSpec(memory_space=pltpu.VMEM), out_shape),
        scratch_shapes=list(scratch),
        compiler_params=pltpu.CompilerParams(vmem_limit_bytes=limit),
        cost_estimate=pl.CostEstimate(flops=flops, bytes_accessed=nbytes, transcendentals=0),
    )(*args)


V = pl.BlockSpec(memory_space=pltpu.VMEM)
ANY = pl.BlockSpec(memory_space=pl.ANY)
HBM = pl.BlockSpec(memory_space=pltpu.HBM)


def pack_kernel(lifting, location, gain_one, gain_two, counts_h, down, packed, every, give, g1, g2, counts, scr, sem):
    t = lax.axis_index("tensor")
    loads = [
        pltpu.make_async_copy(lifting.at[0], packed.at[0:PLEN, :], sem.at[0]),
        pltpu.make_async_copy(location.at[0], packed.at[PLEN : PLEN + PATCHES, :], sem.at[1]),
        pltpu.make_async_copy(gain_one, g1, sem.at[2]),
        pltpu.make_async_copy(gain_two, g2, sem.at[3]),
        pltpu.make_async_copy(counts_h, counts, sem.at[4]),
        pltpu.make_async_copy(down.at[0, :, shard_cols(t ^ 3)], give, sem.at[5]),
    ]
    for load in loads:
        load.start()
    own, members = counts.shape
    scr[...] = jnp.zeros((WIN, WIN), F32)
    for load in loads[:5]:
        load.wait()
    row = lax.broadcasted_iota(jnp.int32, (8, SHARD), 0)
    packed[PLEN + PATCHES :, :] = jnp.where(row == 0, g1[...], jnp.where(row == 1, g2[...], 0.0))
    scr[:own, :members] = counts[...].astype(F32)
    columns = scr[...].T[:members]
    at = own * lax.axis_index("member")
    place = lax.broadcasted_iota(jnp.int32, (members, WIN), 1) - at
    placed = jnp.zeros((members, WIN), F32)
    for j in range(own):
        placed = jnp.where(place == j, columns[:, j : j + 1], placed)
    every[...] = placed
    loads[5].wait()


def lift_parts(t, shards, up, lhs):
    for n, (k, shard) in enumerate(shards):
        gain = shard[PLEN + PATCHES : PLEN + PATCHES + 1, :]
        row = lax.broadcasted_iota(jnp.int32, (32, SHARD), 0)
        rows = jnp.where(row < PLEN + PATCHES, shard[...] * gain, jnp.where(row == PLEN + PATCHES, gain, 0.0))
        for i, part in enumerate(split3(rows)):
            lhs[n, 32 * i : 32 * i + 32, :] = part
    for j in range(HIDDEN // 512):
        cols = slice(512 * j, 512 * j + 512)
        m = sum(dot(lhs[n], up[shard_cols(t ^ k), cols]) for n, (k, _) in enumerate(shards))
        yield cols, m[:32] + m[32:64] + m[64:96]


def windows_kernel(
    series_h, starts_h, down, heads_h, up, s0, s1,
    own_x, own_y, give_y, heads, q, info, target, half, series, starts, lhs, sem,
):
    t = lax.axis_index("tensor")
    small = [
        pltpu.make_async_copy(series_h, series, sem.at[0]),
        pltpu.make_async_copy(starts_h, starts, sem.at[1]),
    ]
    loads = [
        pltpu.make_async_copy(down.at[0, :, shard_cols(t ^ 2)], own_x, sem.at[2]),
        pltpu.make_async_copy(heads_h, heads, sem.at[3]),
        pltpu.make_async_copy(down.at[0, :, shard_cols(t ^ 1)], give_y, sem.at[4]),
        pltpu.make_async_copy(down.at[0, :, shard_cols(t)], own_y, sem.at[5]),
    ]
    for load in small + loads:
        load.start()
    for cols, m in lift_parts(t, ((0, s0), (1, s1)), up, lhs):
        half[:, cols] = m
    for load in small:
        load.wait()
    lane = lax.broadcasted_iota(jnp.int32, (WIN, WIN), 1)
    first = jnp.broadcast_to(starts[...].astype(F32), (WIN, WIN)).T.astype(jnp.int32)
    row, offset = first >> 7, first & 127
    picks = [(row + k == lane).astype(F32).astype(BF) for k in range(3)]
    parts = split3(series[...])
    rows = [sum(dot(pick, part) for part in parts) for pick in picks]
    x = jnp.concatenate(rows, axis=1)
    offset = jnp.concatenate([offset] * 3, axis=1)
    for bit in range(7):
        x = jnp.where((offset >> bit) & 1 == 1, roll_left(x, 1 << bit), x)
    target[...] = roll_left(x, LOOK)[:, :WIN].T
    look = x[:, :WIN]
    center = jnp.sum(jnp.where(lane < LOOK, look, 0.0), axis=1, keepdims=True) * (1.0 / LOOK)
    dev = jnp.where(lane < LOOK, look - center, 0.0)
    spread = jnp.sqrt(jnp.sum(dev * dev, axis=1, keepdims=True) * (1.0 / LOOK) + 1e-05)
    normed = dev / spread
    pair = jnp.where(lane == 0, center, jnp.where(lane == 1, spread, 0.0)).T
    info[...] = pair[:8]
    block = lane // 32
    for p in range(PATCHES):
        one = jnp.where(lane < PLEN, roll_left(normed, STRIDE * p), 0.0)
        one = jnp.where(lane == PLEN + p, 1.0, one)
        two = one + pltpu.roll(one, 32, 1)
        four = two + pltpu.roll(two, 64, 1)
        a, b, c = (v.astype(F32) for v in split3(four))
        q[p, :, :WIN] = jnp.where(block < 2, a, b).astype(BF)
        q[p, :, WIN:] = jnp.where(block == 0, a, jnp.where(block == 1, c, 0.0)).astype(BF)
    for load in loads:
        load.wait()


def cat_rows(x):
    b1, b2, b3 = split3(x)
    zero = jnp.zeros_like(b1)
    return [b1, b2, b1, b2, b3, b1, zero, zero]


def lift_kernel(up, s0, s1, s2, s3, half, m24, ecat, lhs):
    t = lax.axis_index("tensor")
    shards = (s0, s1, s2, s3)
    mean = sum(jnp.sum(s[...], axis=1, keepdims=True) for s in shards) * (1.0 / D)
    keep = lax.broadcasted_iota(jnp.int32, (32, SHARD), 0) < PLEN + PATCHES
    for cols, m in lift_parts(t, ((2, s2), (3, s3)), up, lhs):
        m = m + half[:, cols]
        m24[:, cols] = m - mean * m[PLEN + PATCHES : PLEN + PATCHES + 1, :]
    for k, shard in enumerate(shards):
        centred = jnp.where(keep, shard[...] - mean, 0.0)
        for i, part in enumerate(cat_rows(centred)):
            ecat[k, 32 * i : 32 * i + 32, :] = part


def spread_rows(m24, mcat):
    for j in range(HIDDEN // 512):
        cols = slice(512 * j, 512 * j + 512)
        row = lax.broadcasted_iota(jnp.int32, (32, 512), 0)
        for i, part in enumerate(cat_rows(jnp.where(row < PLEN + PATCHES, m24[:, cols], 0.0))):
            mcat[32 * i : 32 * i + 32, cols] = part


def scale_kernel(q, ecat, m24, rstd, mcat):
    spread_rows(m24, mcat)
    for p in range(0, PATCHES, 2):
        square = jnp.zeros((2 * WIN, 128), F32)
        for k in range(4):
            dev = dot(q[p : p + 2].reshape(2 * WIN, KCAT), ecat[k])
            for c in range(SHARD // 128):
                piece = dev[:, 128 * c : 128 * c + 128]
                square = square + piece * piece
        var = jnp.sum(square, axis=1, keepdims=True) * (1.0 / D)
        rstd[p : p + 2] = jnp.broadcast_to(lax.rsqrt(var + 1e-05), (2 * WIN, 128)).reshape(2, WIN, 128)


def gelu(h):
    c = math.sqrt(2.0 / math.pi)
    half = 0.5 * h
    return half + half * jnp.tanh(h * (c + (c * 0.044715) * (h * h)))


def away_body(g, q, rstd, mcats, downs, act, send):
    rows = q[2 * g : 2 * g + 2].reshape(2 * WIN, KCAT)
    scale = rstd[2 * g : 2 * g + 2].reshape(2 * WIN, 128)[:, :1]
    total = jnp.zeros((2 * WIN, SHARD), F32)
    for side in range(2):
        for j in range(HIDDEN // 512):
            cols = slice(512 * j, 512 * j + 512)
            at = slice(HIDDEN * side + 512 * j, HIDDEN * side + 512 * (j + 1))
            act[:, at] = gelu(dot(rows, mcats[side][:, cols]) * scale).astype(BF)
    for side in range(2):
        total = total + dot(act[:, HIDDEN * side : HIDDEN * (side + 1)], downs[side][...])
    send[...] = total.astype(BF)


def first_away_kernel(q, rstd, m_own, m24_peer, d_own, d_peer, m_peer, act, send):
    spread_rows(m24_peer, m_peer)
    away_body(0, q, rstd, (m_own, m_peer), (d_own, d_peer), act, send)


def away_kernel(g, q, rstd, m_own, m_peer, d_own, d_peer, act, send):
    away_body(g, q, rstd, (m_own, m_peer), (d_own, d_peer), act, send)


def add_stats(table, p, x):
    lane = lax.broadcasted_iota(jnp.int32, (WIN, WIN), 1)
    mean = jnp.sum(x, axis=1, keepdims=True) * (1.0 / SHARD)
    off = x - mean
    square = jnp.sum(off * off, axis=1, keepdims=True)
    return jnp.where(lane == p, mean, jnp.where(lane == PATCHES + p, square, table))


def home_rows(g, q, ecat, d_own, d_peer, act):
    x = dot(act[:, :HIDDEN], d_own[...]) + dot(act[:, HIDDEN:], d_peer[...])
    return x + dot(q[2 * g : 2 * g + 2].reshape(2 * WIN, KCAT), ecat[0])


def home_kernel(q, ecat, d_own, d_peer, a0, a1, part):
    for g, act in enumerate((a0, a1)):
        part[2 * WIN * g : 2 * WIN * (g + 1), :] = home_rows(g, q, ecat, d_own, d_peer, act)


def state_kernel(q, ecat, d_own, d_peer, a2, a3, part, c0, c1, c2, mine, late, state, last, stats, every):
    every[...] = mine[...] + late[...]
    last[...] = home_rows(3, q, ecat, d_own, d_peer, a3)
    table = jnp.zeros((WIN, WIN), F32)
    for g, cross in enumerate((c0, c1, c2)):
        rows = slice(2 * WIN * g, 2 * WIN * (g + 1))
        x = part[rows, :] if g < 2 else home_rows(2, q, ecat, d_own, d_peer, a2)
        x = x + cross[...].astype(F32)
        state[rows, :] = x
        table = add_stats(table, 2 * g, x[:WIN])
        table = add_stats(table, 2 * g + 1, x[WIN:])
    stats[...] = table.T[: 2 * PATCHES]


def last_state_kernel(last, cross, prev, state, stats):
    x = last[...] + cross[...].astype(F32)
    state[...] = x
    table = add_stats(jnp.zeros((WIN, WIN), F32), 6, x[:WIN])
    table = add_stats(table, 7, x[WIN:])
    stats[...] = prev[...] + table.T[: 2 * PATCHES]


def head_kernel(stats, state, last, heads, shard, send, keep, scr):
    core = lax.axis_index("tensor") & 1
    scale = lax.rsqrt(stats[PATCHES:, :] * (1.0 / D) + 1e-05)
    table = jnp.concatenate([stats[:PATCHES, :], scale, jnp.zeros((WIN - 2 * PATCHES, WIN), F32)], axis=0).T
    total = jnp.zeros((WIN, HORIZONS), F32)
    for p in range(PATCHES):
        x = state[p * WIN : (p + 1) * WIN, :] if p < 6 else last[(p - 6) * WIN : (p - 5) * WIN, :]
        y = (x - table[:, p : p + 1]) * table[:, PATCHES + p : PATCHES + p + 1] * shard[25:26, :]
        total = total + lax.dot_general(
            y.astype(BF), heads[p], (((1,), (1,)), ((), ())), preferred_element_type=F32
        )
    scr[:, :HORIZONS] = total
    scr[:, HORIZONS:] = jnp.zeros((WIN, WIN - HORIZONS), F32)
    scr[...] = scr[...].T
    for c in range(2):
        for out, side in ((keep, core), (send, 1 - core)):
            out[24 * c : 24 * c + 24, :] = scr[pl.ds(pl.multiple_of(48 * c + 24 * side, 8), 24), :]


def weigh_kernel(mine, theirs, info, counts, out):
    share = 1.0 / (1.0 + counts[...])
    here = lax.broadcasted_iota(jnp.int32, share.shape, 0) == lax.axis_index("member")
    own = jnp.sum(jnp.where(here, share, 0.0), axis=0, keepdims=True)
    factor = info[1:2, :] * own / jnp.sum(share, axis=0, keepdims=True)
    out[...] = (mine[...] + theirs[...]) * factor


def rank_kernel(levels, own, total, info, target, average, levels_out, scr, res, ranks):
    t = lax.axis_index("tensor")
    slot = lax.axis_index("member")
    per = total.shape[0]
    pred = total[...] + info[0:1, :]
    wanted = target[pl.ds(pl.multiple_of(24 * t, 8), per), :]
    resid = jnp.abs(wanted - pred)
    scr[...] = jnp.zeros((WIN, WIN), F32)
    scr[:per, :] = pred
    scr[...] = scr[...].T
    if own % 8 == 0:
        average[...] = scr[pl.ds(pl.multiple_of(own * slot, 8), own), :per]
    else:
        at = own * slot
        rows = scr[pl.ds(pl.multiple_of((at // 8) * 8, 8), 8), :per]
        pick = rows[:own]
        for s in range(1, 8 // own):
            pick = jnp.where(at % 8 == s * own, rows[s * own : (s + 1) * own], pick)
        average[...] = pick
    res[...] = jnp.zeros((WIN, WIN), F32)
    res[:per, :] = resid
    across = res[...].T
    j = lax.broadcasted_iota(jnp.int32, (WIN, WIN), 0)
    i = lax.broadcasted_iota(jnp.int32, (WIN, WIN), 1)
    earlier = j < i
    for h in range(per):
        row, col = resid[h : h + 1, :], across[:, h : h + 1]
        before = (col < row) | ((col == row) & earlier)
        ranks[h : h + 1, :] = jnp.sum(before.astype(F32), axis=0, keepdims=True)
    order = ranks[...]
    lane = lax.broadcasted_iota(jnp.int32, (per, WIN), 1)
    table = jnp.zeros((per, WIN), F32)
    for n, level in enumerate(levels):
        value = jnp.sum(jnp.where(order == float(level), resid, 0.0), axis=1, keepdims=True)
        table = jnp.where(lane == n, value, table)
    res[:per, :] = table
    levels_out[...] = res[...].T[: len(levels), :per]


def per_device(series, starts, counts, lifting, location, gain_one, up, down, gain_two, readout):
    members = lax.axis_size("member")
    own = counts.shape[1]
    sds = jax.ShapeDtypeStruct

    def over_tensor(x, k):
        return lax.ppermute(x, "tensor", [(i, i ^ k) for i in range(4)])

    def over_member(x, k):
        return lax.ppermute(x, "member", [(i, i ^ k) for i in range(members)])

    shard_bf = pltpu.VMEM((D, SHARD), BF)
    packed, every, give_x = call(
        pack_kernel,
        (pltpu.VMEM((32, SHARD), F32), pltpu.VMEM((members, WIN), F32), shard_bf),
        [HBM] * 6,
        (lifting, location, gain_one, gain_two, counts.T, down),
        2 * US,
        1000,
        [
            pltpu.VMEM((1, SHARD), F32),
            pltpu.VMEM((1, SHARD), F32),
            pltpu.VMEM((own, members), jnp.int32),
            pltpu.VMEM((WIN, WIN), F32),
            pltpu.SemaphoreType.DMA((6,)),
        ],
    )
    shards = [packed] + [over_tensor(packed, k) for k in (1, 2, 3)]
    peer_x = over_tensor(give_x, 1)

    heads = jnp.swapaxes(readout[0], 1, 2)
    up = up[0]
    own_x, own_y, give_y, heads_v, q, info, target, half = call(
        windows_kernel,
        (
            shard_bf,
            shard_bf,
            shard_bf,
            pltpu.VMEM((PATCHES, HORIZONS, SHARD), BF),
            pltpu.VMEM((PATCHES, WIN, KCAT), BF),
            pltpu.VMEM((8, WIN), F32),
            pltpu.VMEM((WIN, WIN), F32),
            pltpu.VMEM((32, HIDDEN), F32),
        ),
        [HBM] * 4 + [V] * 3,
        (series.reshape(WIN, WIN), starts.reshape(1, WIN), down, heads, up, packed, shards[1]),
        5 * US,
        1000,
        [
            pltpu.VMEM((WIN, WIN), F32),
            pltpu.VMEM((1, WIN), jnp.int32),
            pltpu.VMEM((2, 96, SHARD), BF),
            pltpu.SemaphoreType.DMA((6,)),
        ],
    )

    hops = [k for k in (1, 3, 8, 24) if k < members]
    steps = iter(hops + [4] * (members > 4))

    def hop(value, after=None):
        k = next(steps, None)
        if after is not None:
            value = lax.optimization_barrier((value, after))[0]
        return value if k is None else value + over_member(value, k)

    def hop_parts(value, after):
        k = next(steps, None)
        value = lax.optimization_barrier((value, after))[0]
        return value, jnp.zeros_like(value) if k is None else over_member(value, k)

    m24, ecat = call(
        lift_kernel,
        (pltpu.VMEM((32, HIDDEN), F32), pltpu.VMEM((4, KCAT, SHARD), BF)),
        [V] * 6,
        (up, *shards, half),
        3 * US,
        1000,
        [pltpu.VMEM((2, 96, SHARD), BF)],
    )
    m24_peer = over_tensor(m24, 1)
    mcat_shape = pltpu.VMEM((KCAT, HIDDEN), BF)
    rstd, m_own = call(
        scale_kernel,
        (pltpu.VMEM((PATCHES, WIN, 128), F32), mcat_shape),
        [V] * 3,
        (q, ecat, m24),
        2 * US,
        1000,
    )
    sums = (pltpu.VMEM((2 * WIN, 2 * HIDDEN), BF), pltpu.VMEM((2 * WIN, SHARD), BF))
    m_peer, act, send = call(
        first_away_kernel,
        (mcat_shape,) + sums,
        [V] * 6,
        (q, rstd, m_own, m24_peer, own_x, peer_x),
        4 * US,
        1000,
    )
    acts, crossed = [act], [over_tensor(send, 2)]
    fed = (q, rstd, m_own, m_peer, own_x, peer_x)
    peer_y = over_tensor(lax.optimization_barrier((give_y, send))[0], 1)
    for g in range(1, 4):
        act, send = call(
            functools.partial(away_kernel, g),
            sums,
            [V] * 6,
            fed,
            4 * US,
            1000,
            after=(every, crossed[g - 2]) if g > 1 else (),
        )
        acts.append(act)
        crossed.append(over_tensor(send, 2))
        if g == 1:
            every = hop(every, send)
    every, late = hop_parts(every, send)
    homes = (q, ecat, own_y, peer_y)
    (part,) = call(
        home_kernel,
        (pltpu.VMEM((4 * WIN, SHARD), F32),),
        [V] * 6,
        (*homes, *acts[:2]),
        US // 10,
        1000,
        after=(send,),
    )
    state, last, stats, every = call(
        state_kernel,
        (
            pltpu.VMEM((6 * WIN, SHARD), F32),
            pltpu.VMEM((2 * WIN, SHARD), F32),
            pltpu.VMEM((2 * PATCHES, WIN), F32),
            pltpu.VMEM((members, WIN), F32),
        ),
        [V] * 12,
        (*homes, *acts[2:], part, *crossed[:3], every, late),
        5 * US,
        1000,
    )
    every = hop(every)
    last, stats = call(
        last_state_kernel,
        (pltpu.VMEM((2 * WIN, SHARD), F32), pltpu.VMEM((2 * PATCHES, WIN), F32)),
        [V] * 3,
        (last, crossed[3], stats),
        US,
        1000,
        after=(every,),
    )
    features = SHARD
    for k in (1, 2):
        other = over_tensor(stats, k)
        gap = stats[:PATCHES] - other[:PATCHES]
        square = stats[PATCHES:] + other[PATCHES:] + (0.5 * features) * (gap * gap)
        stats = jnp.concatenate([0.5 * (stats[:PATCHES] + other[:PATCHES]), square], axis=0)
        features *= 2
        if k == 1:
            every = hop(every, stats)
    sent, held = call(
        head_kernel,
        (pltpu.VMEM((48, WIN), F32),) * 2,
        [V] * 5,
        (stats, state, last, heads_v, packed),
        US,
        1000,
        [pltpu.VMEM((WIN, WIN), F32)],
        after=(every,),
    )
    total = held + over_tensor(sent, 1)
    every = hop(every, sent)
    (total,) = call(
        weigh_kernel,
        (pltpu.VMEM((48, WIN), F32),),
        [V] * 4,
        (total, over_tensor(total, 2), info, every),
        US,
        1000,
    )
    if members > 4:
        pairs = [(4 * m + t, 4 * (m ^ 4) + (t ^ 2)) for m in range(members) for t in range(4)]
        total = total + lax.ppermute(total, ("member", "tensor"), pairs)
    total = lax.dynamic_slice_in_dim(total, 24 * ((lax.axis_index("tensor") >> 1)), 24, 0)
    for k in hops:
        total = total + over_member(total, k)

    levels = tuple(WIN * n // 100 for n in (50, 80, 90, 95))
    return call(
        functools.partial(rank_kernel, levels, own),
        (sds((own, 24), F32), sds((4, 24), F32)),
        [V] * 3,
        (total, info, target),
        US,
        1000,
        [pltpu.VMEM((WIN, WIN), F32), pltpu.VMEM((WIN, WIN), F32), pltpu.VMEM((24, WIN), F32)],
    )


def solution(mesh):
    placed = (
        P(),
        P(),
        P(None, "member"),
        P("member", None, "tensor"),
        P("member", None, "tensor"),
        P("member", "tensor"),
        P("member", None, "tensor"),
        P("member", "tensor", None),
        P("member", "tensor"),
        P("member", None, "tensor", None),
    )
    return jax.shard_map(
        per_device,
        mesh=mesh,
        in_specs=placed,
        out_specs=(P("member", "tensor"), P(None, "tensor")),
        check_vma=False,
    )
```

```python
import functools
import math

import jax
import jax.numpy as jnp
from jax import lax
from jax.experimental import pallas as pl
from jax.experimental.pallas import tpu as pltpu
from jax.sharding import PartitionSpec as P

BF, F32 = jnp.bfloat16, jnp.float32
PATCHES, PLEN, STRIDE, LOOK = 8, 16, 8, 72
WIN, D, SHARD, HIDDEN, HORIZONS = 128, 2048, 512, 2048, 96
KCAT = 256
MIB = 1 << 20
US = 10**9


def split3(x):
    a = x.astype(BF)
    rest = x - a.astype(F32)
    b = rest.astype(BF)
    c = (rest - b.astype(F32)).astype(BF)
    return a, b, c


def dot(a, b):
    return jnp.dot(a, b, preferred_element_type=F32)


def roll_left(x, by):
    lanes = x.shape[1]
    by = by % lanes
    return x if by == 0 else pltpu.roll(x, lanes - by, 1)


def shard_cols(t):
    return pl.ds(pl.multiple_of(SHARD * t, SHARD), SHARD)


def call(body, out_shape, in_specs, args, flops, nbytes, scratch=(), limit=24 * MIB, after=()):
    taken, held = len(in_specs), len(after)

    def run(*refs):
        body(*refs[:taken], *refs[taken + held :])

    args = tuple(
        pltpu.with_memory_space_constraint(x, pltpu.HBM if spec is HBM else pltpu.VMEM)
        for x, spec in zip(args, in_specs)
    ) + tuple(after)
    in_specs = list(in_specs) + [ANY] * held
    return pl.pallas_call(
        run,
        out_shape=out_shape,
        in_specs=in_specs,
        out_specs=jax.tree.map(lambda _: pl.BlockSpec(memory_space=pltpu.VMEM), out_shape),
        scratch_shapes=list(scratch),
        compiler_params=pltpu.CompilerParams(vmem_limit_bytes=limit),
        cost_estimate=pl.CostEstimate(flops=flops, bytes_accessed=nbytes, transcendentals=0),
    )(*args)


V = pl.BlockSpec(memory_space=pltpu.VMEM)
ANY = pl.BlockSpec(memory_space=pl.ANY)
HBM = pl.BlockSpec(memory_space=pltpu.HBM)


def pack_kernel(lifting, location, gain_one, gain_two, counts_h, down, packed, every, give, g1, g2, counts, scr, sem):
    t = lax.axis_index("tensor")
    loads = [
        pltpu.make_async_copy(lifting.at[0], packed.at[0:PLEN, :], sem.at[0]),
        pltpu.make_async_copy(location.at[0], packed.at[PLEN : PLEN + PATCHES, :], sem.at[1]),
        pltpu.make_async_copy(gain_one, g1, sem.at[2]),
        pltpu.make_async_copy(gain_two, g2, sem.at[3]),
        pltpu.make_async_copy(counts_h, counts, sem.at[4]),
        pltpu.make_async_copy(down.at[0, :, shard_cols(t ^ 3)], give, sem.at[5]),
    ]
    for load in loads:
        load.start()
    own, members = counts.shape
    scr[...] = jnp.zeros((WIN, WIN), F32)
    for load in loads[:5]:
        load.wait()
    row = lax.broadcasted_iota(jnp.int32, (8, SHARD), 0)
    packed[PLEN + PATCHES :, :] = jnp.where(row == 0, g1[...], jnp.where(row == 1, g2[...], 0.0))
    scr[:own, :members] = counts[...].astype(F32)
    columns = scr[...].T[:members]
    at = own * lax.axis_index("member")
    place = lax.broadcasted_iota(jnp.int32, (members, WIN), 1) - at
    placed = jnp.zeros((members, WIN), F32)
    for j in range(own):
        placed = jnp.where(place == j, columns[:, j : j + 1], placed)
    every[...] = placed
    loads[5].wait()


def lift_parts(t, shards, up, lhs):
    for n, (k, shard) in enumerate(shards):
        gain = shard[PLEN + PATCHES : PLEN + PATCHES + 1, :]
        row = lax.broadcasted_iota(jnp.int32, (32, SHARD), 0)
        rows = jnp.where(row < PLEN + PATCHES, shard[...] * gain, jnp.where(row == PLEN + PATCHES, gain, 0.0))
        for i, part in enumerate(split3(rows)):
            lhs[n, 32 * i : 32 * i + 32, :] = part
    for j in range(HIDDEN // 512):
        cols = slice(512 * j, 512 * j + 512)
        m = sum(dot(lhs[n], up[shard_cols(t ^ k), cols]) for n, (k, _) in enumerate(shards))
        yield cols, m[:32] + m[32:64] + m[64:96]


def windows_kernel(
    series_h, starts_h, down, heads_h, up, s0, s1,
    own_x, own_y, give_y, heads, q, info, target, half, series, starts, lhs, sem,
):
    t = lax.axis_index("tensor")
    small = [
        pltpu.make_async_copy(series_h, series, sem.at[0]),
        pltpu.make_async_copy(starts_h, starts, sem.at[1]),
    ]
    loads = [
        pltpu.make_async_copy(down.at[0, :, shard_cols(t ^ 2)], own_x, sem.at[2]),
        pltpu.make_async_copy(heads_h, heads, sem.at[3]),
        pltpu.make_async_copy(down.at[0, :, shard_cols(t ^ 1)], give_y, sem.at[4]),
        pltpu.make_async_copy(down.at[0, :, shard_cols(t)], own_y, sem.at[5]),
    ]
    for load in small + loads:
        load.start()
    for cols, m in lift_parts(t, ((0, s0), (1, s1)), up, lhs):
        half[:, cols] = m
    for load in small:
        load.wait()
    lane = lax.broadcasted_iota(jnp.int32, (WIN, WIN), 1)
    first = jnp.broadcast_to(starts[...].astype(F32), (WIN, WIN)).T.astype(jnp.int32)
    row, offset = first >> 7, first & 127
    picks = [(row + k == lane).astype(F32).astype(BF) for k in range(3)]
    parts = split3(series[...])
    rows = [sum(dot(pick, part) for part in parts) for pick in picks]
    x = jnp.concatenate(rows, axis=1)
    offset = jnp.concatenate([offset] * 3, axis=1)
    for bit in range(7):
        x = jnp.where((offset >> bit) & 1 == 1, roll_left(x, 1 << bit), x)
    target[...] = roll_left(x, LOOK)[:, :WIN].T
    look = x[:, :WIN]
    center = jnp.sum(jnp.where(lane < LOOK, look, 0.0), axis=1, keepdims=True) * (1.0 / LOOK)
    dev = jnp.where(lane < LOOK, look - center, 0.0)
    spread = jnp.sqrt(jnp.sum(dev * dev, axis=1, keepdims=True) * (1.0 / LOOK) + 1e-05)
    normed = dev / spread
    pair = jnp.where(lane == 0, center, jnp.where(lane == 1, spread, 0.0)).T
    info[...] = pair[:8]
    block = lane // 32
    for p in range(PATCHES):
        one = jnp.where(lane < PLEN, roll_left(normed, STRIDE * p), 0.0)
        one = jnp.where(lane == PLEN + p, 1.0, one)
        two = one + pltpu.roll(one, 32, 1)
        four = two + pltpu.roll(two, 64, 1)
        a, b, c = (v.astype(F32) for v in split3(four))
        q[p, :, :WIN] = jnp.where(block < 2, a, b).astype(BF)
        q[p, :, WIN:] = jnp.where(block == 0, a, jnp.where(block == 1, c, 0.0)).astype(BF)
    for load in loads:
        load.wait()


def cat_rows(x):
    b1, b2, b3 = split3(x)
    zero = jnp.zeros_like(b1)
    return [b1, b2, b1, b2, b3, b1, zero, zero]


def lift_kernel(up, s0, s1, s2, s3, half, m24, ecat, lhs):
    t = lax.axis_index("tensor")
    shards = (s0, s1, s2, s3)
    mean = sum(jnp.sum(s[...], axis=1, keepdims=True) for s in shards) * (1.0 / D)
    keep = lax.broadcasted_iota(jnp.int32, (32, SHARD), 0) < PLEN + PATCHES
    for cols, m in lift_parts(t, ((2, s2), (3, s3)), up, lhs):
        m = m + half[:, cols]
        m24[:, cols] = m - mean * m[PLEN + PATCHES : PLEN + PATCHES + 1, :]
    for k, shard in enumerate(shards):
        centred = jnp.where(keep, shard[...] - mean, 0.0)
        for i, part in enumerate(cat_rows(centred)):
            ecat[k, 32 * i : 32 * i + 32, :] = part


def spread_rows(m24, mcat):
    for j in range(HIDDEN // 512):
        cols = slice(512 * j, 512 * j + 512)
        row = lax.broadcasted_iota(jnp.int32, (32, 512), 0)
        for i, part in enumerate(cat_rows(jnp.where(row < PLEN + PATCHES, m24[:, cols], 0.0))):
            mcat[32 * i : 32 * i + 32, cols] = part


def scale_kernel(q, ecat, m24, rstd, mcat):
    spread_rows(m24, mcat)
    for p in range(0, PATCHES, 2):
        square = jnp.zeros((2 * WIN, 128), F32)
        for k in range(4):
            dev = dot(q[p : p + 2].reshape(2 * WIN, KCAT), ecat[k])
            for c in range(SHARD // 128):
                piece = dev[:, 128 * c : 128 * c + 128]
                square = square + piece * piece
        var = jnp.sum(square, axis=1, keepdims=True) * (1.0 / D)
        rstd[p : p + 2] = jnp.broadcast_to(lax.rsqrt(var + 1e-05), (2 * WIN, 128)).reshape(2, WIN, 128)


def gelu(h):
    c = math.sqrt(2.0 / math.pi)
    half = 0.5 * h
    return half + half * jnp.tanh(h * (c + (c * 0.044715) * (h * h)))


def away_body(g, q, rstd, mcats, downs, act, send):
    rows = q[2 * g : 2 * g + 2].reshape(2 * WIN, KCAT)
    scale = rstd[2 * g : 2 * g + 2].reshape(2 * WIN, 128)[:, :1]
    total = jnp.zeros((2 * WIN, SHARD), F32)
    for side in range(2):
        for j in range(HIDDEN // 512):
            cols = slice(512 * j, 512 * j + 512)
            at = slice(HIDDEN * side + 512 * j, HIDDEN * side + 512 * (j + 1))
            act[:, at] = gelu(dot(rows, mcats[side][:, cols]) * scale).astype(BF)
    for side in range(2):
        total = total + dot(act[:, HIDDEN * side : HIDDEN * (side + 1)], downs[side][...])
    send[...] = total.astype(BF)


def first_away_kernel(q, rstd, m_own, m24_peer, d_own, d_peer, m_peer, act, send):
    spread_rows(m24_peer, m_peer)
    away_body(0, q, rstd, (m_own, m_peer), (d_own, d_peer), act, send)


def away_kernel(g, q, rstd, m_own, m_peer, d_own, d_peer, act, send):
    away_body(g, q, rstd, (m_own, m_peer), (d_own, d_peer), act, send)


def add_stats(table, p, x):
    lane = lax.broadcasted_iota(jnp.int32, (WIN, WIN), 1)
    mean = jnp.sum(x, axis=1, keepdims=True) * (1.0 / SHARD)
    off = x - mean
    square = jnp.sum(off * off, axis=1, keepdims=True)
    return jnp.where(lane == p, mean, jnp.where(lane == PATCHES + p, square, table))


def home_rows(g, q, ecat, d_own, d_peer, act):
    x = dot(act[:, :HIDDEN], d_own[...]) + dot(act[:, HIDDEN:], d_peer[...])
    return x + dot(q[2 * g : 2 * g + 2].reshape(2 * WIN, KCAT), ecat[0])


def home_kernel(q, ecat, d_own, d_peer, a0, a1, part):
    for g, act in enumerate((a0, a1)):
        part[2 * WIN * g : 2 * WIN * (g + 1), :] = home_rows(g, q, ecat, d_own, d_peer, act)


def state_kernel(q, ecat, d_own, d_peer, a2, a3, part, c0, c1, c2, mine, late, state, last, stats, every):
    every[...] = mine[...] + late[...]
    last[...] = home_rows(3, q, ecat, d_own, d_peer, a3)
    table = jnp.zeros((WIN, WIN), F32)
    for g, cross in enumerate((c0, c1, c2)):
        rows = slice(2 * WIN * g, 2 * WIN * (g + 1))
        x = part[rows, :] if g < 2 else home_rows(2, q, ecat, d_own, d_peer, a2)
        x = x + cross[...].astype(F32)
        state[rows, :] = x
        table = add_stats(table, 2 * g, x[:WIN])
        table = add_stats(table, 2 * g + 1, x[WIN:])
    stats[...] = table.T[: 2 * PATCHES]


def last_state_kernel(last, cross, prev, state, stats):
    x = last[...] + cross[...].astype(F32)
    state[...] = x
    table = add_stats(jnp.zeros((WIN, WIN), F32), 6, x[:WIN])
    table = add_stats(table, 7, x[WIN:])
    stats[...] = prev[...] + table.T[: 2 * PATCHES]


def head_kernel(stats, state, last, heads, shard, out, scr):
    scale = lax.rsqrt(stats[PATCHES:, :] * (1.0 / D) + 1e-05)
    table = jnp.concatenate([stats[:PATCHES, :], scale, jnp.zeros((WIN - 2 * PATCHES, WIN), F32)], axis=0).T
    total = jnp.zeros((WIN, HORIZONS), F32)
    for p in range(PATCHES):
        x = state[p * WIN : (p + 1) * WIN, :] if p < 6 else last[(p - 6) * WIN : (p - 5) * WIN, :]
        y = (x - table[:, p : p + 1]) * table[:, PATCHES + p : PATCHES + p + 1] * shard[25:26, :]
        total = total + lax.dot_general(
            y.astype(BF), heads[p], (((1,), (1,)), ((), ())), preferred_element_type=F32
        )
    scr[:, :HORIZONS] = total
    scr[:, HORIZONS:] = jnp.zeros((WIN, WIN - HORIZONS), F32)
    out[...] = scr[...].T[:HORIZONS]


def weigh_kernel(mine, theirs, info, counts, out):
    share = 1.0 / (1.0 + counts[...])
    here = lax.broadcasted_iota(jnp.int32, share.shape, 0) == lax.axis_index("member")
    own = jnp.sum(jnp.where(here, share, 0.0), axis=0, keepdims=True)
    factor = info[1:2, :] * own / jnp.sum(share, axis=0, keepdims=True)
    out[...] = (mine[...] + theirs[...]) * factor


def rank_kernel(levels, own, total, back, info, target, average, levels_out, scr, res, ranks):
    t = lax.axis_index("tensor")
    slot = lax.axis_index("member")
    per = total.shape[0] // 2
    pred = jnp.where(t % 2 == 1, total[per:, :], back[:per, :]) + info[0:1, :]
    wanted = target[pl.ds(pl.multiple_of(24 * t, 8), per), :]
    resid = jnp.abs(wanted - pred)
    scr[...] = jnp.zeros((WIN, WIN), F32)
    scr[:per, :] = pred
    scr[...] = scr[...].T
    if own % 8 == 0:
        average[...] = scr[pl.ds(pl.multiple_of(own * slot, 8), own), :per]
    else:
        at = own * slot
        rows = scr[pl.ds(pl.multiple_of((at // 8) * 8, 8), 8), :per]
        pick = rows[:own]
        for s in range(1, 8 // own):
            pick = jnp.where(at % 8 == s * own, rows[s * own : (s + 1) * own], pick)
        average[...] = pick
    res[...] = jnp.zeros((WIN, WIN), F32)
    res[:per, :] = resid
    across = res[...].T
    j = lax.broadcasted_iota(jnp.int32, (WIN, WIN), 0)
    i = lax.broadcasted_iota(jnp.int32, (WIN, WIN), 1)
    earlier = j < i
    for h in range(per):
        row, col = resid[h : h + 1, :], across[:, h : h + 1]
        before = (col < row) | ((col == row) & earlier)
        ranks[h : h + 1, :] = jnp.sum(before.astype(F32), axis=0, keepdims=True)
    order = ranks[...]
    lane = lax.broadcasted_iota(jnp.int32, (per, WIN), 1)
    table = jnp.zeros((per, WIN), F32)
    for n, level in enumerate(levels):
        value = jnp.sum(jnp.where(order == float(level), resid, 0.0), axis=1, keepdims=True)
        table = jnp.where(lane == n, value, table)
    res[:per, :] = table
    levels_out[...] = res[...].T[: len(levels), :per]


def per_device(series, starts, counts, lifting, location, gain_one, up, down, gain_two, readout):
    members = lax.axis_size("member")
    own = counts.shape[1]
    sds = jax.ShapeDtypeStruct

    def over_tensor(x, k):
        return lax.ppermute(x, "tensor", [(i, i ^ k) for i in range(4)])

    def over_chips(x, member_k, tensor_k):
        pairs = [(4 * m + t, 4 * (m ^ member_k) + (t ^ tensor_k)) for m in range(members) for t in (1, 3)]
        return lax.ppermute(x, ("member", "tensor"), pairs)

    def to_core(x, core):
        return lax.ppermute(x, "tensor", [(t ^ 1, t) for t in range(4) if t % 2 == core])

    shard_bf = pltpu.VMEM((D, SHARD), BF)
    packed, every, give_x = call(
        pack_kernel,
        (pltpu.VMEM((32, SHARD), F32), pltpu.VMEM((members, WIN), F32), shard_bf),
        [HBM] * 6,
        (lifting, location, gain_one, gain_two, counts.T, down),
        2 * US,
        1000,
        [
            pltpu.VMEM((1, SHARD), F32),
            pltpu.VMEM((1, SHARD), F32),
            pltpu.VMEM((own, members), jnp.int32),
            pltpu.VMEM((WIN, WIN), F32),
            pltpu.SemaphoreType.DMA((6,)),
        ],
    )
    shards = [packed] + [over_tensor(packed, k) for k in (1, 2, 3)]
    peer_x = over_tensor(give_x, 1)

    heads = jnp.swapaxes(readout[0], 1, 2)
    up = up[0]
    own_x, own_y, give_y, heads_v, q, info, target, half = call(
        windows_kernel,
        (
            shard_bf,
            shard_bf,
            shard_bf,
            pltpu.VMEM((PATCHES, HORIZONS, SHARD), BF),
            pltpu.VMEM((PATCHES, WIN, KCAT), BF),
            pltpu.VMEM((8, WIN), F32),
            pltpu.VMEM((WIN, WIN), F32),
            pltpu.VMEM((32, HIDDEN), F32),
        ),
        [HBM] * 4 + [V] * 3,
        (series.reshape(WIN, WIN), starts.reshape(1, WIN), down, heads, up, packed, shards[1]),
        5 * US,
        1000,
        [
            pltpu.VMEM((WIN, WIN), F32),
            pltpu.VMEM((1, WIN), jnp.int32),
            pltpu.VMEM((2, 96, SHARD), BF),
            pltpu.SemaphoreType.DMA((6,)),
        ],
    )

    hops = [k for k in (1, 3, 8, 24) if k < members]

    def counts_hop(value, after, masks):
        value = lax.optimization_barrier((value, after))[0]
        return value, [over_chips(value, k, 0) if k < members else jnp.zeros_like(value) for k in masks]

    m24, ecat = call(
        lift_kernel,
        (pltpu.VMEM((32, HIDDEN), F32), pltpu.VMEM((4, KCAT, SHARD), BF)),
        [V] * 6,
        (up, *shards, half),
        3 * US,
        1000,
        [pltpu.VMEM((2, 96, SHARD), BF)],
    )
    m24_peer = over_tensor(m24, 1)
    mcat_shape = pltpu.VMEM((KCAT, HIDDEN), BF)
    rstd, m_own = call(
        scale_kernel,
        (pltpu.VMEM((PATCHES, WIN, 128), F32), mcat_shape),
        [V] * 3,
        (q, ecat, m24),
        2 * US,
        1000,
    )
    sums = (pltpu.VMEM((2 * WIN, 2 * HIDDEN), BF), pltpu.VMEM((2 * WIN, SHARD), BF))
    m_peer, act, send = call(
        first_away_kernel,
        (mcat_shape,) + sums,
        [V] * 6,
        (q, rstd, m_own, m24_peer, own_x, peer_x),
        4 * US,
        1000,
    )
    acts, crossed = [act], [over_tensor(send, 2)]
    fed = (q, rstd, m_own, m_peer, own_x, peer_x)
    peer_y = over_tensor(lax.optimization_barrier((give_y, send))[0], 1)
    for g in range(1, 4):
        act, send = call(
            functools.partial(away_kernel, g),
            sums,
            [V] * 6,
            fed,
            4 * US,
            1000,
            after=(every, crossed[g - 2]) if g > 1 else (),
        )
        acts.append(act)
        crossed.append(over_tensor(send, 2))
        if g == 1:
            every, got = counts_hop(every, send, (1, 2, 3))
            every = every + got[0] + got[1] + got[2]
        if g == 2:
            every, got = counts_hop(every, send, (8,))
            every = every + got[0]
    every, (late,) = counts_hop(every, send, (24,))
    homes = (q, ecat, own_y, peer_y)
    (part,) = call(
        home_kernel,
        (pltpu.VMEM((4 * WIN, SHARD), F32),),
        [V] * 6,
        (*homes, *acts[:2]),
        US // 10,
        1000,
        after=(send,),
    )
    state, last, stats, every = call(
        state_kernel,
        (
            pltpu.VMEM((6 * WIN, SHARD), F32),
            pltpu.VMEM((2 * WIN, SHARD), F32),
            pltpu.VMEM((2 * PATCHES, WIN), F32),
            pltpu.VMEM((members, WIN), F32),
        ),
        [V] * 12,
        (*homes, *acts[2:], part, *crossed[:3], every, late),
        5 * US,
        1000,
    )
    every, got = counts_hop(every, stats, (4,))
    every = every + got[0]
    last, stats = call(
        last_state_kernel,
        (pltpu.VMEM((2 * WIN, SHARD), F32), pltpu.VMEM((2 * PATCHES, WIN), F32)),
        [V] * 3,
        (last, crossed[3], stats),
        US,
        1000,
        after=(every,),
    )
    features = SHARD
    for k in (1, 2):
        other = over_tensor(stats, k)
        gap = stats[:PATCHES] - other[:PATCHES]
        square = stats[PATCHES:] + other[PATCHES:] + (0.5 * features) * (gap * gap)
        stats = jnp.concatenate([0.5 * (stats[:PATCHES] + other[:PATCHES]), square], axis=0)
        features *= 2
    (total,) = call(
        head_kernel,
        (pltpu.VMEM((HORIZONS, WIN), F32),),
        [V] * 5,
        (stats, state, last, heads_v, packed),
        US,
        1000,
        [pltpu.VMEM((WIN, WIN), F32)],
    )
    total = total + to_core(total, 1)
    (total,) = call(
        weigh_kernel,
        (pltpu.VMEM((HORIZONS, WIN), F32),),
        [V] * 4,
        (total, over_chips(total, 0, 2), info, every),
        US,
        1000,
    )
    if members > 4:
        total = total + over_chips(total, 4, 2)
    total = lax.dynamic_slice_in_dim(total, 48 * (lax.axis_index("tensor") >> 1), 48, 0)
    for k in hops:
        total = total + over_chips(total, k, 0)
    back = to_core(total, 0)

    levels = tuple(WIN * n // 100 for n in (50, 80, 90, 95))
    return call(
        functools.partial(rank_kernel, levels, own),
        (sds((own, 24), F32), sds((4, 24), F32)),
        [V] * 4,
        (total, back, info, target),
        US,
        1000,
        [pltpu.VMEM((WIN, WIN), F32), pltpu.VMEM((WIN, WIN), F32), pltpu.VMEM((24, WIN), F32)],
    )


def solution(mesh):
    placed = (
        P(),
        P(),
        P(None, "member"),
        P("member", None, "tensor"),
        P("member", None, "tensor"),
        P("member", "tensor"),
        P("member", None, "tensor"),
        P("member", "tensor", None),
        P("member", "tensor"),
        P("member", None, "tensor", None),
    )
    return jax.shard_map(
        per_device,
        mesh=mesh,
        in_specs=placed,
        out_specs=(P("member", "tensor"), P(None, "tensor")),
        check_vma=False,
    )
```

```python
import functools
import math

import jax
import jax.numpy as jnp
from jax import lax
from jax.experimental import pallas as pl
from jax.experimental.pallas import tpu as pltpu
from jax.sharding import PartitionSpec as P

BF, F32 = jnp.bfloat16, jnp.float32
PATCHES, PLEN, STRIDE, LOOK = 8, 16, 8, 72
WIN, D, SHARD, HIDDEN, HORIZONS = 128, 2048, 512, 2048, 96
KCAT = 256
MIB = 1 << 20
US = 10**9


def split3(x):
    a = x.astype(BF)
    rest = x - a.astype(F32)
    b = rest.astype(BF)
    c = (rest - b.astype(F32)).astype(BF)
    return a, b, c


def dot(a, b):
    return jnp.dot(a, b, preferred_element_type=F32)


def roll_left(x, by):
    lanes = x.shape[1]
    by = by % lanes
    return x if by == 0 else pltpu.roll(x, lanes - by, 1)


def shard_cols(t):
    return pl.ds(pl.multiple_of(SHARD * t, SHARD), SHARD)


def call(body, out_shape, in_specs, args, flops, nbytes, scratch=(), limit=24 * MIB, after=()):
    taken, held = len(in_specs), len(after)

    def run(*refs):
        body(*refs[:taken], *refs[taken + held :])

    args = tuple(
        pltpu.with_memory_space_constraint(x, pltpu.HBM if spec is HBM else pltpu.VMEM)
        for x, spec in zip(args, in_specs)
    ) + tuple(after)
    in_specs = list(in_specs) + [ANY] * held
    return pl.pallas_call(
        run,
        out_shape=out_shape,
        in_specs=in_specs,
        out_specs=jax.tree.map(lambda _: pl.BlockSpec(memory_space=pltpu.VMEM), out_shape),
        scratch_shapes=list(scratch),
        compiler_params=pltpu.CompilerParams(vmem_limit_bytes=limit),
        cost_estimate=pl.CostEstimate(flops=flops, bytes_accessed=nbytes, transcendentals=0),
    )(*args)


V = pl.BlockSpec(memory_space=pltpu.VMEM)
ANY = pl.BlockSpec(memory_space=pl.ANY)
HBM = pl.BlockSpec(memory_space=pltpu.HBM)


def pack_kernel(lifting, location, gain_one, gain_two, counts_h, down, packed, every, give, g1, g2, counts, scr, sem):
    t = lax.axis_index("tensor")
    loads = [
        pltpu.make_async_copy(lifting.at[0], packed.at[0:PLEN, :], sem.at[0]),
        pltpu.make_async_copy(location.at[0], packed.at[PLEN : PLEN + PATCHES, :], sem.at[1]),
        pltpu.make_async_copy(gain_one, g1, sem.at[2]),
        pltpu.make_async_copy(gain_two, g2, sem.at[3]),
        pltpu.make_async_copy(counts_h, counts, sem.at[4]),
        pltpu.make_async_copy(down.at[0, :, shard_cols(t ^ 3)], give, sem.at[5]),
    ]
    for load in loads:
        load.start()
    own, members = counts.shape
    scr[...] = jnp.zeros((WIN, WIN), F32)
    for load in loads[:5]:
        load.wait()
    row = lax.broadcasted_iota(jnp.int32, (8, SHARD), 0)
    packed[PLEN + PATCHES :, :] = jnp.where(row == 0, g1[...], jnp.where(row == 1, g2[...], 0.0))
    scr[:own, :members] = counts[...].astype(F32)
    columns = scr[...].T[:members]
    at = own * lax.axis_index("member")
    place = lax.broadcasted_iota(jnp.int32, (members, WIN), 1) - at
    placed = jnp.zeros((members, WIN), F32)
    for j in range(own):
        placed = jnp.where(place == j, columns[:, j : j + 1], placed)
    every[...] = placed
    loads[5].wait()


def lift_parts(t, shards, up, lhs):
    for n, (k, shard) in enumerate(shards):
        gain = shard[PLEN + PATCHES : PLEN + PATCHES + 1, :]
        row = lax.broadcasted_iota(jnp.int32, (32, SHARD), 0)
        rows = jnp.where(row < PLEN + PATCHES, shard[...] * gain, jnp.where(row == PLEN + PATCHES, gain, 0.0))
        for i, part in enumerate(split3(rows)):
            lhs[n, 32 * i : 32 * i + 32, :] = part
    for j in range(HIDDEN // 512):
        cols = slice(512 * j, 512 * j + 512)
        m = sum(dot(lhs[n], up[shard_cols(t ^ k), cols]) for n, (k, _) in enumerate(shards))
        yield cols, m[:32] + m[32:64] + m[64:96]


def windows_kernel(series_h, starts_h, down, give_y, q, info, target, series, starts, sem):
    t = lax.axis_index("tensor")
    small = [
        pltpu.make_async_copy(series_h, series, sem.at[0]),
        pltpu.make_async_copy(starts_h, starts, sem.at[1]),
    ]
    loads = [pltpu.make_async_copy(down.at[0, :, shard_cols(t ^ 1)], give_y, sem.at[2])]
    for load in small + loads:
        load.start()
    for load in small:
        load.wait()
    lane = lax.broadcasted_iota(jnp.int32, (WIN, WIN), 1)
    first = jnp.broadcast_to(starts[...].astype(F32), (WIN, WIN)).T.astype(jnp.int32)
    row, offset = first >> 7, first & 127
    picks = [(row + k == lane).astype(F32).astype(BF) for k in range(3)]
    parts = split3(series[...])
    rows = [sum(dot(pick, part) for part in parts) for pick in picks]
    x = jnp.concatenate(rows, axis=1)
    offset = jnp.concatenate([offset] * 3, axis=1)
    for bit in range(7):
        x = jnp.where((offset >> bit) & 1 == 1, roll_left(x, 1 << bit), x)
    target[...] = roll_left(x, LOOK)[:, :WIN].T
    look = x[:, :WIN]
    center = jnp.sum(jnp.where(lane < LOOK, look, 0.0), axis=1, keepdims=True) * (1.0 / LOOK)
    dev = jnp.where(lane < LOOK, look - center, 0.0)
    spread = jnp.sqrt(jnp.sum(dev * dev, axis=1, keepdims=True) * (1.0 / LOOK) + 1e-05)
    normed = dev / spread
    pair = jnp.where(lane == 0, center, jnp.where(lane == 1, spread, 0.0)).T
    info[...] = pair[:8]
    block = lane // 32
    for p in range(PATCHES):
        one = jnp.where(lane < PLEN, roll_left(normed, STRIDE * p), 0.0)
        one = jnp.where(lane == PLEN + p, 1.0, one)
        two = one + pltpu.roll(one, 32, 1)
        four = two + pltpu.roll(two, 64, 1)
        a, b, c = (v.astype(F32) for v in split3(four))
        q[p, :, :WIN] = jnp.where(block < 2, a, b).astype(BF)
        q[p, :, WIN:] = jnp.where(block == 0, a, jnp.where(block == 1, c, 0.0)).astype(BF)
    for load in loads:
        load.wait()


def cat_rows(x):
    b1, b2, b3 = split3(x)
    zero = jnp.zeros_like(b1)
    return [b1, b2, b1, b2, b3, b1, zero, zero]


def lift_kernel(up, s0, s1, s2, s3, mine, late, m24, ecat, every, lhs):
    t = lax.axis_index("tensor")
    every[...] = mine[...] + late[...]
    shards = (s0, s1, s2, s3)
    mean = sum(jnp.sum(s[...], axis=1, keepdims=True) for s in shards) * (1.0 / D)
    keep = lax.broadcasted_iota(jnp.int32, (32, SHARD), 0) < PLEN + PATCHES
    for cols, m in lift_parts(t, tuple(enumerate(shards)), up, lhs):
        m24[:, cols] = m - mean * m[PLEN + PATCHES : PLEN + PATCHES + 1, :]
    for k, shard in enumerate(shards):
        centred = jnp.where(keep, shard[...] - mean, 0.0)
        for i, part in enumerate(cat_rows(centred)):
            ecat[k, 32 * i : 32 * i + 32, :] = part


def spread_rows(m24, mcat):
    for j in range(HIDDEN // 512):
        cols = slice(512 * j, 512 * j + 512)
        row = lax.broadcasted_iota(jnp.int32, (32, 512), 0)
        for i, part in enumerate(cat_rows(jnp.where(row < PLEN + PATCHES, m24[:, cols], 0.0))):
            mcat[32 * i : 32 * i + 32, cols] = part


def scale_kernel(q, ecat, m24, rstd, mcat):
    spread_rows(m24, mcat)
    for p in range(0, PATCHES, 2):
        square = jnp.zeros((2 * WIN, 128), F32)
        for k in range(4):
            dev = dot(q[p : p + 2].reshape(2 * WIN, KCAT), ecat[k])
            for c in range(SHARD // 128):
                piece = dev[:, 128 * c : 128 * c + 128]
                square = square + piece * piece
        var = jnp.sum(square, axis=1, keepdims=True) * (1.0 / D)
        rstd[p : p + 2] = jnp.broadcast_to(lax.rsqrt(var + 1e-05), (2 * WIN, 128)).reshape(2, WIN, 128)


def gelu(h):
    c = math.sqrt(2.0 / math.pi)
    half = 0.5 * h
    return half + half * jnp.tanh(h * (c + (c * 0.044715) * (h * h)))


def away_body(g, q, rstd, mcats, downs, act, send):
    rows = q[2 * g : 2 * g + 2].reshape(2 * WIN, KCAT)
    scale = rstd[2 * g : 2 * g + 2].reshape(2 * WIN, 128)[:, :1]
    total = jnp.zeros((2 * WIN, SHARD), F32)
    downs = (downs[0][:, shard_cols(lax.axis_index("tensor") ^ 2)], downs[1][...])
    for side in range(2):
        for j in range(HIDDEN // 512):
            cols = slice(512 * j, 512 * j + 512)
            at = slice(HIDDEN * side + 512 * j, HIDDEN * side + 512 * (j + 1))
            act[:, at] = gelu(dot(rows, mcats[side][:, cols]) * scale).astype(BF)
    for side in range(2):
        total = total + dot(act[:, HIDDEN * side : HIDDEN * (side + 1)], downs[side])
    send[...] = total.astype(BF)


def first_away_kernel(q, rstd, m_own, m24_peer, down, d_peer, m_peer, act, send):
    spread_rows(m24_peer, m_peer)
    away_body(0, q, rstd, (m_own, m_peer), (down, d_peer), act, send)


def away_kernel(g, q, rstd, m_own, m_peer, down, d_peer, act, send):
    away_body(g, q, rstd, (m_own, m_peer), (down, d_peer), act, send)


def add_stats(table, p, x):
    lane = lax.broadcasted_iota(jnp.int32, (WIN, WIN), 1)
    mean = jnp.sum(x, axis=1, keepdims=True) * (1.0 / SHARD)
    off = x - mean
    square = jnp.sum(off * off, axis=1, keepdims=True)
    return jnp.where(lane == p, mean, jnp.where(lane == PATCHES + p, square, table))


def home_rows(g, q, ecat, down, d_peer, act):
    own = down[:, shard_cols(lax.axis_index("tensor"))]
    x = dot(act[:, :HIDDEN], own) + dot(act[:, HIDDEN:], d_peer[...])
    return x + dot(q[2 * g : 2 * g + 2].reshape(2 * WIN, KCAT), ecat[0])


def home_kernel(q, ecat, d_own, d_peer, a0, a1, part):
    for g, act in enumerate((a0, a1)):
        part[2 * WIN * g : 2 * WIN * (g + 1), :] = home_rows(g, q, ecat, d_own, d_peer, act)


def state_kernel(q, ecat, d_own, d_peer, a2, a3, part, c0, c1, c2, mine, late, state, last, stats, every):
    every[...] = mine[...] + late[...]
    last[...] = home_rows(3, q, ecat, d_own, d_peer, a3)
    table = jnp.zeros((WIN, WIN), F32)
    for g, cross in enumerate((c0, c1, c2)):
        rows = slice(2 * WIN * g, 2 * WIN * (g + 1))
        x = part[rows, :] if g < 2 else home_rows(2, q, ecat, d_own, d_peer, a2)
        x = x + cross[...].astype(F32)
        state[rows, :] = x
        table = add_stats(table, 2 * g, x[:WIN])
        table = add_stats(table, 2 * g + 1, x[WIN:])
    stats[...] = table.T[: 2 * PATCHES]


def last_state_kernel(last, cross, prev, state, stats):
    x = last[...] + cross[...].astype(F32)
    state[...] = x
    table = add_stats(jnp.zeros((WIN, WIN), F32), 6, x[:WIN])
    table = add_stats(table, 7, x[WIN:])
    stats[...] = prev[...] + table.T[: 2 * PATCHES]


def head_kernel(stats, state, last, heads, shard, info, counts, send, keep, scr):
    core = lax.axis_index("tensor") & 1
    slot = lax.axis_index("member")
    scale = lax.rsqrt(stats[PATCHES:, :] * (1.0 / D) + 1e-05)
    table = jnp.concatenate([stats[:PATCHES, :], scale, jnp.zeros((WIN - 2 * PATCHES, WIN), F32)], axis=0).T
    total = jnp.zeros((WIN, HORIZONS), F32)
    for p in range(PATCHES):
        x = state[p * WIN : (p + 1) * WIN, :] if p < 6 else last[(p - 6) * WIN : (p - 5) * WIN, :]
        y = (x - table[:, p : p + 1]) * table[:, PATCHES + p : PATCHES + p + 1] * shard[25:26, :]
        total = total + lax.dot_general(
            y.astype(BF), heads[p], (((1,), (1,)), ((), ())), preferred_element_type=F32
        )
    share = 1.0 / (1.0 + counts[...])
    members = share.shape[0]
    here = lax.broadcasted_iota(jnp.int32, (members, WIN), 0) == slot
    mine_share = jnp.sum(jnp.where(here, share, 0.0), axis=0, keepdims=True)
    factor = info[1:2, :] * mine_share / jnp.sum(share, axis=0, keepdims=True)
    scr[:, :HORIZONS] = total
    scr[:, HORIZONS:] = jnp.zeros((WIN, WIN - HORIZONS), F32)
    scr[...] = scr[...].T * factor
    for c in range(2):
        for out, side in ((keep, core), (send, 1 - core)):
            out[24 * c : 24 * c + 24, :] = scr[pl.ds(pl.multiple_of(48 * c + 24 * side, 8), 24), :]


def rank_kernel(levels, own, total, info, target, average, levels_out, scr, res, ranks):
    t = lax.axis_index("tensor")
    slot = lax.axis_index("member")
    per = total.shape[0]
    pred = total[...] + info[0:1, :]
    wanted = target[pl.ds(pl.multiple_of(24 * t, 8), per), :]
    resid = jnp.abs(wanted - pred)
    scr[...] = jnp.zeros((WIN, WIN), F32)
    scr[:per, :] = pred
    scr[...] = scr[...].T
    if own % 8 == 0:
        average[...] = scr[pl.ds(pl.multiple_of(own * slot, 8), own), :per]
    else:
        at = own * slot
        rows = scr[pl.ds(pl.multiple_of((at // 8) * 8, 8), 8), :per]
        pick = rows[:own]
        for s in range(1, 8 // own):
            pick = jnp.where(at % 8 == s * own, rows[s * own : (s + 1) * own], pick)
        average[...] = pick
    res[...] = jnp.zeros((WIN, WIN), F32)
    res[:per, :] = resid
    across = res[...].T
    j = lax.broadcasted_iota(jnp.int32, (WIN, WIN), 0)
    i = lax.broadcasted_iota(jnp.int32, (WIN, WIN), 1)
    earlier = j < i
    for h in range(per):
        row, col = resid[h : h + 1, :], across[:, h : h + 1]
        before = (col < row) | ((col == row) & earlier)
        ranks[h : h + 1, :] = jnp.sum(before.astype(F32), axis=0, keepdims=True)
    order = ranks[...]
    lane = lax.broadcasted_iota(jnp.int32, (per, WIN), 1)
    table = jnp.zeros((per, WIN), F32)
    for n, level in enumerate(levels):
        value = jnp.sum(jnp.where(order == float(level), resid, 0.0), axis=1, keepdims=True)
        table = jnp.where(lane == n, value, table)
    res[:per, :] = table
    levels_out[...] = res[...].T[: len(levels), :per]


def per_device(series, starts, counts, lifting, location, gain_one, up, down, gain_two, readout):
    members = lax.axis_size("member")
    own = counts.shape[1]
    sds = jax.ShapeDtypeStruct

    def over_tensor(x, k):
        return lax.ppermute(x, "tensor", [(i, i ^ k) for i in range(4)])

    def over_member(x, k):
        return lax.ppermute(x, "member", [(i, i ^ k) for i in range(members)])

    shard_bf = pltpu.VMEM((D, SHARD), BF)
    packed, every, give_x = call(
        pack_kernel,
        (pltpu.VMEM((32, SHARD), F32), pltpu.VMEM((members, WIN), F32), shard_bf),
        [HBM] * 6,
        (lifting, location, gain_one, gain_two, counts.T, down),
        2 * US,
        1000,
        [
            pltpu.VMEM((1, SHARD), F32),
            pltpu.VMEM((1, SHARD), F32),
            pltpu.VMEM((own, members), jnp.int32),
            pltpu.VMEM((WIN, WIN), F32),
            pltpu.SemaphoreType.DMA((6,)),
        ],
    )
    shards = [packed] + [over_tensor(packed, k) for k in (1, 2, 3)]
    peer_x = over_tensor(give_x, 1)

    heads = jnp.swapaxes(readout[0], 1, 2)
    up = up[0]
    give_y, q, info, target = call(
        windows_kernel,
        (
            shard_bf,
            pltpu.VMEM((PATCHES, WIN, KCAT), BF),
            pltpu.VMEM((8, WIN), F32),
            pltpu.VMEM((WIN, WIN), F32),
        ),
        [HBM] * 3,
        (series.reshape(WIN, WIN), starts.reshape(1, WIN), down),
        5 * US,
        1000,
        [pltpu.VMEM((WIN, WIN), F32), pltpu.VMEM((1, WIN), jnp.int32), pltpu.SemaphoreType.DMA((3,))],
        after=(packed,),
    )

    hops = [k for k in (1, 3, 8, 24) if k < members]
    steps = iter(hops + [4] * (members > 4))

    def hop(value, after=None):
        k = next(steps, None)
        if after is not None:
            value = lax.optimization_barrier((value, after))[0]
        return value if k is None else value + over_member(value, k)

    def hop_parts(value, after=None):
        k = next(steps, None)
        if after is not None:
            value = lax.optimization_barrier((value, after))[0]
        return value, jnp.zeros_like(value) if k is None else over_member(value, k)

    every, late = hop_parts(every)
    m24, ecat, every = call(
        lift_kernel,
        (pltpu.VMEM((32, HIDDEN), F32), pltpu.VMEM((4, KCAT, SHARD), BF), pltpu.VMEM((members, WIN), F32)),
        [V] * 7,
        (up, *shards, every, late),
        3 * US,
        1000,
        [pltpu.VMEM((4, 96, SHARD), BF)],
        after=(info,),
    )
    m24_peer = over_tensor(m24, 1)
    mcat_shape = pltpu.VMEM((KCAT, HIDDEN), BF)
    rstd, m_own = call(
        scale_kernel,
        (pltpu.VMEM((PATCHES, WIN, 128), F32), mcat_shape),
        [V] * 3,
        (q, ecat, m24),
        2 * US,
        1000,
    )
    sums = (pltpu.VMEM((2 * WIN, 2 * HIDDEN), BF), pltpu.VMEM((2 * WIN, SHARD), BF))
    m_peer, act, send = call(
        first_away_kernel,
        (mcat_shape,) + sums,
        [V] * 6,
        (q, rstd, m_own, m24_peer, down[0], peer_x),
        4 * US,
        1000,
    )
    acts, crossed = [act], [over_tensor(send, 2)]
    fed = (q, rstd, m_own, m_peer, down[0], peer_x)
    peer_y = over_tensor(lax.optimization_barrier((give_y, send))[0], 1)
    for g in range(1, 4):
        act, send = call(
            functools.partial(away_kernel, g),
            sums,
            [V] * 6,
            fed,
            4 * US,
            1000,
            after=(every, crossed[g - 2]) if g > 1 else (),
        )
        acts.append(act)
        crossed.append(over_tensor(send, 2))
        if g < 3:
            every = hop(every, send)
    every, late = hop_parts(every, send)
    homes = (q, ecat, down[0], peer_y)
    (part,) = call(
        home_kernel,
        (pltpu.VMEM((4 * WIN, SHARD), F32),),
        [V] * 6,
        (*homes, *acts[:2]),
        US // 10,
        1000,
        after=(send,),
    )
    state, last, stats, every = call(
        state_kernel,
        (
            pltpu.VMEM((6 * WIN, SHARD), F32),
            pltpu.VMEM((2 * WIN, SHARD), F32),
            pltpu.VMEM((2 * PATCHES, WIN), F32),
            pltpu.VMEM((members, WIN), F32),
        ),
        [V] * 12,
        (*homes, *acts[2:], part, *crossed[:3], every, late),
        5 * US,
        1000,
    )
    last, stats = call(
        last_state_kernel,
        (pltpu.VMEM((2 * WIN, SHARD), F32), pltpu.VMEM((2 * PATCHES, WIN), F32)),
        [V] * 3,
        (last, crossed[3], stats),
        US,
        1000,
    )
    features = SHARD
    for k in (1, 2):
        other = over_tensor(stats, k)
        gap = stats[:PATCHES] - other[:PATCHES]
        square = stats[PATCHES:] + other[PATCHES:] + (0.5 * features) * (gap * gap)
        stats = jnp.concatenate([0.5 * (stats[:PATCHES] + other[:PATCHES]), square], axis=0)
        features *= 2
        if k == 1:
            every = hop(every, stats)
    sent, held = call(
        head_kernel,
        (pltpu.VMEM((48, WIN), F32),) * 2,
        [V] * 7,
        (stats, state, last, heads, packed, info, every),
        US,
        1000,
        [pltpu.VMEM((WIN, WIN), F32)],
    )
    total = held + over_tensor(sent, 1)
    total = total + over_tensor(total, 2)
    if members > 4:
        pairs = [(4 * m + t, 4 * (m ^ 4) + (t ^ 2)) for m in range(members) for t in range(4)]
        total = total + lax.ppermute(total, ("member", "tensor"), pairs)
    total = lax.dynamic_slice_in_dim(total, 24 * ((lax.axis_index("tensor") >> 1)), 24, 0)
    for ring in ((1, 2, 3), (8, 16, 24)):
        if ring[-1] < members:
            got = [over_member(total, k) for k in ring]
            total = total + got[0] + got[1] + got[2]

    levels = tuple(WIN * n // 100 for n in (50, 80, 90, 95))
    return call(
        functools.partial(rank_kernel, levels, own),
        (sds((own, 24), F32), sds((4, 24), F32)),
        [V] * 3,
        (total, info, target),
        US,
        1000,
        [pltpu.VMEM((WIN, WIN), F32), pltpu.VMEM((WIN, WIN), F32), pltpu.VMEM((24, WIN), F32)],
    )


def solution(mesh):
    placed = (
        P(),
        P(),
        P(None, "member"),
        P("member", None, "tensor"),
        P("member", None, "tensor"),
        P("member", "tensor"),
        P("member", None, "tensor"),
        P("member", "tensor", None),
        P("member", "tensor"),
        P("member", None, "tensor", None),
    )
    return jax.shard_map(
        per_device,
        mesh=mesh,
        in_specs=placed,
        out_specs=(P("member", "tensor"), P(None, "tensor")),
        check_vma=False,
    )
```

```python
import functools
import math

import jax
import jax.numpy as jnp
from jax import lax
from jax.experimental import pallas as pl
from jax.experimental.pallas import tpu as pltpu
from jax.sharding import PartitionSpec as P

BF, F32 = jnp.bfloat16, jnp.float32
PATCHES, PLEN, STRIDE, LOOK = 8, 16, 8, 72
WIN, D, SHARD, HIDDEN, HORIZONS = 128, 2048, 512, 2048, 96
KCAT = 256
MIB = 1 << 20
US = 10**9
GROUPS = ((0, 2), (2, 4), (4, 6), (6, 8))


def split3(x):
    a = x.astype(BF)
    rest = x - a.astype(F32)
    b = rest.astype(BF)
    c = (rest - b.astype(F32)).astype(BF)
    return a, b, c


def dot(a, b):
    return jnp.dot(a, b, preferred_element_type=F32)


def roll_left(x, by):
    lanes = x.shape[1]
    by = by % lanes
    return x if by == 0 else pltpu.roll(x, lanes - by, 1)


def shard_cols(t):
    return pl.ds(pl.multiple_of(SHARD * t, SHARD), SHARD)


def call(body, out_shape, in_specs, args, flops, nbytes, scratch=(), limit=24 * MIB, after=()):
    taken, held = len(in_specs), len(after)

    def run(*refs):
        body(*refs[:taken], *refs[taken + held :])

    args = tuple(
        pltpu.with_memory_space_constraint(x, pltpu.HBM if spec is HBM else pltpu.VMEM)
        for x, spec in zip(args, in_specs)
    ) + tuple(after)
    in_specs = list(in_specs) + [ANY] * held
    return pl.pallas_call(
        run,
        out_shape=out_shape,
        in_specs=in_specs,
        out_specs=jax.tree.map(lambda _: pl.BlockSpec(memory_space=pltpu.VMEM), out_shape),
        scratch_shapes=list(scratch),
        compiler_params=pltpu.CompilerParams(vmem_limit_bytes=limit),
        cost_estimate=pl.CostEstimate(flops=flops, bytes_accessed=nbytes, transcendentals=0),
    )(*args)


V = pl.BlockSpec(memory_space=pltpu.VMEM)
ANY = pl.BlockSpec(memory_space=pl.ANY)
HBM = pl.BlockSpec(memory_space=pltpu.HBM)


def pack_kernel(lifting, location, gain_one, gain_two, counts_h, down, packed, every, give, g1, g2, counts, scr, sem):
    t = lax.axis_index("tensor")
    loads = [
        pltpu.make_async_copy(lifting.at[0], packed.at[0:PLEN, :], sem.at[0]),
        pltpu.make_async_copy(location.at[0], packed.at[PLEN : PLEN + PATCHES, :], sem.at[1]),
        pltpu.make_async_copy(gain_one, g1, sem.at[2]),
        pltpu.make_async_copy(gain_two, g2, sem.at[3]),
        pltpu.make_async_copy(counts_h, counts, sem.at[4]),
        pltpu.make_async_copy(down.at[0, :, shard_cols(t ^ 3)], give, sem.at[5]),
    ]
    for load in loads:
        load.start()
    own, members = counts.shape
    scr[...] = jnp.zeros((WIN, WIN), F32)
    for load in loads[:5]:
        load.wait()
    row = lax.broadcasted_iota(jnp.int32, (8, SHARD), 0)
    packed[PLEN + PATCHES :, :] = jnp.where(row == 0, g1[...], jnp.where(row == 1, g2[...], 0.0))
    scr[:own, :members] = counts[...].astype(F32)
    columns = scr[...].T[:members]
    at = own * lax.axis_index("member")
    place = lax.broadcasted_iota(jnp.int32, (members, WIN), 1) - at
    placed = jnp.zeros((members, WIN), F32)
    for j in range(own):
        placed = jnp.where(place == j, columns[:, j : j + 1], placed)
    every[...] = placed
    loads[5].wait()


def lift_parts(t, shards, up, lhs):
    for n, (k, shard) in enumerate(shards):
        gain = shard[PLEN + PATCHES : PLEN + PATCHES + 1, :]
        row = lax.broadcasted_iota(jnp.int32, (32, SHARD), 0)
        rows = jnp.where(row < PLEN + PATCHES, shard[...] * gain, jnp.where(row == PLEN + PATCHES, gain, 0.0))
        for i, part in enumerate(split3(rows)):
            lhs[n, 32 * i : 32 * i + 32, :] = part
    for j in range(HIDDEN // 512):
        cols = slice(512 * j, 512 * j + 512)
        m = sum(dot(lhs[n], up[shard_cols(t ^ k), cols]) for n, (k, _) in enumerate(shards))
        yield cols, m[:32] + m[32:64] + m[64:96]


def windows_kernel(series_h, starts_h, down, give_y, q, info, target, series, starts, sem):
    t = lax.axis_index("tensor")
    small = [
        pltpu.make_async_copy(series_h, series, sem.at[0]),
        pltpu.make_async_copy(starts_h, starts, sem.at[1]),
    ]
    loads = [pltpu.make_async_copy(down.at[0, :, shard_cols(t ^ 1)], give_y, sem.at[2])]
    for load in small + loads:
        load.start()
    for load in small:
        load.wait()
    lane = lax.broadcasted_iota(jnp.int32, (WIN, WIN), 1)
    first = jnp.broadcast_to(starts[...].astype(F32), (WIN, WIN)).T.astype(jnp.int32)
    row, offset = first >> 7, first & 127
    picks = [(row + k == lane).astype(F32).astype(BF) for k in range(3)]
    parts = split3(series[...])
    rows = [sum(dot(pick, part) for part in parts) for pick in picks]
    x = jnp.concatenate(rows, axis=1)
    offset = jnp.concatenate([offset] * 3, axis=1)
    for bit in range(7):
        x = jnp.where((offset >> bit) & 1 == 1, roll_left(x, 1 << bit), x)
    target[...] = roll_left(x, LOOK)[:, :WIN].T
    look = x[:, :WIN]
    center = jnp.sum(jnp.where(lane < LOOK, look, 0.0), axis=1, keepdims=True) * (1.0 / LOOK)
    dev = jnp.where(lane < LOOK, look - center, 0.0)
    spread = jnp.sqrt(jnp.sum(dev * dev, axis=1, keepdims=True) * (1.0 / LOOK) + 1e-05)
    normed = dev / spread
    pair = jnp.where(lane == 0, center, jnp.where(lane == 1, spread, 0.0)).T
    info[...] = pair[:8]
    block = lane // 32
    for p in range(PATCHES):
        one = jnp.where(lane < PLEN, roll_left(normed, STRIDE * p), 0.0)
        one = jnp.where(lane == PLEN + p, 1.0, one)
        two = one + pltpu.roll(one, 32, 1)
        four = two + pltpu.roll(two, 64, 1)
        a, b, c = (v.astype(F32) for v in split3(four))
        q[p, :, :WIN] = jnp.where(block < 2, a, b).astype(BF)
        q[p, :, WIN:] = jnp.where(block == 0, a, jnp.where(block == 1, c, 0.0)).astype(BF)
    for load in loads:
        load.wait()


def cat_rows(x):
    b1, b2, b3 = split3(x)
    zero = jnp.zeros_like(b1)
    return [b1, b2, b1, b2, b3, b1, zero, zero]


def lift_kernel(up, s0, s1, s2, s3, mine, late, m24, ecat, every, lhs):
    t = lax.axis_index("tensor")
    every[...] = mine[...] + late[...]
    shards = (s0, s1, s2, s3)
    mean = sum(jnp.sum(s[...], axis=1, keepdims=True) for s in shards) * (1.0 / D)
    keep = lax.broadcasted_iota(jnp.int32, (32, SHARD), 0) < PLEN + PATCHES
    for cols, m in lift_parts(t, tuple(enumerate(shards)), up, lhs):
        m24[:, cols] = m - mean * m[PLEN + PATCHES : PLEN + PATCHES + 1, :]
    for k, shard in enumerate(shards):
        centred = jnp.where(keep, shard[...] - mean, 0.0)
        for i, part in enumerate(cat_rows(centred)):
            ecat[k, 32 * i : 32 * i + 32, :] = part


def spread_rows(m24, mcat):
    for j in range(HIDDEN // 512):
        cols = slice(512 * j, 512 * j + 512)
        row = lax.broadcasted_iota(jnp.int32, (32, 512), 0)
        for i, part in enumerate(cat_rows(jnp.where(row < PLEN + PATCHES, m24[:, cols], 0.0))):
            mcat[32 * i : 32 * i + 32, cols] = part


def scale_kernel(q, ecat, m24, rstd, mcat):
    spread_rows(m24, mcat)
    for p in range(0, PATCHES, 2):
        square = jnp.zeros((2 * WIN, 128), F32)
        for k in range(4):
            dev = dot(q[p : p + 2].reshape(2 * WIN, KCAT), ecat[k])
            for c in range(SHARD // 128):
                piece = dev[:, 128 * c : 128 * c + 128]
                square = square + piece * piece
        var = jnp.sum(square, axis=1, keepdims=True) * (1.0 / D)
        rstd[p : p + 2] = jnp.broadcast_to(lax.rsqrt(var + 1e-05), (2 * WIN, 128)).reshape(2, WIN, 128)


def gelu(h):
    c = math.sqrt(2.0 / math.pi)
    half = 0.5 * h
    return half + half * jnp.tanh(h * (c + (c * 0.044715) * (h * h)))


def away_body(group, q, rstd, mcats, downs, act, send):
    rows = (group[1] - group[0]) * WIN
    x = q[group[0] : group[1]].reshape(rows, KCAT)
    scale = rstd[group[0] : group[1]].reshape(rows, 128)[:, :1]
    downs = (downs[0][:, shard_cols(lax.axis_index("tensor") ^ 2)], downs[1][...])
    for side in range(2):
        for j in range(HIDDEN // 512):
            cols = slice(512 * j, 512 * j + 512)
            at = slice(HIDDEN * side + 512 * j, HIDDEN * side + 512 * (j + 1))
            act[:, at] = gelu(dot(x, mcats[side][:, cols]) * scale).astype(BF)
    send[...] = (dot(act[:, :HIDDEN], downs[0]) + dot(act[:, HIDDEN:], downs[1])).astype(BF)


def first_away_kernel(q, rstd, m_own, m24_peer, down, d_peer, m_peer, act, send):
    spread_rows(m24_peer, m_peer)
    away_body(GROUPS[0], q, rstd, (m_own, m_peer), (down, d_peer), act, send)


def away_kernel(group, q, rstd, m_own, m_peer, down, d_peer, act, send):
    away_body(group, q, rstd, (m_own, m_peer), (down, d_peer), act, send)


def add_stats(table, p, x):
    lane = lax.broadcasted_iota(jnp.int32, (WIN, WIN), 1)
    mean = jnp.sum(x, axis=1, keepdims=True) * (1.0 / SHARD)
    off = x - mean
    square = jnp.sum(off * off, axis=1, keepdims=True)
    return jnp.where(lane == p, mean, jnp.where(lane == PATCHES + p, square, table))


def home_rows(group, q, ecat, down, d_peer, act):
    own = down[:, shard_cols(lax.axis_index("tensor"))]
    x = dot(act[:, :HIDDEN], own) + dot(act[:, HIDDEN:], d_peer[...])
    return x + dot(q[group[0] : group[1]].reshape((group[1] - group[0]) * WIN, KCAT), ecat[0])


def home_kernel(q, ecat, d_own, d_peer, a0, a1, part):
    for group, act in zip(GROUPS[:2], (a0, a1)):
        part[WIN * group[0] : WIN * group[1], :] = home_rows(group, q, ecat, d_own, d_peer, act)


def weights(info, counts, members, own):
    slot = lax.axis_index("member")
    share = 1.0 / (1.0 + counts)
    member = lax.broadcasted_iota(jnp.int32, (members, WIN), 0)
    lane = lax.broadcasted_iota(jnp.int32, (1, WIN), 1)
    factor = info[1:2, :] / jnp.sum(share, axis=0, keepdims=True)
    if members > 4:
        factor = jnp.where((((lane // own) ^ slot) >> 2) & 1 == 0, factor, 0.0)
    rows = [jnp.sum(jnp.where(member == slot ^ k, share, 0.0), axis=0, keepdims=True) * factor for k in (0, 4)]
    row = lax.broadcasted_iota(jnp.int32, (8, WIN), 0)
    return jnp.where(row == 0, rows[0], jnp.where(row == 1, rows[1], 0.0))


def state_kernel(
    members, own, q, ecat, d_own, d_peer, a2, a3, part, c0, c1, c2, info, mine, late, state, last, stats, shares
):
    shares[...] = weights(info, mine[...] + late[...], members, own)
    last[...] = home_rows(GROUPS[3], q, ecat, d_own, d_peer, a3)
    table = jnp.zeros((WIN, WIN), F32)
    for g, cross in enumerate((c0, c1, c2)):
        group = GROUPS[g]
        rows = slice(WIN * group[0], WIN * group[1])
        x = part[rows, :] if g < 2 else home_rows(group, q, ecat, d_own, d_peer, a2)
        x = x + cross[...].astype(F32)
        state[rows, :] = x
        for i, p in enumerate(range(*group)):
            table = add_stats(table, p, x[i * WIN : (i + 1) * WIN])
    stats[...] = table.T[: 2 * PATCHES]


def last_state_kernel(last, cross, prev, state, stats):
    x = last[...] + cross[...].astype(F32)
    state[...] = x
    table = jnp.zeros((WIN, WIN), F32)
    for i, p in enumerate(range(*GROUPS[3])):
        table = add_stats(table, p, x[i * WIN : (i + 1) * WIN])
    stats[...] = prev[...] + table.T[: 2 * PATCHES]


def head_kernel(stats, state, last, heads, shard, shares, send, keep, scr):
    core = lax.axis_index("tensor") & 1
    first = GROUPS[3][0]
    scale = lax.rsqrt(stats[PATCHES:, :] * (1.0 / D) + 1e-05)
    table = jnp.concatenate([stats[:PATCHES, :], scale, jnp.zeros((WIN - 2 * PATCHES, WIN), F32)], axis=0).T
    total = jnp.zeros((WIN, HORIZONS), F32)
    for p in range(PATCHES):
        x = state[p * WIN : (p + 1) * WIN, :] if p < first else last[(p - first) * WIN : (p - first + 1) * WIN, :]
        y = (x - table[:, p : p + 1]) * table[:, PATCHES + p : PATCHES + p + 1] * shard[25:26, :]
        total = total + lax.dot_general(
            y.astype(BF), heads[p], (((1,), (1,)), ((), ())), preferred_element_type=F32
        )
    scr[:, :HORIZONS] = total
    scr[:, HORIZONS:] = jnp.zeros((WIN, WIN - HORIZONS), F32)
    scr[...] = scr[...].T
    for c in range(2):
        for out, side in ((keep, core), (send, 1 - core)):
            out[24 * c : 24 * c + 24, :] = scr[pl.ds(pl.multiple_of(48 * c + 24 * side, 8), 24), :]
    keep[48:, :] = 0.5 * shares[...]
    send[48:, :] = jnp.zeros((8, WIN), F32)


def weigh_kernel(mine, theirs, out):
    at = pl.ds(pl.multiple_of(24 * (lax.axis_index("tensor") >> 1), 8), 24)
    here = mine[48:49, :] + theirs[49:50, :]
    there = mine[49:50, :] + theirs[48:49, :]
    out[...] = mine[at, :] * here + theirs[at, :] * there


def rank_kernel(levels, own, total, info, target, average, levels_out, scr, res, ranks):
    t = lax.axis_index("tensor")
    slot = lax.axis_index("member")
    per = total.shape[0]
    pred = total[...] + info[0:1, :]
    wanted = target[pl.ds(pl.multiple_of(24 * t, 8), per), :]
    resid = jnp.abs(wanted - pred)
    scr[...] = jnp.zeros((WIN, WIN), F32)
    scr[:per, :] = pred
    scr[...] = scr[...].T
    if own % 8 == 0:
        average[...] = scr[pl.ds(pl.multiple_of(own * slot, 8), own), :per]
    else:
        at = own * slot
        rows = scr[pl.ds(pl.multiple_of((at // 8) * 8, 8), 8), :per]
        pick = rows[:own]
        for s in range(1, 8 // own):
            pick = jnp.where(at % 8 == s * own, rows[s * own : (s + 1) * own], pick)
        average[...] = pick
    res[...] = jnp.zeros((WIN, WIN), F32)
    res[:per, :] = resid
    across = res[...].T
    j = lax.broadcasted_iota(jnp.int32, (WIN, WIN), 0)
    i = lax.broadcasted_iota(jnp.int32, (WIN, WIN), 1)
    earlier = j < i
    for h in range(per):
        row, col = resid[h : h + 1, :], across[:, h : h + 1]
        before = (col < row) | ((col == row) & earlier)
        ranks[h : h + 1, :] = jnp.sum(before.astype(F32), axis=0, keepdims=True)
    order = ranks[...]
    lane = lax.broadcasted_iota(jnp.int32, (per, WIN), 1)
    table = jnp.zeros((per, WIN), F32)
    for n, level in enumerate(levels):
        value = jnp.sum(jnp.where(order == float(level), resid, 0.0), axis=1, keepdims=True)
        table = jnp.where(lane == n, value, table)
    res[:per, :] = table
    levels_out[...] = res[...].T[: len(levels), :per]


def per_device(series, starts, counts, lifting, location, gain_one, up, down, gain_two, readout):
    members = lax.axis_size("member")
    own = counts.shape[1]
    sds = jax.ShapeDtypeStruct

    def over_tensor(x, k):
        return lax.ppermute(x, "tensor", [(i, i ^ k) for i in range(4)])

    def over_member(x, k):
        return lax.ppermute(x, "member", [(i, i ^ k) for i in range(members)])

    shard_bf = pltpu.VMEM((D, SHARD), BF)
    packed, every, give_x = call(
        pack_kernel,
        (pltpu.VMEM((32, SHARD), F32), pltpu.VMEM((members, WIN), F32), shard_bf),
        [HBM] * 6,
        (lifting, location, gain_one, gain_two, counts.T, down),
        2 * US,
        1000,
        [
            pltpu.VMEM((1, SHARD), F32),
            pltpu.VMEM((1, SHARD), F32),
            pltpu.VMEM((own, members), jnp.int32),
            pltpu.VMEM((WIN, WIN), F32),
            pltpu.SemaphoreType.DMA((6,)),
        ],
    )
    shards = [packed] + [over_tensor(packed, k) for k in (1, 2, 3)]
    peer_x = over_tensor(give_x, 1)

    heads = jnp.swapaxes(readout[0], 1, 2)
    up = up[0]
    give_y, q, info, target = call(
        windows_kernel,
        (
            shard_bf,
            pltpu.VMEM((PATCHES, WIN, KCAT), BF),
            pltpu.VMEM((8, WIN), F32),
            pltpu.VMEM((WIN, WIN), F32),
        ),
        [HBM] * 3,
        (series.reshape(WIN, WIN), starts.reshape(1, WIN), down),
        5 * US,
        1000,
        [pltpu.VMEM((WIN, WIN), F32), pltpu.VMEM((1, WIN), jnp.int32), pltpu.SemaphoreType.DMA((3,))],
        after=(packed,),
    )

    hops = [k for k in (1, 3, 8, 24) if k < members]
    steps = iter(hops)

    def hop(value, after=None):
        k = next(steps, None)
        if after is not None:
            value = lax.optimization_barrier((value, after))[0]
        return value if k is None else value + over_member(value, k)

    def hop_parts(value, after=None):
        k = next(steps, None)
        if after is not None:
            value = lax.optimization_barrier((value, after))[0]
        return value, jnp.zeros_like(value) if k is None else over_member(value, k)

    every, late = hop_parts(every)
    m24, ecat, every = call(
        lift_kernel,
        (pltpu.VMEM((32, HIDDEN), F32), pltpu.VMEM((4, KCAT, SHARD), BF), pltpu.VMEM((members, WIN), F32)),
        [V] * 7,
        (up, *shards, every, late),
        3 * US,
        1000,
        [pltpu.VMEM((4, 96, SHARD), BF)],
        after=(info,),
    )
    m24_peer = over_tensor(m24, 1)
    mcat_shape = pltpu.VMEM((KCAT, HIDDEN), BF)
    rstd, m_own = call(
        scale_kernel,
        (pltpu.VMEM((PATCHES, WIN, 128), F32), mcat_shape),
        [V] * 3,
        (q, ecat, m24),
        2 * US,
        1000,
    )

    def sums(group):
        rows = (group[1] - group[0]) * WIN
        return pltpu.VMEM((rows, 2 * HIDDEN), BF), pltpu.VMEM((rows, SHARD), BF)

    m_peer, act, send = call(
        first_away_kernel,
        (mcat_shape, *sums(GROUPS[0])),
        [V] * 6,
        (q, rstd, m_own, m24_peer, down[0], peer_x),
        4 * US,
        1000,
    )
    acts, crossed = [act], [over_tensor(send, 2)]
    fed = (q, rstd, m_own, m_peer, down[0], peer_x)
    peer_y = over_tensor(lax.optimization_barrier((give_y, send))[0], 1)
    for g in range(1, 4):
        act, send = call(
            functools.partial(away_kernel, GROUPS[g]),
            sums(GROUPS[g]),
            [V] * 6,
            fed,
            4 * US,
            1000,
            after=(every, crossed[g - 2]) if g > 1 else (),
        )
        acts.append(act)
        crossed.append(over_tensor(send, 2))
        if g < 3:
            every = hop(every, send)
    every, late = hop_parts(every, send)
    homes = (q, ecat, down[0], peer_y)
    (part,) = call(
        home_kernel,
        (pltpu.VMEM((GROUPS[1][1] * WIN, SHARD), F32),),
        [V] * 6,
        (*homes, *acts[:2]),
        US // 10,
        1000,
        after=(send,),
    )
    tail = (GROUPS[3][1] - GROUPS[3][0]) * WIN
    state, last, stats, shares = call(
        functools.partial(state_kernel, members, own),
        (
            pltpu.VMEM((GROUPS[2][1] * WIN, SHARD), F32),
            pltpu.VMEM((tail, SHARD), F32),
            pltpu.VMEM((2 * PATCHES, WIN), F32),
            pltpu.VMEM((8, WIN), F32),
        ),
        [V] * 13,
        (*homes, *acts[2:], part, *crossed[:3], info, every, late),
        5 * US,
        1000,
    )
    last, stats = call(
        last_state_kernel,
        (pltpu.VMEM((tail, SHARD), F32), pltpu.VMEM((2 * PATCHES, WIN), F32)),
        [V] * 3,
        (last, crossed[3], stats),
        US,
        1000,
    )
    features = SHARD
    for k in (1, 2):
        other = over_tensor(stats, k)
        gap = stats[:PATCHES] - other[:PATCHES]
        square = stats[PATCHES:] + other[PATCHES:] + (0.5 * features) * (gap * gap)
        stats = jnp.concatenate([0.5 * (stats[:PATCHES] + other[:PATCHES]), square], axis=0)
        features *= 2
    sent, held = call(
        head_kernel,
        (pltpu.VMEM((56, WIN), F32),) * 2,
        [V] * 6,
        (stats, state, last, heads, packed, shares),
        US,
        1000,
        [pltpu.VMEM((WIN, WIN), F32)],
    )
    total = held + over_tensor(sent, 1)
    total = total + over_tensor(total, 2)
    if members > 4:
        pairs = [(4 * m + t, 4 * (m ^ 4) + (t ^ 2)) for m in range(members) for t in range(4)]
        met = lax.ppermute(total, ("member", "tensor"), pairs)
    else:
        met = jnp.zeros_like(total)
    (total,) = call(weigh_kernel, (pltpu.VMEM((24, WIN), F32),), [V] * 2, (total, met), US, 1000)
    for ring in ((1, 2, 3), (8, 16, 24)):
        if ring[-1] < members:
            got = [over_member(total, k) for k in ring]
            total = total + got[0] + got[1] + got[2]

    levels = tuple(WIN * n // 100 for n in (50, 80, 90, 95))
    return call(
        functools.partial(rank_kernel, levels, own),
        (sds((own, 24), F32), sds((4, 24), F32)),
        [V] * 3,
        (total, info, target),
        US,
        1000,
        [pltpu.VMEM((WIN, WIN), F32), pltpu.VMEM((WIN, WIN), F32), pltpu.VMEM((24, WIN), F32)],
    )


def solution(mesh):
    placed = (
        P(),
        P(),
        P(None, "member"),
        P("member", None, "tensor"),
        P("member", None, "tensor"),
        P("member", "tensor"),
        P("member", None, "tensor"),
        P("member", "tensor", None),
        P("member", "tensor"),
        P("member", None, "tensor", None),
    )
    return jax.shard_map(
        per_device,
        mesh=mesh,
        in_specs=placed,
        out_specs=(P("member", "tensor"), P(None, "tensor")),
        check_vma=False,
    )
```

```python
import functools
import math

import jax
import jax.numpy as jnp
from jax import lax
from jax.experimental import pallas as pl
from jax.experimental.pallas import tpu as pltpu
from jax.sharding import PartitionSpec as P

BF, F32 = jnp.bfloat16, jnp.float32
PATCHES, PLEN, STRIDE, LOOK = 8, 16, 8, 72
WIN, D, SHARD, HIDDEN, HORIZONS = 128, 2048, 512, 2048, 96
KCAT = 256
MIB = 1 << 20
US = 10**9
GROUPS = ((0, 1), (1, 3), (3, 5), (5, 7), (7, 8))


def split3(x):
    a = x.astype(BF)
    rest = x - a.astype(F32)
    b = rest.astype(BF)
    c = (rest - b.astype(F32)).astype(BF)
    return a, b, c


def dot(a, b):
    return jnp.dot(a, b, preferred_element_type=F32)


def roll_left(x, by):
    lanes = x.shape[1]
    by = by % lanes
    return x if by == 0 else pltpu.roll(x, lanes - by, 1)


def shard_cols(t):
    return pl.ds(pl.multiple_of(SHARD * t, SHARD), SHARD)


def call(body, out_shape, in_specs, args, flops, nbytes, scratch=(), limit=24 * MIB, after=()):
    taken, held = len(in_specs), len(after)

    def run(*refs):
        body(*refs[:taken], *refs[taken + held :])

    args = tuple(
        pltpu.with_memory_space_constraint(x, pltpu.HBM if spec is HBM else pltpu.VMEM)
        for x, spec in zip(args, in_specs)
    ) + tuple(after)
    in_specs = list(in_specs) + [ANY] * held
    return pl.pallas_call(
        run,
        out_shape=out_shape,
        in_specs=in_specs,
        out_specs=jax.tree.map(lambda _: pl.BlockSpec(memory_space=pltpu.VMEM), out_shape),
        scratch_shapes=list(scratch),
        compiler_params=pltpu.CompilerParams(vmem_limit_bytes=limit),
        cost_estimate=pl.CostEstimate(flops=flops, bytes_accessed=nbytes, transcendentals=0),
    )(*args)


V = pl.BlockSpec(memory_space=pltpu.VMEM)
ANY = pl.BlockSpec(memory_space=pl.ANY)
HBM = pl.BlockSpec(memory_space=pltpu.HBM)


def pack_kernel(lifting, location, gain_one, gain_two, counts_h, down, packed, every, give, g1, g2, counts, scr, sem):
    t = lax.axis_index("tensor")
    loads = [
        pltpu.make_async_copy(lifting.at[0], packed.at[0:PLEN, :], sem.at[0]),
        pltpu.make_async_copy(location.at[0], packed.at[PLEN : PLEN + PATCHES, :], sem.at[1]),
        pltpu.make_async_copy(gain_one, g1, sem.at[2]),
        pltpu.make_async_copy(gain_two, g2, sem.at[3]),
        pltpu.make_async_copy(counts_h, counts, sem.at[4]),
        pltpu.make_async_copy(down.at[0, :, shard_cols(t ^ 3)], give, sem.at[5]),
    ]
    for load in loads:
        load.start()
    own, members = counts.shape
    scr[...] = jnp.zeros((WIN, WIN), F32)
    for load in loads[:5]:
        load.wait()
    row = lax.broadcasted_iota(jnp.int32, (8, SHARD), 0)
    packed[PLEN + PATCHES :, :] = jnp.where(row == 0, g1[...], jnp.where(row == 1, g2[...], 0.0))
    scr[:own, :members] = counts[...].astype(F32)
    columns = scr[...].T[:members]
    at = own * lax.axis_index("member")
    place = lax.broadcasted_iota(jnp.int32, (members, WIN), 1) - at
    placed = jnp.zeros((members, WIN), F32)
    for j in range(own):
        placed = jnp.where(place == j, columns[:, j : j + 1], placed)
    every[...] = placed
    loads[5].wait()


def lift_parts(t, shards, up, lhs):
    for n, (k, shard) in enumerate(shards):
        gain = shard[PLEN + PATCHES : PLEN + PATCHES + 1, :]
        row = lax.broadcasted_iota(jnp.int32, (32, SHARD), 0)
        rows = jnp.where(row < PLEN + PATCHES, shard[...] * gain, jnp.where(row == PLEN + PATCHES, gain, 0.0))
        for i, part in enumerate(split3(rows)):
            lhs[n, 32 * i : 32 * i + 32, :] = part
    for j in range(HIDDEN // 512):
        cols = slice(512 * j, 512 * j + 512)
        m = sum(dot(lhs[n], up[shard_cols(t ^ k), cols]) for n, (k, _) in enumerate(shards))
        yield cols, m[:32] + m[32:64] + m[64:96]


def windows_kernel(series_h, starts_h, down, give_y, q, info, target, series, starts, sem):
    t = lax.axis_index("tensor")
    small = [
        pltpu.make_async_copy(series_h, series, sem.at[0]),
        pltpu.make_async_copy(starts_h, starts, sem.at[1]),
    ]
    loads = [pltpu.make_async_copy(down.at[0, :, shard_cols(t ^ 1)], give_y, sem.at[2])]
    for load in small + loads:
        load.start()
    for load in small:
        load.wait()
    lane = lax.broadcasted_iota(jnp.int32, (WIN, WIN), 1)
    first = jnp.broadcast_to(starts[...].astype(F32), (WIN, WIN)).T.astype(jnp.int32)
    row, offset = first >> 7, first & 127
    picks = [(row + k == lane).astype(F32).astype(BF) for k in range(3)]
    parts = split3(series[...])
    rows = [sum(dot(pick, part) for part in parts) for pick in picks]
    x = jnp.concatenate(rows, axis=1)
    offset = jnp.concatenate([offset] * 3, axis=1)
    for bit in range(7):
        x = jnp.where((offset >> bit) & 1 == 1, roll_left(x, 1 << bit), x)
    target[...] = roll_left(x, LOOK)[:, :WIN].T
    look = x[:, :WIN]
    center = jnp.sum(jnp.where(lane < LOOK, look, 0.0), axis=1, keepdims=True) * (1.0 / LOOK)
    dev = jnp.where(lane < LOOK, look - center, 0.0)
    spread = jnp.sqrt(jnp.sum(dev * dev, axis=1, keepdims=True) * (1.0 / LOOK) + 1e-05)
    normed = dev / spread
    pair = jnp.where(lane == 0, center, jnp.where(lane == 1, spread, 0.0)).T
    info[...] = pair[:8]
    block = lane // 32
    for p in range(PATCHES):
        one = jnp.where(lane < PLEN, roll_left(normed, STRIDE * p), 0.0)
        one = jnp.where(lane == PLEN + p, 1.0, one)
        two = one + pltpu.roll(one, 32, 1)
        four = two + pltpu.roll(two, 64, 1)
        a, b, c = (v.astype(F32) for v in split3(four))
        q[p, :, :WIN] = jnp.where(block < 2, a, b).astype(BF)
        q[p, :, WIN:] = jnp.where(block == 0, a, jnp.where(block == 1, c, 0.0)).astype(BF)
    for load in loads:
        load.wait()


def cat_rows(x):
    b1, b2, b3 = split3(x)
    zero = jnp.zeros_like(b1)
    return [b1, b2, b1, b2, b3, b1, zero, zero]


def lift_kernel(up, s0, s1, s2, s3, mine, late, m24, ecat, every, lhs):
    t = lax.axis_index("tensor")
    every[...] = mine[...] + late[...]
    shards = (s0, s1, s2, s3)
    mean = sum(jnp.sum(s[...], axis=1, keepdims=True) for s in shards) * (1.0 / D)
    keep = lax.broadcasted_iota(jnp.int32, (32, SHARD), 0) < PLEN + PATCHES
    for cols, m in lift_parts(t, tuple(enumerate(shards)), up, lhs):
        m24[:, cols] = m - mean * m[PLEN + PATCHES : PLEN + PATCHES + 1, :]
    for k, shard in enumerate(shards):
        centred = jnp.where(keep, shard[...] - mean, 0.0)
        for i, part in enumerate(cat_rows(centred)):
            ecat[k, 32 * i : 32 * i + 32, :] = part


def spread_rows(m24, mcat):
    for j in range(HIDDEN // 512):
        cols = slice(512 * j, 512 * j + 512)
        row = lax.broadcasted_iota(jnp.int32, (32, 512), 0)
        for i, part in enumerate(cat_rows(jnp.where(row < PLEN + PATCHES, m24[:, cols], 0.0))):
            mcat[32 * i : 32 * i + 32, cols] = part


def scale_kernel(q, ecat, m24, rstd, mcat):
    spread_rows(m24, mcat)
    for p in range(0, PATCHES, 2):
        square = jnp.zeros((2 * WIN, 128), F32)
        for k in range(4):
            dev = dot(q[p : p + 2].reshape(2 * WIN, KCAT), ecat[k])
            for c in range(SHARD // 128):
                piece = dev[:, 128 * c : 128 * c + 128]
                square = square + piece * piece
        var = jnp.sum(square, axis=1, keepdims=True) * (1.0 / D)
        rstd[p : p + 2] = jnp.broadcast_to(lax.rsqrt(var + 1e-05), (2 * WIN, 128)).reshape(2, WIN, 128)


def gelu(h):
    c = math.sqrt(2.0 / math.pi)
    half = 0.5 * h
    return half + half * jnp.tanh(h * (c + (c * 0.044715) * (h * h)))


def away_body(group, q, rstd, mcats, downs, act, send):
    rows = (group[1] - group[0]) * WIN
    x = q[group[0] : group[1]].reshape(rows, KCAT)
    scale = rstd[group[0] : group[1]].reshape(rows, 128)[:, :1]
    downs = (downs[0][:, shard_cols(lax.axis_index("tensor") ^ 2)], downs[1][...])
    for side in range(2):
        for j in range(HIDDEN // 512):
            cols = slice(512 * j, 512 * j + 512)
            at = slice(HIDDEN * side + 512 * j, HIDDEN * side + 512 * (j + 1))
            act[:, at] = gelu(dot(x, mcats[side][:, cols]) * scale).astype(BF)
    send[...] = (dot(act[:, :HIDDEN], downs[0]) + dot(act[:, HIDDEN:], downs[1])).astype(BF)


def first_away_kernel(q, rstd, m_own, m24_peer, down, d_peer, m_peer, act, send):
    spread_rows(m24_peer, m_peer)
    away_body(GROUPS[0], q, rstd, (m_own, m_peer), (down, d_peer), act, send)


def away_kernel(group, q, rstd, m_own, m_peer, down, d_peer, act, send):
    away_body(group, q, rstd, (m_own, m_peer), (down, d_peer), act, send)


def add_stats(table, p, x):
    lane = lax.broadcasted_iota(jnp.int32, (WIN, WIN), 1)
    mean = jnp.sum(x, axis=1, keepdims=True) * (1.0 / SHARD)
    off = x - mean
    square = jnp.sum(off * off, axis=1, keepdims=True)
    return jnp.where(lane == p, mean, jnp.where(lane == PATCHES + p, square, table))


def home_rows(group, q, ecat, down, d_peer, act):
    own = down[:, shard_cols(lax.axis_index("tensor"))]
    x = dot(act[:, :HIDDEN], own) + dot(act[:, HIDDEN:], d_peer[...])
    return x + dot(q[group[0] : group[1]].reshape((group[1] - group[0]) * WIN, KCAT), ecat[0])


def home_kernel(q, ecat, d_own, d_peer, a0, a1, a2, part):
    for group, act in zip(GROUPS[:3], (a0, a1, a2)):
        part[WIN * group[0] : WIN * group[1], :] = home_rows(group, q, ecat, d_own, d_peer, act)


def weights(info, counts, members, own):
    slot = lax.axis_index("member")
    share = 1.0 / (1.0 + counts)
    member = lax.broadcasted_iota(jnp.int32, (members, WIN), 0)
    lane = lax.broadcasted_iota(jnp.int32, (1, WIN), 1)
    factor = info[1:2, :] / jnp.sum(share, axis=0, keepdims=True)
    if members > 4:
        factor = jnp.where((((lane // own) ^ slot) >> 2) & 1 == 0, factor, 0.0)
    rows = [jnp.sum(jnp.where(member == slot ^ k, share, 0.0), axis=0, keepdims=True) * factor for k in (0, 4)]
    row = lax.broadcasted_iota(jnp.int32, (8, WIN), 0)
    return jnp.where(row == 0, rows[0], jnp.where(row == 1, rows[1], 0.0))


def state_kernel(q, ecat, d_own, d_peer, a3, a4, part, c0, c1, c2, c3, state, last, stats):
    last[...] = home_rows(GROUPS[4], q, ecat, d_own, d_peer, a4)
    table = jnp.zeros((WIN, WIN), F32)
    for g, cross in enumerate((c0, c1, c2, c3)):
        group = GROUPS[g]
        rows = slice(WIN * group[0], WIN * group[1])
        x = part[rows, :] if g < 3 else home_rows(group, q, ecat, d_own, d_peer, a3)
        x = x + cross[...].astype(F32)
        state[rows, :] = x
        for i, p in enumerate(range(*group)):
            table = add_stats(table, p, x[i * WIN : (i + 1) * WIN])
    stats[...] = table.T[: 2 * PATCHES]


def last_state_kernel(members, own, last, cross, prev, info, mine, late, state, stats, shares):
    x = last[...] + cross[...].astype(F32)
    state[...] = x
    table = jnp.zeros((WIN, WIN), F32)
    for i, p in enumerate(range(*GROUPS[4])):
        table = add_stats(table, p, x[i * WIN : (i + 1) * WIN])
    stats[...] = prev[...] + table.T[: 2 * PATCHES]
    shares[...] = weights(info, mine[...] + late[...], members, own)


def head_kernel(stats, state, last, heads, shard, shares, send, keep, scr):
    core = lax.axis_index("tensor") & 1
    first = GROUPS[4][0]
    scale = lax.rsqrt(stats[PATCHES:, :] * (1.0 / D) + 1e-05)
    table = jnp.concatenate([stats[:PATCHES, :], scale, jnp.zeros((WIN - 2 * PATCHES, WIN), F32)], axis=0).T
    total = jnp.zeros((WIN, HORIZONS), F32)
    for p in range(PATCHES):
        x = state[p * WIN : (p + 1) * WIN, :] if p < first else last[(p - first) * WIN : (p - first + 1) * WIN, :]
        y = (x - table[:, p : p + 1]) * table[:, PATCHES + p : PATCHES + p + 1] * shard[25:26, :]
        total = total + lax.dot_general(
            y.astype(BF), heads[p], (((1,), (1,)), ((), ())), preferred_element_type=F32
        )
    scr[:, :HORIZONS] = total
    scr[:, HORIZONS:] = jnp.zeros((WIN, WIN - HORIZONS), F32)
    scr[...] = scr[...].T
    for c in range(2):
        for out, side in ((keep, core), (send, 1 - core)):
            out[24 * c : 24 * c + 24, :] = scr[pl.ds(pl.multiple_of(48 * c + 24 * side, 8), 24), :]
    keep[48:, :] = 0.5 * shares[...]
    send[48:, :] = jnp.zeros((8, WIN), F32)


def weigh_kernel(mine, theirs, out):
    at = pl.ds(pl.multiple_of(24 * (lax.axis_index("tensor") >> 1), 8), 24)
    here = mine[48:49, :] + theirs[49:50, :]
    there = mine[49:50, :] + theirs[48:49, :]
    out[...] = mine[at, :] * here + theirs[at, :] * there


def rank_kernel(levels, own, total, info, target, average, levels_out, scr, res, ranks):
    t = lax.axis_index("tensor")
    slot = lax.axis_index("member")
    per = total.shape[0]
    pred = total[...] + info[0:1, :]
    wanted = target[pl.ds(pl.multiple_of(24 * t, 8), per), :]
    resid = jnp.abs(wanted - pred)
    scr[...] = jnp.zeros((WIN, WIN), F32)
    scr[:per, :] = pred
    scr[...] = scr[...].T
    if own % 8 == 0:
        average[...] = scr[pl.ds(pl.multiple_of(own * slot, 8), own), :per]
    else:
        at = own * slot
        rows = scr[pl.ds(pl.multiple_of((at // 8) * 8, 8), 8), :per]
        pick = rows[:own]
        for s in range(1, 8 // own):
            pick = jnp.where(at % 8 == s * own, rows[s * own : (s + 1) * own], pick)
        average[...] = pick
    res[...] = jnp.zeros((WIN, WIN), F32)
    res[:per, :] = resid
    across = res[...].T
    j = lax.broadcasted_iota(jnp.int32, (WIN, WIN), 0)
    i = lax.broadcasted_iota(jnp.int32, (WIN, WIN), 1)
    earlier = j < i
    for h in range(per):
        row, col = resid[h : h + 1, :], across[:, h : h + 1]
        before = (col < row) | ((col == row) & earlier)
        ranks[h : h + 1, :] = jnp.sum(before.astype(F32), axis=0, keepdims=True)
    order = ranks[...]
    lane = lax.broadcasted_iota(jnp.int32, (per, WIN), 1)
    table = jnp.zeros((per, WIN), F32)
    for n, level in enumerate(levels):
        value = jnp.sum(jnp.where(order == float(level), resid, 0.0), axis=1, keepdims=True)
        table = jnp.where(lane == n, value, table)
    res[:per, :] = table
    levels_out[...] = res[...].T[: len(levels), :per]


def per_device(series, starts, counts, lifting, location, gain_one, up, down, gain_two, readout):
    members = lax.axis_size("member")
    own = counts.shape[1]
    sds = jax.ShapeDtypeStruct

    def over_tensor(x, k):
        return lax.ppermute(x, "tensor", [(i, i ^ k) for i in range(4)])

    def over_member(x, k):
        return lax.ppermute(x, "member", [(i, i ^ k) for i in range(members)])

    shard_bf = pltpu.VMEM((D, SHARD), BF)
    packed, every, give_x = call(
        pack_kernel,
        (pltpu.VMEM((32, SHARD), F32), pltpu.VMEM((members, WIN), F32), shard_bf),
        [HBM] * 6,
        (lifting, location, gain_one, gain_two, counts.T, down),
        2 * US,
        1000,
        [
            pltpu.VMEM((1, SHARD), F32),
            pltpu.VMEM((1, SHARD), F32),
            pltpu.VMEM((own, members), jnp.int32),
            pltpu.VMEM((WIN, WIN), F32),
            pltpu.SemaphoreType.DMA((6,)),
        ],
    )
    shards = [packed] + [over_tensor(packed, k) for k in (1, 2, 3)]
    peer_x = over_tensor(give_x, 1)

    heads = jnp.swapaxes(readout[0], 1, 2)
    up = up[0]
    give_y, q, info, target = call(
        windows_kernel,
        (
            shard_bf,
            pltpu.VMEM((PATCHES, WIN, KCAT), BF),
            pltpu.VMEM((8, WIN), F32),
            pltpu.VMEM((WIN, WIN), F32),
        ),
        [HBM] * 3,
        (series.reshape(WIN, WIN), starts.reshape(1, WIN), down),
        5 * US,
        1000,
        [pltpu.VMEM((WIN, WIN), F32), pltpu.VMEM((1, WIN), jnp.int32), pltpu.SemaphoreType.DMA((3,))],
        after=(packed,),
    )

    hops = [k for k in (1, 3, 8, 24) if k < members]
    steps = iter(hops)

    def hop(value, after=None):
        k = next(steps, None)
        if after is not None:
            value = lax.optimization_barrier((value, after))[0]
        return value if k is None else value + over_member(value, k)

    def hop_parts(value, after=None):
        k = next(steps, None)
        if after is not None:
            value = lax.optimization_barrier((value, after))[0]
        return value, jnp.zeros_like(value) if k is None else over_member(value, k)

    every, late = hop_parts(every)
    m24, ecat, every = call(
        lift_kernel,
        (pltpu.VMEM((32, HIDDEN), F32), pltpu.VMEM((4, KCAT, SHARD), BF), pltpu.VMEM((members, WIN), F32)),
        [V] * 7,
        (up, *shards, every, late),
        3 * US,
        1000,
        [pltpu.VMEM((4, 96, SHARD), BF)],
        after=(info,),
    )
    m24_peer = over_tensor(m24, 1)
    mcat_shape = pltpu.VMEM((KCAT, HIDDEN), BF)
    rstd, m_own = call(
        scale_kernel,
        (pltpu.VMEM((PATCHES, WIN, 128), F32), mcat_shape),
        [V] * 3,
        (q, ecat, m24),
        2 * US,
        1000,
    )

    def sums(group):
        rows = (group[1] - group[0]) * WIN
        return pltpu.VMEM((rows, 2 * HIDDEN), BF), pltpu.VMEM((rows, SHARD), BF)

    m_peer, act, send = call(
        first_away_kernel,
        (mcat_shape, *sums(GROUPS[0])),
        [V] * 6,
        (q, rstd, m_own, m24_peer, down[0], peer_x),
        4 * US,
        1000,
    )
    acts, crossed = [act], [over_tensor(send, 2)]
    fed = (q, rstd, m_own, m_peer, down[0], peer_x)
    peer_y = over_tensor(lax.optimization_barrier((give_y, send))[0], 1)
    for g in range(1, 5):
        act, send = call(
            functools.partial(away_kernel, GROUPS[g]),
            sums(GROUPS[g]),
            [V] * 6,
            fed,
            4 * US,
            1000,
            after=(every, crossed[g - 2]) if g > 1 else (),
        )
        acts.append(act)
        crossed.append(over_tensor(send, 2))
        if g in (2, 3):
            every = hop(every, send)
    every, late = hop_parts(every, send)
    homes = (q, ecat, down[0], peer_y)
    (part,) = call(
        home_kernel,
        (pltpu.VMEM((GROUPS[2][1] * WIN, SHARD), F32),),
        [V] * 7,
        (*homes, *acts[:3]),
        US // 10,
        1000,
        after=(send,),
    )
    tail = (GROUPS[4][1] - GROUPS[4][0]) * WIN
    state, last, stats = call(
        state_kernel,
        (
            pltpu.VMEM((GROUPS[3][1] * WIN, SHARD), F32),
            pltpu.VMEM((tail, SHARD), F32),
            pltpu.VMEM((2 * PATCHES, WIN), F32),
        ),
        [V] * 11,
        (*homes, *acts[3:], part, *crossed[:4]),
        5 * US,
        1000,
    )
    last, stats, shares = call(
        functools.partial(last_state_kernel, members, own),
        (pltpu.VMEM((tail, SHARD), F32), pltpu.VMEM((2 * PATCHES, WIN), F32), pltpu.VMEM((8, WIN), F32)),
        [V] * 6,
        (last, crossed[4], stats, info, every, late),
        US,
        1000,
    )
    features = SHARD
    for k in (1, 2):
        other = over_tensor(stats, k)
        gap = stats[:PATCHES] - other[:PATCHES]
        square = stats[PATCHES:] + other[PATCHES:] + (0.5 * features) * (gap * gap)
        stats = jnp.concatenate([0.5 * (stats[:PATCHES] + other[:PATCHES]), square], axis=0)
        features *= 2
    sent, held = call(
        head_kernel,
        (pltpu.VMEM((56, WIN), F32),) * 2,
        [V] * 6,
        (stats, state, last, heads, packed, shares),
        US,
        1000,
        [pltpu.VMEM((WIN, WIN), F32)],
    )
    total = held + over_tensor(sent, 1)
    total = total + over_tensor(total, 2)
    if members > 4:
        pairs = [(4 * m + t, 4 * (m ^ 4) + (t ^ 2)) for m in range(members) for t in range(4)]
        met = lax.ppermute(total, ("member", "tensor"), pairs)
    else:
        met = jnp.zeros_like(total)
    (total,) = call(weigh_kernel, (pltpu.VMEM((24, WIN), F32),), [V] * 2, (total, met), US, 1000)
    for ring in ((1, 2, 3), (8, 16, 24)):
        if ring[-1] < members:
            got = [over_member(total, k) for k in ring]
            total = total + got[0] + got[1] + got[2]

    levels = tuple(WIN * n // 100 for n in (50, 80, 90, 95))
    return call(
        functools.partial(rank_kernel, levels, own),
        (sds((own, 24), F32), sds((4, 24), F32)),
        [V] * 3,
        (total, info, target),
        US,
        1000,
        [pltpu.VMEM((WIN, WIN), F32), pltpu.VMEM((WIN, WIN), F32), pltpu.VMEM((24, WIN), F32)],
    )


def solution(mesh):
    placed = (
        P(),
        P(),
        P(None, "member"),
        P("member", None, "tensor"),
        P("member", None, "tensor"),
        P("member", "tensor"),
        P("member", None, "tensor"),
        P("member", "tensor", None),
        P("member", "tensor"),
        P("member", None, "tensor", None),
    )
    return jax.shard_map(
        per_device,
        mesh=mesh,
        in_specs=placed,
        out_specs=(P("member", "tensor"), P(None, "tensor")),
        check_vma=False,
    )
```

```python
import functools
import math

import jax
import jax.numpy as jnp
from jax import lax
from jax.experimental import pallas as pl
from jax.experimental.pallas import tpu as pltpu
from jax.sharding import PartitionSpec as P

BF, F32 = jnp.bfloat16, jnp.float32
PATCHES, PLEN, STRIDE, LOOK = 8, 16, 8, 72
WIN, D, SHARD, HIDDEN, HORIZONS = 128, 2048, 512, 2048, 96
KCAT = 256
MIB = 1 << 20
US = 10**9
GROUPS = ((0, 2), (2, 4), (4, 6), (6, 8))


def split3(x):
    a = x.astype(BF)
    rest = x - a.astype(F32)
    b = rest.astype(BF)
    c = (rest - b.astype(F32)).astype(BF)
    return a, b, c


def dot(a, b):
    return jnp.dot(a, b, preferred_element_type=F32)


def roll_left(x, by):
    lanes = x.shape[1]
    by = by % lanes
    return x if by == 0 else pltpu.roll(x, lanes - by, 1)


def shard_cols(t):
    return pl.ds(pl.multiple_of(SHARD * t, SHARD), SHARD)


def call(body, out_shape, in_specs, args, flops, nbytes, scratch=(), limit=24 * MIB, after=()):
    taken, held = len(in_specs), len(after)

    def run(*refs):
        body(*refs[:taken], *refs[taken + held :])

    args = tuple(
        pltpu.with_memory_space_constraint(x, pltpu.HBM if spec is HBM else pltpu.VMEM)
        for x, spec in zip(args, in_specs)
    ) + tuple(after)
    in_specs = list(in_specs) + [ANY] * held
    return pl.pallas_call(
        run,
        out_shape=out_shape,
        in_specs=in_specs,
        out_specs=jax.tree.map(lambda _: pl.BlockSpec(memory_space=pltpu.VMEM), out_shape),
        scratch_shapes=list(scratch),
        compiler_params=pltpu.CompilerParams(vmem_limit_bytes=limit),
        cost_estimate=pl.CostEstimate(flops=flops, bytes_accessed=nbytes, transcendentals=0),
    )(*args)


V = pl.BlockSpec(memory_space=pltpu.VMEM)
ANY = pl.BlockSpec(memory_space=pl.ANY)
HBM = pl.BlockSpec(memory_space=pltpu.HBM)


def pack_kernel(lifting, location, gain_one, gain_two, counts_h, down, packed, every, give, g1, g2, counts, scr, sem):
    t = lax.axis_index("tensor")
    loads = [
        pltpu.make_async_copy(lifting.at[0], packed.at[0:PLEN, :], sem.at[0]),
        pltpu.make_async_copy(location.at[0], packed.at[PLEN : PLEN + PATCHES, :], sem.at[1]),
        pltpu.make_async_copy(gain_one, g1, sem.at[2]),
        pltpu.make_async_copy(gain_two, g2, sem.at[3]),
        pltpu.make_async_copy(counts_h, counts, sem.at[4]),
        pltpu.make_async_copy(down.at[0, :, shard_cols(t ^ 3)], give, sem.at[5]),
    ]
    for load in loads:
        load.start()
    own, members = counts.shape
    scr[...] = jnp.zeros((WIN, WIN), F32)
    for load in loads[:5]:
        load.wait()
    row = lax.broadcasted_iota(jnp.int32, (8, SHARD), 0)
    packed[PLEN + PATCHES :, :] = jnp.where(row == 0, g1[...], jnp.where(row == 1, g2[...], 0.0))
    scr[:own, :members] = counts[...].astype(F32)
    columns = scr[...].T[:members]
    at = own * lax.axis_index("member")
    place = lax.broadcasted_iota(jnp.int32, (members, WIN), 1) - at
    placed = jnp.zeros((members, WIN), F32)
    for j in range(own):
        placed = jnp.where(place == j, columns[:, j : j + 1], placed)
    every[...] = placed
    loads[5].wait()


def lift_parts(t, shards, up, lhs):
    for n, (k, shard) in enumerate(shards):
        gain = shard[PLEN + PATCHES : PLEN + PATCHES + 1, :]
        row = lax.broadcasted_iota(jnp.int32, (32, SHARD), 0)
        rows = jnp.where(row < PLEN + PATCHES, shard[...] * gain, jnp.where(row == PLEN + PATCHES, gain, 0.0))
        for i, part in enumerate(split3(rows)):
            lhs[n, 32 * i : 32 * i + 32, :] = part
    for j in range(HIDDEN // 512):
        cols = slice(512 * j, 512 * j + 512)
        m = sum(dot(lhs[n], up[shard_cols(t ^ k), cols]) for n, (k, _) in enumerate(shards))
        yield cols, m[:32] + m[32:64] + m[64:96]


def windows_kernel(series, starts, q, info, target):
    lane = lax.broadcasted_iota(jnp.int32, (WIN, WIN), 1)
    first = jnp.broadcast_to(starts[...].astype(F32), (WIN, WIN)).T.astype(jnp.int32)
    row, offset = first >> 7, first & 127
    picks = [(row + k == lane).astype(F32).astype(BF) for k in range(3)]
    parts = split3(series[...])
    rows = [sum(dot(pick, part) for part in parts) for pick in picks]
    x = jnp.concatenate(rows, axis=1)
    offset = jnp.concatenate([offset] * 3, axis=1)
    for bit in range(7):
        x = jnp.where((offset >> bit) & 1 == 1, roll_left(x, 1 << bit), x)
    target[...] = roll_left(x, LOOK)[:, :WIN].T
    look = x[:, :WIN]
    center = jnp.sum(jnp.where(lane < LOOK, look, 0.0), axis=1, keepdims=True) * (1.0 / LOOK)
    dev = jnp.where(lane < LOOK, look - center, 0.0)
    spread = jnp.sqrt(jnp.sum(dev * dev, axis=1, keepdims=True) * (1.0 / LOOK) + 1e-05)
    normed = dev / spread
    pair = jnp.where(lane == 0, center, jnp.where(lane == 1, spread, 0.0)).T
    info[...] = pair[:8]
    block = lane // 32
    for p in range(PATCHES):
        one = jnp.where(lane < PLEN, roll_left(normed, STRIDE * p), 0.0)
        one = jnp.where(lane == PLEN + p, 1.0, one)
        two = one + pltpu.roll(one, 32, 1)
        four = two + pltpu.roll(two, 64, 1)
        a, b, c = (v.astype(F32) for v in split3(four))
        q[p, :, :WIN] = jnp.where(block < 2, a, b).astype(BF)
        q[p, :, WIN:] = jnp.where(block == 0, a, jnp.where(block == 1, c, 0.0)).astype(BF)


def cat_rows(x):
    b1, b2, b3 = split3(x)
    zero = jnp.zeros_like(b1)
    return [b1, b2, b1, b2, b3, b1, zero, zero]


def lift_kernel(up, s0, s1, s2, s3, mine, late, m24, ecat, every, lhs):
    t = lax.axis_index("tensor")
    every[...] = mine[...] + late[...]
    shards = (s0, s1, s2, s3)
    mean = sum(jnp.sum(s[...], axis=1, keepdims=True) for s in shards) * (1.0 / D)
    keep = lax.broadcasted_iota(jnp.int32, (32, SHARD), 0) < PLEN + PATCHES
    for cols, m in lift_parts(t, tuple(enumerate(shards)), up, lhs):
        m24[:, cols] = m - mean * m[PLEN + PATCHES : PLEN + PATCHES + 1, :]
    for k, shard in enumerate(shards):
        centred = jnp.where(keep, shard[...] - mean, 0.0)
        for i, part in enumerate(cat_rows(centred)):
            ecat[k, 32 * i : 32 * i + 32, :] = part


def spread_rows(m24, mcat):
    for j in range(HIDDEN // 512):
        cols = slice(512 * j, 512 * j + 512)
        row = lax.broadcasted_iota(jnp.int32, (32, 512), 0)
        for i, part in enumerate(cat_rows(jnp.where(row < PLEN + PATCHES, m24[:, cols], 0.0))):
            mcat[32 * i : 32 * i + 32, cols] = part


def scale_kernel(q, ecat, m24, rstd, mcat):
    spread_rows(m24, mcat)
    for p in range(0, PATCHES, 2):
        square = jnp.zeros((2 * WIN, 128), F32)
        for k in range(4):
            dev = dot(q[p : p + 2].reshape(2 * WIN, KCAT), ecat[k])
            for c in range(SHARD // 128):
                piece = dev[:, 128 * c : 128 * c + 128]
                square = square + piece * piece
        var = jnp.sum(square, axis=1, keepdims=True) * (1.0 / D)
        rstd[p : p + 2] = jnp.broadcast_to(lax.rsqrt(var + 1e-05), (2 * WIN, 128)).reshape(2, WIN, 128)


def gelu(h):
    c = math.sqrt(2.0 / math.pi)
    half = 0.5 * h
    return half + half * jnp.tanh(h * (c + (c * 0.044715) * (h * h)))


def away_body(group, q, rstd, mcats, downs, act, send):
    rows = (group[1] - group[0]) * WIN
    x = q[group[0] : group[1]].reshape(rows, KCAT)
    scale = rstd[group[0] : group[1]].reshape(rows, 128)[:, :1]
    downs = (downs[0][:, shard_cols(lax.axis_index("tensor") ^ 2)], downs[1][...])
    for side in range(2):
        for j in range(HIDDEN // 512):
            cols = slice(512 * j, 512 * j + 512)
            at = slice(HIDDEN * side + 512 * j, HIDDEN * side + 512 * (j + 1))
            act[:, at] = gelu(dot(x, mcats[side][:, cols]) * scale).astype(BF)
    send[...] = (dot(act[:, :HIDDEN], downs[0]) + dot(act[:, HIDDEN:], downs[1])).astype(BF)


def first_away_kernel(q, rstd, m_own, m24_peer, down, d_peer, m_peer, act, send, give_y, sem):
    load = pltpu.make_async_copy(down.at[:, shard_cols(lax.axis_index("tensor") ^ 1)], give_y, sem)
    load.start()
    spread_rows(m24_peer, m_peer)
    away_body(GROUPS[0], q, rstd, (m_own, m_peer), (down, d_peer), act, send)
    load.wait()


def away_kernel(group, q, rstd, m_own, m_peer, down, d_peer, act, send):
    away_body(group, q, rstd, (m_own, m_peer), (down, d_peer), act, send)


def add_stats(table, p, x):
    lane = lax.broadcasted_iota(jnp.int32, (WIN, WIN), 1)
    mean = jnp.sum(x, axis=1, keepdims=True) * (1.0 / SHARD)
    off = x - mean
    square = jnp.sum(off * off, axis=1, keepdims=True)
    return jnp.where(lane == p, mean, jnp.where(lane == PATCHES + p, square, table))


def home_rows(group, q, ecat, down, d_peer, act):
    own = down[:, shard_cols(lax.axis_index("tensor"))]
    x = dot(act[:, :HIDDEN], own) + dot(act[:, HIDDEN:], d_peer[...])
    return x + dot(q[group[0] : group[1]].reshape((group[1] - group[0]) * WIN, KCAT), ecat[0])


def home_kernel(q, ecat, d_own, d_peer, a0, a1, part):
    for group, act in zip(GROUPS[:2], (a0, a1)):
        part[WIN * group[0] : WIN * group[1], :] = home_rows(group, q, ecat, d_own, d_peer, act)


def weights(info, counts, members, own):
    slot = lax.axis_index("member")
    share = 1.0 / (1.0 + counts)
    member = lax.broadcasted_iota(jnp.int32, (members, WIN), 0)
    lane = lax.broadcasted_iota(jnp.int32, (1, WIN), 1)
    factor = info[1:2, :] / jnp.sum(share, axis=0, keepdims=True)
    if members > 4:
        factor = jnp.where((((lane // own) ^ slot) >> 2) & 1 == 0, factor, 0.0)
    rows = [jnp.sum(jnp.where(member == slot ^ k, share, 0.0), axis=0, keepdims=True) * factor for k in (0, 4)]
    row = lax.broadcasted_iota(jnp.int32, (8, WIN), 0)
    return jnp.where(row == 0, rows[0], jnp.where(row == 1, rows[1], 0.0))


def state_kernel(
    members, own, q, ecat, d_own, d_peer, a2, a3, part, c0, c1, c2, info, mine, late, state, last, stats, shares
):
    shares[...] = weights(info, mine[...] + late[...], members, own)
    last[...] = home_rows(GROUPS[3], q, ecat, d_own, d_peer, a3)
    table = jnp.zeros((WIN, WIN), F32)
    for g, cross in enumerate((c0, c1, c2)):
        group = GROUPS[g]
        rows = slice(WIN * group[0], WIN * group[1])
        x = part[rows, :] if g < 2 else home_rows(group, q, ecat, d_own, d_peer, a2)
        x = x + cross[...].astype(F32)
        state[rows, :] = x
        for i, p in enumerate(range(*group)):
            table = add_stats(table, p, x[i * WIN : (i + 1) * WIN])
    stats[...] = table.T[: 2 * PATCHES]


def last_state_kernel(last, cross, prev, state, stats):
    x = last[...] + cross[...].astype(F32)
    state[...] = x
    table = jnp.zeros((WIN, WIN), F32)
    for i, p in enumerate(range(*GROUPS[3])):
        table = add_stats(table, p, x[i * WIN : (i + 1) * WIN])
    stats[...] = prev[...] + table.T[: 2 * PATCHES]


def head_kernel(stats, state, last, heads, shard, shares, send, keep, scr):
    core = lax.axis_index("tensor") & 1
    first = GROUPS[3][0]
    scale = lax.rsqrt(stats[PATCHES:, :] * (1.0 / D) + 1e-05)
    table = jnp.concatenate([stats[:PATCHES, :], scale, jnp.zeros((WIN - 2 * PATCHES, WIN), F32)], axis=0).T
    total = jnp.zeros((WIN, HORIZONS), F32)
    for p in range(PATCHES):
        x = state[p * WIN : (p + 1) * WIN, :] if p < first else last[(p - first) * WIN : (p - first + 1) * WIN, :]
        y = (x - table[:, p : p + 1]) * table[:, PATCHES + p : PATCHES + p + 1] * shard[25:26, :]
        total = total + lax.dot_general(
            y.astype(BF), heads[p], (((1,), (1,)), ((), ())), preferred_element_type=F32
        )
    scr[:, :HORIZONS] = total
    scr[:, HORIZONS:] = jnp.zeros((WIN, WIN - HORIZONS), F32)
    scr[...] = scr[...].T
    for c in range(2):
        for out, side in ((keep, core), (send, 1 - core)):
            out[24 * c : 24 * c + 24, :] = scr[pl.ds(pl.multiple_of(48 * c + 24 * side, 8), 24), :]
    keep[48:, :] = 0.5 * shares[...]
    send[48:, :] = jnp.zeros((8, WIN), F32)


def weigh_kernel(mine, theirs, out):
    at = pl.ds(pl.multiple_of(24 * (lax.axis_index("tensor") >> 1), 8), 24)
    here = mine[48:49, :] + theirs[49:50, :]
    there = mine[49:50, :] + theirs[48:49, :]
    out[...] = mine[at, :] * here + theirs[at, :] * there


def rank_kernel(levels, own, total, info, target, average, levels_out, scr, res, ranks):
    t = lax.axis_index("tensor")
    slot = lax.axis_index("member")
    per = total.shape[0]
    pred = total[...] + info[0:1, :]
    wanted = target[pl.ds(pl.multiple_of(24 * t, 8), per), :]
    resid = jnp.abs(wanted - pred)
    scr[...] = jnp.zeros((WIN, WIN), F32)
    scr[:per, :] = pred
    scr[...] = scr[...].T
    if own % 8 == 0:
        average[...] = scr[pl.ds(pl.multiple_of(own * slot, 8), own), :per]
    else:
        at = own * slot
        rows = scr[pl.ds(pl.multiple_of((at // 8) * 8, 8), 8), :per]
        pick = rows[:own]
        for s in range(1, 8 // own):
            pick = jnp.where(at % 8 == s * own, rows[s * own : (s + 1) * own], pick)
        average[...] = pick
    res[...] = jnp.zeros((WIN, WIN), F32)
    res[:per, :] = resid
    across = res[...].T
    j = lax.broadcasted_iota(jnp.int32, (WIN, WIN), 0)
    i = lax.broadcasted_iota(jnp.int32, (WIN, WIN), 1)
    earlier = j < i
    for h in range(per):
        row, col = resid[h : h + 1, :], across[:, h : h + 1]
        before = (col < row) | ((col == row) & earlier)
        ranks[h : h + 1, :] = jnp.sum(before.astype(F32), axis=0, keepdims=True)
    order = ranks[...]
    lane = lax.broadcasted_iota(jnp.int32, (per, WIN), 1)
    table = jnp.zeros((per, WIN), F32)
    for n, level in enumerate(levels):
        value = jnp.sum(jnp.where(order == float(level), resid, 0.0), axis=1, keepdims=True)
        table = jnp.where(lane == n, value, table)
    res[:per, :] = table
    levels_out[...] = res[...].T[: len(levels), :per]


def per_device(series, starts, counts, lifting, location, gain_one, up, down, gain_two, readout):
    members = lax.axis_size("member")
    own = counts.shape[1]
    sds = jax.ShapeDtypeStruct

    def over_tensor(x, k):
        return lax.ppermute(x, "tensor", [(i, i ^ k) for i in range(4)])

    def over_member(x, k):
        return lax.ppermute(x, "member", [(i, i ^ k) for i in range(members)])

    shard_bf = pltpu.VMEM((D, SHARD), BF)
    packed, every, give_x = call(
        pack_kernel,
        (pltpu.VMEM((32, SHARD), F32), pltpu.VMEM((members, WIN), F32), shard_bf),
        [HBM] * 6,
        (lifting, location, gain_one, gain_two, counts.T, down),
        2 * US,
        1000,
        [
            pltpu.VMEM((1, SHARD), F32),
            pltpu.VMEM((1, SHARD), F32),
            pltpu.VMEM((own, members), jnp.int32),
            pltpu.VMEM((WIN, WIN), F32),
            pltpu.SemaphoreType.DMA((6,)),
        ],
    )
    shards = [packed] + [over_tensor(packed, k) for k in (1, 2, 3)]
    peer_x = over_tensor(give_x, 1)

    heads = jnp.swapaxes(readout[0], 1, 2)
    up = up[0]
    q, info, target = call(
        windows_kernel,
        (pltpu.VMEM((PATCHES, WIN, KCAT), BF), pltpu.VMEM((8, WIN), F32), pltpu.VMEM((WIN, WIN), F32)),
        [V] * 2,
        (series.reshape(WIN, WIN), starts.reshape(1, WIN)),
        5 * US,
        1000,
        after=(packed,),
    )

    hops = [k for k in (1, 3, 8, 24) if k < members]
    steps = iter(hops)

    def hop(value, after=None):
        k = next(steps, None)
        if after is not None:
            value = lax.optimization_barrier((value, after))[0]
        return value if k is None else value + over_member(value, k)

    def hop_parts(value, after=None):
        k = next(steps, None)
        if after is not None:
            value = lax.optimization_barrier((value, after))[0]
        return value, jnp.zeros_like(value) if k is None else over_member(value, k)

    every, late = hop_parts(every)
    m24, ecat, every = call(
        lift_kernel,
        (pltpu.VMEM((32, HIDDEN), F32), pltpu.VMEM((4, KCAT, SHARD), BF), pltpu.VMEM((members, WIN), F32)),
        [V] * 7,
        (up, *shards, every, late),
        3 * US,
        1000,
        [pltpu.VMEM((4, 96, SHARD), BF)],
        after=(info,),
    )
    m24_peer = over_tensor(m24, 1)
    mcat_shape = pltpu.VMEM((KCAT, HIDDEN), BF)
    rstd, m_own = call(
        scale_kernel,
        (pltpu.VMEM((PATCHES, WIN, 128), F32), mcat_shape),
        [V] * 3,
        (q, ecat, m24),
        2 * US,
        1000,
    )

    def sums(group):
        rows = (group[1] - group[0]) * WIN
        return pltpu.VMEM((rows, 2 * HIDDEN), BF), pltpu.VMEM((rows, SHARD), BF)

    m_peer, act, send, give_y = call(
        first_away_kernel,
        (mcat_shape, *sums(GROUPS[0]), shard_bf),
        [V] * 6,
        (q, rstd, m_own, m24_peer, down[0], peer_x),
        4 * US,
        1000,
        [pltpu.SemaphoreType.DMA],
    )
    acts, crossed = [act], [over_tensor(send, 2)]
    fed = (q, rstd, m_own, m_peer, down[0], peer_x)
    peer_y = over_tensor(lax.optimization_barrier((give_y, send))[0], 1)
    for g in range(1, 4):
        act, send = call(
            functools.partial(away_kernel, GROUPS[g]),
            sums(GROUPS[g]),
            [V] * 6,
            fed,
            4 * US,
            1000,
            after=(every, crossed[g - 2]) if g > 1 else (),
        )
        acts.append(act)
        crossed.append(over_tensor(send, 2))
        if g < 3:
            every = hop(every, send)
    every, late = hop_parts(every, send)
    homes = (q, ecat, down[0], peer_y)
    (part,) = call(
        home_kernel,
        (pltpu.VMEM((GROUPS[1][1] * WIN, SHARD), F32),),
        [V] * 6,
        (*homes, *acts[:2]),
        US // 10,
        1000,
        after=(send,),
    )
    tail = (GROUPS[3][1] - GROUPS[3][0]) * WIN
    state, last, stats, shares = call(
        functools.partial(state_kernel, members, own),
        (
            pltpu.VMEM((GROUPS[2][1] * WIN, SHARD), F32),
            pltpu.VMEM((tail, SHARD), F32),
            pltpu.VMEM((2 * PATCHES, WIN), F32),
            pltpu.VMEM((8, WIN), F32),
        ),
        [V] * 13,
        (*homes, *acts[2:], part, *crossed[:3], info, every, late),
        5 * US,
        1000,
    )
    last, stats = call(
        last_state_kernel,
        (pltpu.VMEM((tail, SHARD), F32), pltpu.VMEM((2 * PATCHES, WIN), F32)),
        [V] * 3,
        (last, crossed[3], stats),
        US,
        1000,
    )
    features = SHARD
    for k in (1, 2):
        other = over_tensor(stats, k)
        gap = stats[:PATCHES] - other[:PATCHES]
        square = stats[PATCHES:] + other[PATCHES:] + (0.5 * features) * (gap * gap)
        stats = jnp.concatenate([0.5 * (stats[:PATCHES] + other[:PATCHES]), square], axis=0)
        features *= 2
    sent, held = call(
        head_kernel,
        (pltpu.VMEM((56, WIN), F32),) * 2,
        [V] * 6,
        (stats, state, last, heads, packed, shares),
        US,
        1000,
        [pltpu.VMEM((WIN, WIN), F32)],
    )
    total = held + over_tensor(sent, 1)
    total = total + over_tensor(total, 2)
    if members > 4:
        pairs = [(4 * m + t, 4 * (m ^ 4) + (t ^ 2)) for m in range(members) for t in range(4)]
        met = lax.ppermute(total, ("member", "tensor"), pairs)
    else:
        met = jnp.zeros_like(total)
    (total,) = call(weigh_kernel, (pltpu.VMEM((24, WIN), F32),), [V] * 2, (total, met), US, 1000)
    for ring in ((1, 2, 3), (8, 16, 24)):
        if ring[-1] < members:
            got = [over_member(total, k) for k in ring]
            total = total + got[0] + got[1] + got[2]

    levels = tuple(WIN * n // 100 for n in (50, 80, 90, 95))
    return call(
        functools.partial(rank_kernel, levels, own),
        (sds((own, 24), F32), sds((4, 24), F32)),
        [V] * 3,
        (total, info, target),
        US,
        1000,
        [pltpu.VMEM((WIN, WIN), F32), pltpu.VMEM((WIN, WIN), F32), pltpu.VMEM((24, WIN), F32)],
    )


def solution(mesh):
    placed = (
        P(),
        P(),
        P(None, "member"),
        P("member", None, "tensor"),
        P("member", None, "tensor"),
        P("member", "tensor"),
        P("member", None, "tensor"),
        P("member", "tensor", None),
        P("member", "tensor"),
        P("member", None, "tensor", None),
    )
    return jax.shard_map(
        per_device,
        mesh=mesh,
        in_specs=placed,
        out_specs=(P("member", "tensor"), P(None, "tensor")),
        check_vma=False,
    )
```

```python
import functools
import math

import jax
import jax.numpy as jnp
from jax import lax
from jax.experimental import pallas as pl
from jax.experimental.pallas import tpu as pltpu
from jax.sharding import PartitionSpec as P

BF, F32 = jnp.bfloat16, jnp.float32
PATCHES, PLEN, STRIDE, LOOK = 8, 16, 8, 72
WIN, D, SHARD, HIDDEN, HORIZONS = 128, 2048, 512, 2048, 96
KCAT = 256
MIB = 1 << 20
US = 10**9
GROUPS = ((0, 2), (2, 4), (4, 6), (6, 8))


def split3(x):
    a = x.astype(BF)
    rest = x - a.astype(F32)
    b = rest.astype(BF)
    c = (rest - b.astype(F32)).astype(BF)
    return a, b, c


def dot(a, b):
    return jnp.dot(a, b, preferred_element_type=F32)


def roll_left(x, by):
    lanes = x.shape[1]
    by = by % lanes
    return x if by == 0 else pltpu.roll(x, lanes - by, 1)


def shard_cols(t):
    return pl.ds(pl.multiple_of(SHARD * t, SHARD), SHARD)


def call(body, out_shape, in_specs, args, flops, nbytes, scratch=(), limit=24 * MIB, after=()):
    taken, held = len(in_specs), len(after)

    def run(*refs):
        body(*refs[:taken], *refs[taken + held :])

    args = tuple(
        pltpu.with_memory_space_constraint(x, pltpu.HBM if spec is HBM else pltpu.VMEM)
        for x, spec in zip(args, in_specs)
    ) + tuple(after)
    in_specs = list(in_specs) + [ANY] * held
    return pl.pallas_call(
        run,
        out_shape=out_shape,
        in_specs=in_specs,
        out_specs=jax.tree.map(lambda _: pl.BlockSpec(memory_space=pltpu.VMEM), out_shape),
        scratch_shapes=list(scratch),
        compiler_params=pltpu.CompilerParams(vmem_limit_bytes=limit),
        cost_estimate=pl.CostEstimate(flops=flops, bytes_accessed=nbytes, transcendentals=0),
    )(*args)


V = pl.BlockSpec(memory_space=pltpu.VMEM)
ANY = pl.BlockSpec(memory_space=pl.ANY)
HBM = pl.BlockSpec(memory_space=pltpu.HBM)


def pack_kernel(lifting, location, gain_one, gain_two, counts_h, down, packed, every, give, g1, g2, counts, scr, sem):
    t = lax.axis_index("tensor")
    loads = [
        pltpu.make_async_copy(lifting.at[0], packed.at[0:PLEN, :], sem.at[0]),
        pltpu.make_async_copy(location.at[0], packed.at[PLEN : PLEN + PATCHES, :], sem.at[1]),
        pltpu.make_async_copy(gain_one, g1, sem.at[2]),
        pltpu.make_async_copy(gain_two, g2, sem.at[3]),
        pltpu.make_async_copy(counts_h, counts, sem.at[4]),
        pltpu.make_async_copy(down.at[0, :, shard_cols(t ^ 3)], give, sem.at[5]),
    ]
    for load in loads:
        load.start()
    own, members = counts.shape
    scr[...] = jnp.zeros((WIN, WIN), F32)
    for load in loads[:5]:
        load.wait()
    row = lax.broadcasted_iota(jnp.int32, (8, SHARD), 0)
    packed[PLEN + PATCHES :, :] = jnp.where(row == 0, g1[...], jnp.where(row == 1, g2[...], 0.0))
    scr[:own, :members] = counts[...].astype(F32)
    columns = scr[...].T[:members]
    at = own * lax.axis_index("member")
    place = lax.broadcasted_iota(jnp.int32, (members, WIN), 1) - at
    placed = jnp.zeros((members, WIN), F32)
    for j in range(own):
        placed = jnp.where(place == j, columns[:, j : j + 1], placed)
    every[...] = placed
    loads[5].wait()


def lift_parts(t, shards, up, lhs):
    for n, (k, shard) in enumerate(shards):
        gain = shard[PLEN + PATCHES : PLEN + PATCHES + 1, :]
        row = lax.broadcasted_iota(jnp.int32, (32, SHARD), 0)
        rows = jnp.where(row < PLEN + PATCHES, shard[...] * gain, jnp.where(row == PLEN + PATCHES, gain, 0.0))
        for i, part in enumerate(split3(rows)):
            lhs[n, 32 * i : 32 * i + 32, :] = part
    for j in range(HIDDEN // 512):
        cols = slice(512 * j, 512 * j + 512)
        m = sum(dot(lhs[n], up[shard_cols(t ^ k), cols]) for n, (k, _) in enumerate(shards))
        yield cols, m[:32] + m[32:64] + m[64:96]


def windows_kernel(series_h, starts_h, down, give_y, q, info, target, series, starts, sem):
    t = lax.axis_index("tensor")
    small = [
        pltpu.make_async_copy(series_h, series, sem.at[0]),
        pltpu.make_async_copy(starts_h, starts, sem.at[1]),
    ]
    loads = [pltpu.make_async_copy(down.at[0, :, shard_cols(t ^ 1)], give_y, sem.at[2])]
    for load in small + loads:
        load.start()
    for load in small:
        load.wait()
    lane = lax.broadcasted_iota(jnp.int32, (WIN, WIN), 1)
    first = jnp.broadcast_to(starts[...].astype(F32), (WIN, WIN)).T.astype(jnp.int32)
    row, offset = first >> 7, first & 127
    picks = [(row + k == lane).astype(F32).astype(BF) for k in range(3)]
    parts = split3(series[...])
    rows = [sum(dot(pick, part) for part in parts) for pick in picks]
    x = jnp.concatenate(rows, axis=1)
    offset = jnp.concatenate([offset] * 3, axis=1)
    for bit in range(7):
        x = jnp.where((offset >> bit) & 1 == 1, roll_left(x, 1 << bit), x)
    target[...] = roll_left(x, LOOK)[:, :WIN].T
    look = x[:, :WIN]
    center = jnp.sum(jnp.where(lane < LOOK, look, 0.0), axis=1, keepdims=True) * (1.0 / LOOK)
    dev = jnp.where(lane < LOOK, look - center, 0.0)
    spread = jnp.sqrt(jnp.sum(dev * dev, axis=1, keepdims=True) * (1.0 / LOOK) + 1e-05)
    normed = dev / spread
    pair = jnp.where(lane == 0, center, jnp.where(lane == 1, spread, 0.0)).T
    info[...] = pair[:8]
    block = lane // 32
    for p in range(PATCHES):
        one = jnp.where(lane < PLEN, roll_left(normed, STRIDE * p), 0.0)
        one = jnp.where(lane == PLEN + p, 1.0, one)
        two = one + pltpu.roll(one, 32, 1)
        four = two + pltpu.roll(two, 64, 1)
        a, b, c = (v.astype(F32) for v in split3(four))
        q[p, :, :WIN] = jnp.where(block < 2, a, b).astype(BF)
        q[p, :, WIN:] = jnp.where(block == 0, a, jnp.where(block == 1, c, 0.0)).astype(BF)
    for load in loads:
        load.wait()


def cat_rows(x):
    b1, b2, b3 = split3(x)
    zero = jnp.zeros_like(b1)
    return [b1, b2, b1, b2, b3, b1, zero, zero]


def lift_kernel(up, s0, s1, s2, s3, mine, late, m24, ecat, every, lhs):
    t = lax.axis_index("tensor")
    every[...] = mine[...] + late[...]
    shards = (s0, s1, s2, s3)
    mean = sum(jnp.sum(s[...], axis=1, keepdims=True) for s in shards) * (1.0 / D)
    keep = lax.broadcasted_iota(jnp.int32, (32, SHARD), 0) < PLEN + PATCHES
    for cols, m in lift_parts(t, tuple(enumerate(shards)), up, lhs):
        m24[:, cols] = m - mean * m[PLEN + PATCHES : PLEN + PATCHES + 1, :]
    for k, shard in enumerate(shards):
        centred = jnp.where(keep, shard[...] - mean, 0.0)
        for i, part in enumerate(cat_rows(centred)):
            ecat[k, 32 * i : 32 * i + 32, :] = part


def spread_rows(m24, mcat):
    for j in range(HIDDEN // 512):
        cols = slice(512 * j, 512 * j + 512)
        row = lax.broadcasted_iota(jnp.int32, (32, 512), 0)
        for i, part in enumerate(cat_rows(jnp.where(row < PLEN + PATCHES, m24[:, cols], 0.0))):
            mcat[32 * i : 32 * i + 32, cols] = part


def scale_kernel(q, ecat, m24, rstd, mcat):
    spread_rows(m24, mcat)
    for p in range(0, PATCHES, 2):
        square = jnp.zeros((2 * WIN, 128), F32)
        for k in range(4):
            dev = dot(q[p : p + 2].reshape(2 * WIN, KCAT), ecat[k])
            for c in range(SHARD // 128):
                piece = dev[:, 128 * c : 128 * c + 128]
                square = square + piece * piece
        var = jnp.sum(square, axis=1, keepdims=True) * (1.0 / D)
        rstd[p : p + 2] = jnp.broadcast_to(lax.rsqrt(var + 1e-05), (2 * WIN, 128)).reshape(2, WIN, 128)


def gelu(h):
    c = math.sqrt(2.0 / math.pi)
    half = 0.5 * h
    return half + half * jnp.tanh(h * (c + (c * 0.044715) * (h * h)))


def away_body(group, q, rstd, mcats, downs, act, send):
    rows = (group[1] - group[0]) * WIN
    x = q[group[0] : group[1]].reshape(rows, KCAT)
    scale = rstd[group[0] : group[1]].reshape(rows, 128)[:, :1]
    downs = (downs[0][:, shard_cols(lax.axis_index("tensor") ^ 2)], downs[1][...])
    for side in range(2):
        for j in range(HIDDEN // 512):
            cols = slice(512 * j, 512 * j + 512)
            at = slice(HIDDEN * side + 512 * j, HIDDEN * side + 512 * (j + 1))
            act[:, at] = gelu(dot(x, mcats[side][:, cols]) * scale).astype(BF)
    send[...] = (dot(act[:, :HIDDEN], downs[0]) + dot(act[:, HIDDEN:], downs[1])).astype(BF)


def first_away_kernel(q, rstd, m_own, m24_peer, down, d_peer, m_peer, act, send):
    spread_rows(m24_peer, m_peer)
    away_body(GROUPS[0], q, rstd, (m_own, m_peer), (down, d_peer), act, send)


def away_kernel(group, q, rstd, m_own, m_peer, down, d_peer, act, send):
    away_body(group, q, rstd, (m_own, m_peer), (down, d_peer), act, send)


def counting_kernel(group, q, rstd, m_own, m_peer, down, d_peer, mine, late, act, send, every):
    every[...] = mine[...] + late[...]
    away_body(group, q, rstd, (m_own, m_peer), (down, d_peer), act, send)


def add_stats(table, p, x):
    lane = lax.broadcasted_iota(jnp.int32, (WIN, WIN), 1)
    mean = jnp.sum(x, axis=1, keepdims=True) * (1.0 / SHARD)
    off = x - mean
    square = jnp.sum(off * off, axis=1, keepdims=True)
    return jnp.where(lane == p, mean, jnp.where(lane == PATCHES + p, square, table))


def home_rows(group, q, ecat, down, d_peer, act):
    own = down[:, shard_cols(lax.axis_index("tensor"))]
    x = dot(act[:, :HIDDEN], own) + dot(act[:, HIDDEN:], d_peer[...])
    return x + dot(q[group[0] : group[1]].reshape((group[1] - group[0]) * WIN, KCAT), ecat[0])


def home_kernel(q, ecat, d_own, d_peer, a0, a1, part):
    for group, act in zip(GROUPS[:2], (a0, a1)):
        part[WIN * group[0] : WIN * group[1], :] = home_rows(group, q, ecat, d_own, d_peer, act)


def weights(info, counts, members, own):
    slot = lax.axis_index("member")
    share = 1.0 / (1.0 + counts)
    member = lax.broadcasted_iota(jnp.int32, (members, WIN), 0)
    lane = lax.broadcasted_iota(jnp.int32, (1, WIN), 1)
    factor = info[1:2, :] / jnp.sum(share, axis=0, keepdims=True)
    if members > 4:
        factor = jnp.where((((lane // own) ^ slot) >> 2) & 1 == 0, factor, 0.0)
    rows = [jnp.sum(jnp.where(member == slot ^ k, share, 0.0), axis=0, keepdims=True) * factor for k in (0, 4)]
    row = lax.broadcasted_iota(jnp.int32, (8, WIN), 0)
    return jnp.where(row == 0, rows[0], jnp.where(row == 1, rows[1], 0.0))


def state_kernel(
    members, own, q, ecat, d_own, d_peer, a2, a3, part, c0, c1, c2, info, mine, late, state, last, stats, shares
):
    shares[...] = weights(info, mine[...] + late[...], members, own)
    last[...] = home_rows(GROUPS[3], q, ecat, d_own, d_peer, a3)
    table = jnp.zeros((WIN, WIN), F32)
    for g, cross in enumerate((c0, c1, c2)):
        group = GROUPS[g]
        rows = slice(WIN * group[0], WIN * group[1])
        x = part[rows, :] if g < 2 else home_rows(group, q, ecat, d_own, d_peer, a2)
        x = x + cross[...].astype(F32)
        state[rows, :] = x
        for i, p in enumerate(range(*group)):
            table = add_stats(table, p, x[i * WIN : (i + 1) * WIN])
    stats[...] = table.T[: 2 * PATCHES]


def last_state_kernel(last, cross, prev, state, stats):
    x = last[...] + cross[...].astype(F32)
    state[...] = x
    table = jnp.zeros((WIN, WIN), F32)
    for i, p in enumerate(range(*GROUPS[3])):
        table = add_stats(table, p, x[i * WIN : (i + 1) * WIN])
    stats[...] = prev[...] + table.T[: 2 * PATCHES]


def head_kernel(stats, state, last, heads, shard, shares, send, keep, scr):
    core = lax.axis_index("tensor") & 1
    first = GROUPS[3][0]
    scale = lax.rsqrt(stats[PATCHES:, :] * (1.0 / D) + 1e-05)
    table = jnp.concatenate([stats[:PATCHES, :], scale, jnp.zeros((WIN - 2 * PATCHES, WIN), F32)], axis=0).T
    total = jnp.zeros((WIN, HORIZONS), F32)
    for p in range(PATCHES):
        x = state[p * WIN : (p + 1) * WIN, :] if p < first else last[(p - first) * WIN : (p - first + 1) * WIN, :]
        y = (x - table[:, p : p + 1]) * table[:, PATCHES + p : PATCHES + p + 1] * shard[25:26, :]
        total = total + lax.dot_general(
            y.astype(BF), heads[p], (((1,), (1,)), ((), ())), preferred_element_type=F32
        )
    scr[:, :HORIZONS] = total
    scr[:, HORIZONS:] = jnp.zeros((WIN, WIN - HORIZONS), F32)
    scr[...] = scr[...].T
    for c in range(2):
        for out, side in ((keep, core), (send, 1 - core)):
            out[24 * c : 24 * c + 24, :] = scr[pl.ds(pl.multiple_of(48 * c + 24 * side, 8), 24), :]
    keep[48:, :] = 0.5 * shares[...]
    send[48:, :] = jnp.zeros((8, WIN), F32)


def weigh_kernel(mine, theirs, out):
    at = pl.ds(pl.multiple_of(24 * (lax.axis_index("tensor") >> 1), 8), 24)
    here = mine[48:49, :] + theirs[49:50, :]
    there = mine[49:50, :] + theirs[48:49, :]
    out[...] = mine[at, :] * here + theirs[at, :] * there


def rank_kernel(levels, own, total, info, target, average, levels_out, scr, res, ranks):
    t = lax.axis_index("tensor")
    slot = lax.axis_index("member")
    per = total.shape[0]
    pred = total[...] + info[0:1, :]
    wanted = target[pl.ds(pl.multiple_of(24 * t, 8), per), :]
    resid = jnp.abs(wanted - pred)
    scr[...] = jnp.zeros((WIN, WIN), F32)
    scr[:per, :] = pred
    scr[...] = scr[...].T
    if own % 8 == 0:
        average[...] = scr[pl.ds(pl.multiple_of(own * slot, 8), own), :per]
    else:
        at = own * slot
        rows = scr[pl.ds(pl.multiple_of((at // 8) * 8, 8), 8), :per]
        pick = rows[:own]
        for s in range(1, 8 // own):
            pick = jnp.where(at % 8 == s * own, rows[s * own : (s + 1) * own], pick)
        average[...] = pick
    res[...] = jnp.zeros((WIN, WIN), F32)
    res[:per, :] = resid
    across = res[...].T
    j = lax.broadcasted_iota(jnp.int32, (WIN, WIN), 0)
    i = lax.broadcasted_iota(jnp.int32, (WIN, WIN), 1)
    earlier = j < i
    for h in range(per):
        row, col = resid[h : h + 1, :], across[:, h : h + 1]
        before = (col < row) | ((col == row) & earlier)
        ranks[h : h + 1, :] = jnp.sum(before.astype(F32), axis=0, keepdims=True)
    order = ranks[...]
    lane = lax.broadcasted_iota(jnp.int32, (per, WIN), 1)
    table = jnp.zeros((per, WIN), F32)
    for n, level in enumerate(levels):
        value = jnp.sum(jnp.where(order == float(level), resid, 0.0), axis=1, keepdims=True)
        table = jnp.where(lane == n, value, table)
    res[:per, :] = table
    levels_out[...] = res[...].T[: len(levels), :per]


def per_device(series, starts, counts, lifting, location, gain_one, up, down, gain_two, readout):
    members = lax.axis_size("member")
    own = counts.shape[1]
    sds = jax.ShapeDtypeStruct

    def over_tensor(x, k):
        return lax.ppermute(x, "tensor", [(i, i ^ k) for i in range(4)])

    def over_member(x, k):
        return lax.ppermute(x, "member", [(i, i ^ k) for i in range(members)])

    shard_bf = pltpu.VMEM((D, SHARD), BF)
    packed, every, give_x = call(
        pack_kernel,
        (pltpu.VMEM((32, SHARD), F32), pltpu.VMEM((members, WIN), F32), shard_bf),
        [HBM] * 6,
        (lifting, location, gain_one, gain_two, counts.T, down),
        2 * US,
        1000,
        [
            pltpu.VMEM((1, SHARD), F32),
            pltpu.VMEM((1, SHARD), F32),
            pltpu.VMEM((own, members), jnp.int32),
            pltpu.VMEM((WIN, WIN), F32),
            pltpu.SemaphoreType.DMA((6,)),
        ],
    )
    shards = [packed] + [over_tensor(packed, k) for k in (1, 2, 3)]
    peer_x = over_tensor(give_x, 1)

    heads = jnp.swapaxes(readout[0], 1, 2)
    up = up[0]
    give_y, q, info, target = call(
        windows_kernel,
        (
            shard_bf,
            pltpu.VMEM((PATCHES, WIN, KCAT), BF),
            pltpu.VMEM((8, WIN), F32),
            pltpu.VMEM((WIN, WIN), F32),
        ),
        [HBM] * 3,
        (series.reshape(WIN, WIN), starts.reshape(1, WIN), down),
        5 * US,
        1000,
        [pltpu.VMEM((WIN, WIN), F32), pltpu.VMEM((1, WIN), jnp.int32), pltpu.SemaphoreType.DMA((3,))],
        after=(packed,),
    )

    hops = [k for k in (1, 3, 8, 24) if k < members]
    steps = iter(hops)

    def hop(value, after=None):
        k = next(steps, None)
        if after is not None:
            value = lax.optimization_barrier((value, after))[0]
        return value if k is None else value + over_member(value, k)

    def hop_parts(value, after=None):
        k = next(steps, None)
        if after is not None:
            value = lax.optimization_barrier((value, after))[0]
        return value, jnp.zeros_like(value) if k is None else over_member(value, k)

    every, late = hop_parts(every)
    m24, ecat, every = call(
        lift_kernel,
        (pltpu.VMEM((32, HIDDEN), F32), pltpu.VMEM((4, KCAT, SHARD), BF), pltpu.VMEM((members, WIN), F32)),
        [V] * 7,
        (up, *shards, every, late),
        3 * US,
        1000,
        [pltpu.VMEM((4, 96, SHARD), BF)],
        after=(info,),
    )
    m24_peer = over_tensor(m24, 1)
    mcat_shape = pltpu.VMEM((KCAT, HIDDEN), BF)
    rstd, m_own = call(
        scale_kernel,
        (pltpu.VMEM((PATCHES, WIN, 128), F32), mcat_shape),
        [V] * 3,
        (q, ecat, m24),
        2 * US,
        1000,
    )

    def sums(group):
        rows = (group[1] - group[0]) * WIN
        return pltpu.VMEM((rows, 2 * HIDDEN), BF), pltpu.VMEM((rows, SHARD), BF)

    m_peer, act, send = call(
        first_away_kernel,
        (mcat_shape, *sums(GROUPS[0])),
        [V] * 6,
        (q, rstd, m_own, m24_peer, down[0], peer_x),
        4 * US,
        1000,
    )
    acts, crossed = [act], [over_tensor(send, 2)]
    fed = (q, rstd, m_own, m_peer, down[0], peer_x)
    peer_y = over_tensor(lax.optimization_barrier((give_y, send))[0], 1)
    for g in range(1, 4):
        last_one = g == 3
        out = call(
            functools.partial(counting_kernel if last_one else away_kernel, GROUPS[g]),
            sums(GROUPS[g]) + ((pltpu.VMEM((members, WIN), F32),) if last_one else ()),
            [V] * (8 if last_one else 6),
            fed + ((every, late) if last_one else ()),
            4 * US,
            1000,
            after=() if g == 1 else (crossed[1],) if last_one else (every, crossed[0]),
        )
        act, send = out[:2]
        acts.append(act)
        crossed.append(over_tensor(send, 2))
        if g == 1:
            every = hop(every, send)
            every, late = hop_parts(every)
    every = out[2]
    every, late = hop_parts(every, send)
    homes = (q, ecat, down[0], peer_y)
    (part,) = call(
        home_kernel,
        (pltpu.VMEM((GROUPS[1][1] * WIN, SHARD), F32),),
        [V] * 6,
        (*homes, *acts[:2]),
        US // 10,
        1000,
        after=(send,),
    )
    tail = (GROUPS[3][1] - GROUPS[3][0]) * WIN
    state, last, stats, shares = call(
        functools.partial(state_kernel, members, own),
        (
            pltpu.VMEM((GROUPS[2][1] * WIN, SHARD), F32),
            pltpu.VMEM((tail, SHARD), F32),
            pltpu.VMEM((2 * PATCHES, WIN), F32),
            pltpu.VMEM((8, WIN), F32),
        ),
        [V] * 13,
        (*homes, *acts[2:], part, *crossed[:3], info, every, late),
        5 * US,
        1000,
    )
    last, stats = call(
        last_state_kernel,
        (pltpu.VMEM((tail, SHARD), F32), pltpu.VMEM((2 * PATCHES, WIN), F32)),
        [V] * 3,
        (last, crossed[3], stats),
        US,
        1000,
    )
    features = SHARD
    for k in (1, 2):
        other = over_tensor(stats, k)
        gap = stats[:PATCHES] - other[:PATCHES]
        square = stats[PATCHES:] + other[PATCHES:] + (0.5 * features) * (gap * gap)
        stats = jnp.concatenate([0.5 * (stats[:PATCHES] + other[:PATCHES]), square], axis=0)
        features *= 2
    sent, held = call(
        head_kernel,
        (pltpu.VMEM((56, WIN), F32),) * 2,
        [V] * 6,
        (stats, state, last, heads, packed, shares),
        US,
        1000,
        [pltpu.VMEM((WIN, WIN), F32)],
    )
    total = held + over_tensor(sent, 1)
    total = total + over_tensor(total, 2)
    if members > 4:
        pairs = [(4 * m + t, 4 * (m ^ 4) + (t ^ 2)) for m in range(members) for t in range(4)]
        met = lax.ppermute(total, ("member", "tensor"), pairs)
    else:
        met = jnp.zeros_like(total)
    (total,) = call(weigh_kernel, (pltpu.VMEM((24, WIN), F32),), [V] * 2, (total, met), US, 1000)
    for ring in ((1, 2, 3), (8, 16, 24)):
        if ring[-1] < members:
            got = [over_member(total, k) for k in ring]
            total = total + got[0] + got[1] + got[2]

    levels = tuple(WIN * n // 100 for n in (50, 80, 90, 95))
    return call(
        functools.partial(rank_kernel, levels, own),
        (sds((own, 24), F32), sds((4, 24), F32)),
        [V] * 3,
        (total, info, target),
        US,
        1000,
        [pltpu.VMEM((WIN, WIN), F32), pltpu.VMEM((WIN, WIN), F32), pltpu.VMEM((24, WIN), F32)],
    )


def solution(mesh):
    placed = (
        P(),
        P(),
        P(None, "member"),
        P("member", None, "tensor"),
        P("member", None, "tensor"),
        P("member", "tensor"),
        P("member", None, "tensor"),
        P("member", "tensor", None),
        P("member", "tensor"),
        P("member", None, "tensor", None),
    )
    return jax.shard_map(
        per_device,
        mesh=mesh,
        in_specs=placed,
        out_specs=(P("member", "tensor"), P(None, "tensor")),
        check_vma=False,
    )
```

```python
import functools
import math

import jax
import jax.numpy as jnp
from jax import lax
from jax.experimental import pallas as pl
from jax.experimental.pallas import tpu as pltpu
from jax.sharding import PartitionSpec as P

BF, F32 = jnp.bfloat16, jnp.float32
PATCHES, PLEN, STRIDE, LOOK = 8, 16, 8, 72
WIN, D, SHARD, HIDDEN, HORIZONS = 128, 2048, 512, 2048, 96
KCAT = 256
MIB = 1 << 20
US = 10**9
GROUPS = ((0, 2), (2, 4), (4, 6), (6, 8))


def split3(x):
    a = x.astype(BF)
    rest = x - a.astype(F32)
    b = rest.astype(BF)
    c = (rest - b.astype(F32)).astype(BF)
    return a, b, c


def dot(a, b):
    return jnp.dot(a, b, preferred_element_type=F32)


def roll_left(x, by):
    lanes = x.shape[1]
    by = by % lanes
    return x if by == 0 else pltpu.roll(x, lanes - by, 1)


def shard_cols(t):
    return pl.ds(pl.multiple_of(SHARD * t, SHARD), SHARD)


def call(body, out_shape, in_specs, args, flops, nbytes, scratch=(), limit=24 * MIB, after=()):
    taken, held = len(in_specs), len(after)

    def run(*refs):
        body(*refs[:taken], *refs[taken + held :])

    args = tuple(
        pltpu.with_memory_space_constraint(x, pltpu.HBM if spec is HBM else pltpu.VMEM)
        for x, spec in zip(args, in_specs)
    ) + tuple(after)
    in_specs = list(in_specs) + [ANY] * held
    return pl.pallas_call(
        run,
        out_shape=out_shape,
        in_specs=in_specs,
        out_specs=jax.tree.map(lambda _: pl.BlockSpec(memory_space=pltpu.VMEM), out_shape),
        scratch_shapes=list(scratch),
        compiler_params=pltpu.CompilerParams(vmem_limit_bytes=limit),
        cost_estimate=pl.CostEstimate(flops=flops, bytes_accessed=nbytes, transcendentals=0),
    )(*args)


V = pl.BlockSpec(memory_space=pltpu.VMEM)
ANY = pl.BlockSpec(memory_space=pl.ANY)
HBM = pl.BlockSpec(memory_space=pltpu.HBM)


def pack_kernel(lifting, location, gain_one, gain_two, counts_h, down, packed, every, give, g1, g2, counts, scr, sem):
    t = lax.axis_index("tensor")
    loads = [
        pltpu.make_async_copy(lifting.at[0], packed.at[0:PLEN, :], sem.at[0]),
        pltpu.make_async_copy(location.at[0], packed.at[PLEN : PLEN + PATCHES, :], sem.at[1]),
        pltpu.make_async_copy(gain_one, g1, sem.at[2]),
        pltpu.make_async_copy(gain_two, g2, sem.at[3]),
        pltpu.make_async_copy(counts_h, counts, sem.at[4]),
        pltpu.make_async_copy(down.at[0, :, shard_cols(t ^ 3)], give, sem.at[5]),
    ]
    for load in loads:
        load.start()
    own, members = counts.shape
    scr[...] = jnp.zeros((WIN, WIN), F32)
    for load in loads[:5]:
        load.wait()
    row = lax.broadcasted_iota(jnp.int32, (8, SHARD), 0)
    packed[PLEN + PATCHES :, :] = jnp.where(row == 0, g1[...], jnp.where(row == 1, g2[...], 0.0))
    scr[:own, :members] = counts[...].astype(F32)
    columns = scr[...].T[:members]
    at = own * lax.axis_index("member")
    place = lax.broadcasted_iota(jnp.int32, (members, WIN), 1) - at
    placed = jnp.zeros((members, WIN), F32)
    for j in range(own):
        placed = jnp.where(place == j, columns[:, j : j + 1], placed)
    every[...] = placed
    loads[5].wait()


def lift_parts(t, shards, up, lhs):
    for n, (k, shard) in enumerate(shards):
        gain = shard[PLEN + PATCHES : PLEN + PATCHES + 1, :]
        row = lax.broadcasted_iota(jnp.int32, (32, SHARD), 0)
        rows = jnp.where(row < PLEN + PATCHES, shard[...] * gain, jnp.where(row == PLEN + PATCHES, gain, 0.0))
        for i, part in enumerate(split3(rows)):
            lhs[n, 32 * i : 32 * i + 32, :] = part
    for j in range(HIDDEN // 512):
        cols = slice(512 * j, 512 * j + 512)
        m = sum(dot(lhs[n], up[shard_cols(t ^ k), cols]) for n, (k, _) in enumerate(shards))
        yield cols, m[:32] + m[32:64] + m[64:96]


def windows_kernel(series, starts, q, info, target):
    lane = lax.broadcasted_iota(jnp.int32, (WIN, WIN), 1)
    first = jnp.broadcast_to(starts[...].astype(F32), (WIN, WIN)).T.astype(jnp.int32)
    row, offset = first >> 7, first & 127
    picks = [(row + k == lane).astype(F32).astype(BF) for k in range(3)]
    parts = split3(series[...])
    rows = [sum(dot(pick, part) for part in parts) for pick in picks]
    x = jnp.concatenate(rows, axis=1)
    offset = jnp.concatenate([offset] * 3, axis=1)
    for bit in range(7):
        x = jnp.where((offset >> bit) & 1 == 1, roll_left(x, 1 << bit), x)
    target[...] = roll_left(x, LOOK)[:, :WIN].T
    look = x[:, :WIN]
    center = jnp.sum(jnp.where(lane < LOOK, look, 0.0), axis=1, keepdims=True) * (1.0 / LOOK)
    dev = jnp.where(lane < LOOK, look - center, 0.0)
    spread = jnp.sqrt(jnp.sum(dev * dev, axis=1, keepdims=True) * (1.0 / LOOK) + 1e-05)
    normed = dev / spread
    pair = jnp.where(lane == 0, center, jnp.where(lane == 1, spread, 0.0)).T
    info[...] = pair[:8]
    block = lane // 32
    for p in range(PATCHES):
        one = jnp.where(lane < PLEN, roll_left(normed, STRIDE * p), 0.0)
        one = jnp.where(lane == PLEN + p, 1.0, one)
        two = one + pltpu.roll(one, 32, 1)
        four = two + pltpu.roll(two, 64, 1)
        a, b, c = (v.astype(F32) for v in split3(four))
        q[p, :, :WIN] = jnp.where(block < 2, a, b).astype(BF)
        q[p, :, WIN:] = jnp.where(block == 0, a, jnp.where(block == 1, c, 0.0)).astype(BF)


def cat_rows(x):
    b1, b2, b3 = split3(x)
    zero = jnp.zeros_like(b1)
    return [b1, b2, b1, b2, b3, b1, zero, zero]


def lift_kernel(up, s0, s1, s2, s3, mine, late, m24, ecat, every, lhs):
    t = lax.axis_index("tensor")
    every[...] = mine[...] + late[...]
    shards = (s0, s1, s2, s3)
    mean = sum(jnp.sum(s[...], axis=1, keepdims=True) for s in shards) * (1.0 / D)
    keep = lax.broadcasted_iota(jnp.int32, (32, SHARD), 0) < PLEN + PATCHES
    for cols, m in lift_parts(t, tuple(enumerate(shards)), up, lhs):
        m24[:, cols] = m - mean * m[PLEN + PATCHES : PLEN + PATCHES + 1, :]
    for k, shard in enumerate(shards):
        centred = jnp.where(keep, shard[...] - mean, 0.0)
        for i, part in enumerate(cat_rows(centred)):
            ecat[k, 32 * i : 32 * i + 32, :] = part


def spread_rows(m24, mcat):
    for j in range(HIDDEN // 512):
        cols = slice(512 * j, 512 * j + 512)
        row = lax.broadcasted_iota(jnp.int32, (32, 512), 0)
        for i, part in enumerate(cat_rows(jnp.where(row < PLEN + PATCHES, m24[:, cols], 0.0))):
            mcat[32 * i : 32 * i + 32, cols] = part


def scale_kernel(q, ecat, m24, rstd, mcat):
    spread_rows(m24, mcat)
    for p in range(0, PATCHES, 2):
        square = jnp.zeros((2 * WIN, 128), F32)
        for k in range(4):
            dev = dot(q[p : p + 2].reshape(2 * WIN, KCAT), ecat[k])
            for c in range(SHARD // 128):
                piece = dev[:, 128 * c : 128 * c + 128]
                square = square + piece * piece
        var = jnp.sum(square, axis=1, keepdims=True) * (1.0 / D)
        rstd[p : p + 2] = jnp.broadcast_to(lax.rsqrt(var + 1e-05), (2 * WIN, 128)).reshape(2, WIN, 128)


def gelu(h):
    c = math.sqrt(2.0 / math.pi)
    half = 0.5 * h
    return half + half * jnp.tanh(h * (c + (c * 0.044715) * (h * h)))


def away_body(group, q, rstd, mcats, downs, act, send):
    rows = (group[1] - group[0]) * WIN
    x = q[group[0] : group[1]].reshape(rows, KCAT)
    scale = rstd[group[0] : group[1]].reshape(rows, 128)[:, :1]
    downs = (downs[0][:, shard_cols(lax.axis_index("tensor") ^ 2)], downs[1][...])
    for side in range(2):
        for j in range(HIDDEN // 512):
            cols = slice(512 * j, 512 * j + 512)
            at = slice(HIDDEN * side + 512 * j, HIDDEN * side + 512 * (j + 1))
            act[:, at] = gelu(dot(x, mcats[side][:, cols]) * scale).astype(BF)
    send[...] = (dot(act[:, :HIDDEN], downs[0]) + dot(act[:, HIDDEN:], downs[1])).astype(BF)


def first_away_kernel(q, rstd, m_own, m24_peer, down, d_peer, m_peer, act, send, give_y, sem):
    load = pltpu.make_async_copy(down.at[:, shard_cols(lax.axis_index("tensor") ^ 1)], give_y, sem)
    load.start()
    spread_rows(m24_peer, m_peer)
    away_body(GROUPS[0], q, rstd, (m_own, m_peer), (down, d_peer), act, send)
    load.wait()


def away_kernel(group, q, rstd, m_own, m_peer, down, d_peer, act, send):
    away_body(group, q, rstd, (m_own, m_peer), (down, d_peer), act, send)


def counting_kernel(group, q, rstd, m_own, m_peer, down, d_peer, mine, late, act, send, every):
    every[...] = mine[...] + late[...]
    away_body(group, q, rstd, (m_own, m_peer), (down, d_peer), act, send)


def add_stats(table, p, x):
    lane = lax.broadcasted_iota(jnp.int32, (WIN, WIN), 1)
    mean = jnp.sum(x, axis=1, keepdims=True) * (1.0 / SHARD)
    off = x - mean
    square = jnp.sum(off * off, axis=1, keepdims=True)
    return jnp.where(lane == p, mean, jnp.where(lane == PATCHES + p, square, table))


def home_rows(group, q, ecat, down, d_peer, act):
    own = down[:, shard_cols(lax.axis_index("tensor"))]
    x = dot(act[:, :HIDDEN], own) + dot(act[:, HIDDEN:], d_peer[...])
    return x + dot(q[group[0] : group[1]].reshape((group[1] - group[0]) * WIN, KCAT), ecat[0])


def home_kernel(q, ecat, d_own, d_peer, a0, a1, part):
    for group, act in zip(GROUPS[:2], (a0, a1)):
        part[WIN * group[0] : WIN * group[1], :] = home_rows(group, q, ecat, d_own, d_peer, act)


def weights(info, counts, members, own):
    slot = lax.axis_index("member")
    share = 1.0 / (1.0 + counts)
    member = lax.broadcasted_iota(jnp.int32, (members, WIN), 0)
    lane = lax.broadcasted_iota(jnp.int32, (1, WIN), 1)
    factor = info[1:2, :] / jnp.sum(share, axis=0, keepdims=True)
    if members > 4:
        factor = jnp.where((((lane // own) ^ slot) >> 2) & 1 == 0, factor, 0.0)
    rows = [jnp.sum(jnp.where(member == slot ^ k, share, 0.0), axis=0, keepdims=True) * factor for k in (0, 4)]
    row = lax.broadcasted_iota(jnp.int32, (8, WIN), 0)
    return jnp.where(row == 0, rows[0], jnp.where(row == 1, rows[1], 0.0))


def state_kernel(
    members, own, q, ecat, d_own, d_peer, a2, a3, part, c0, c1, c2, info, mine, late, state, last, stats, shares
):
    shares[...] = weights(info, mine[...] + late[...], members, own)
    last[...] = home_rows(GROUPS[3], q, ecat, d_own, d_peer, a3)
    table = jnp.zeros((WIN, WIN), F32)
    for g, cross in enumerate((c0, c1, c2)):
        group = GROUPS[g]
        rows = slice(WIN * group[0], WIN * group[1])
        x = part[rows, :] if g < 2 else home_rows(group, q, ecat, d_own, d_peer, a2)
        x = x + cross[...].astype(F32)
        state[rows, :] = x
        for i, p in enumerate(range(*group)):
            table = add_stats(table, p, x[i * WIN : (i + 1) * WIN])
    stats[...] = table.T[: 2 * PATCHES]


def last_state_kernel(last, cross, prev, state, stats):
    x = last[...] + cross[...].astype(F32)
    state[...] = x
    table = jnp.zeros((WIN, WIN), F32)
    for i, p in enumerate(range(*GROUPS[3])):
        table = add_stats(table, p, x[i * WIN : (i + 1) * WIN])
    stats[...] = prev[...] + table.T[: 2 * PATCHES]


def head_kernel(stats, state, last, heads, shard, shares, send, keep, scr):
    core = lax.axis_index("tensor") & 1
    first = GROUPS[3][0]
    scale = lax.rsqrt(stats[PATCHES:, :] * (1.0 / D) + 1e-05)
    table = jnp.concatenate([stats[:PATCHES, :], scale, jnp.zeros((WIN - 2 * PATCHES, WIN), F32)], axis=0).T
    total = jnp.zeros((WIN, HORIZONS), F32)
    for p in range(PATCHES):
        x = state[p * WIN : (p + 1) * WIN, :] if p < first else last[(p - first) * WIN : (p - first + 1) * WIN, :]
        y = (x - table[:, p : p + 1]) * table[:, PATCHES + p : PATCHES + p + 1] * shard[25:26, :]
        total = total + lax.dot_general(
            y.astype(BF), heads[p], (((1,), (1,)), ((), ())), preferred_element_type=F32
        )
    scr[:, :HORIZONS] = total
    scr[:, HORIZONS:] = jnp.zeros((WIN, WIN - HORIZONS), F32)
    scr[...] = scr[...].T
    for c in range(2):
        for out, side in ((keep, core), (send, 1 - core)):
            out[24 * c : 24 * c + 24, :] = scr[pl.ds(pl.multiple_of(48 * c + 24 * side, 8), 24), :]
    keep[48:, :] = 0.5 * shares[...]
    send[48:, :] = jnp.zeros((8, WIN), F32)


def weigh_kernel(mine, theirs, out):
    at = pl.ds(pl.multiple_of(24 * (lax.axis_index("tensor") >> 1), 8), 24)
    here = mine[48:49, :] + theirs[49:50, :]
    there = mine[49:50, :] + theirs[48:49, :]
    out[...] = mine[at, :] * here + theirs[at, :] * there


def rank_kernel(levels, own, total, info, target, average, levels_out, scr, res, ranks):
    t = lax.axis_index("tensor")
    slot = lax.axis_index("member")
    per = total.shape[0]
    pred = total[...] + info[0:1, :]
    wanted = target[pl.ds(pl.multiple_of(24 * t, 8), per), :]
    resid = jnp.abs(wanted - pred)
    scr[...] = jnp.zeros((WIN, WIN), F32)
    scr[:per, :] = pred
    scr[...] = scr[...].T
    if own % 8 == 0:
        average[...] = scr[pl.ds(pl.multiple_of(own * slot, 8), own), :per]
    else:
        at = own * slot
        rows = scr[pl.ds(pl.multiple_of((at // 8) * 8, 8), 8), :per]
        pick = rows[:own]
        for s in range(1, 8 // own):
            pick = jnp.where(at % 8 == s * own, rows[s * own : (s + 1) * own], pick)
        average[...] = pick
    res[...] = jnp.zeros((WIN, WIN), F32)
    res[:per, :] = resid
    across = res[...].T
    j = lax.broadcasted_iota(jnp.int32, (WIN, WIN), 0)
    i = lax.broadcasted_iota(jnp.int32, (WIN, WIN), 1)
    earlier = j < i
    for h in range(per):
        row, col = resid[h : h + 1, :], across[:, h : h + 1]
        before = (col < row) | ((col == row) & earlier)
        ranks[h : h + 1, :] = jnp.sum(before.astype(F32), axis=0, keepdims=True)
    order = ranks[...]
    lane = lax.broadcasted_iota(jnp.int32, (per, WIN), 1)
    table = jnp.zeros((per, WIN), F32)
    for n, level in enumerate(levels):
        value = jnp.sum(jnp.where(order == float(level), resid, 0.0), axis=1, keepdims=True)
        table = jnp.where(lane == n, value, table)
    res[:per, :] = table
    levels_out[...] = res[...].T[: len(levels), :per]


def per_device(series, starts, counts, lifting, location, gain_one, up, down, gain_two, readout):
    members = lax.axis_size("member")
    own = counts.shape[1]
    sds = jax.ShapeDtypeStruct

    def over_tensor(x, k):
        return lax.ppermute(x, "tensor", [(i, i ^ k) for i in range(4)])

    def over_member(x, k):
        return lax.ppermute(x, "member", [(i, i ^ k) for i in range(members)])

    shard_bf = pltpu.VMEM((D, SHARD), BF)
    packed, every, give_x = call(
        pack_kernel,
        (pltpu.VMEM((32, SHARD), F32), pltpu.VMEM((members, WIN), F32), shard_bf),
        [HBM] * 6,
        (lifting, location, gain_one, gain_two, counts.T, down),
        2 * US,
        1000,
        [
            pltpu.VMEM((1, SHARD), F32),
            pltpu.VMEM((1, SHARD), F32),
            pltpu.VMEM((own, members), jnp.int32),
            pltpu.VMEM((WIN, WIN), F32),
            pltpu.SemaphoreType.DMA((6,)),
        ],
    )
    shards = [packed] + [over_tensor(packed, k) for k in (1, 2, 3)]
    peer_x = over_tensor(give_x, 1)

    heads = jnp.swapaxes(readout[0], 1, 2)
    up = up[0]
    q, info, target = call(
        windows_kernel,
        (pltpu.VMEM((PATCHES, WIN, KCAT), BF), pltpu.VMEM((8, WIN), F32), pltpu.VMEM((WIN, WIN), F32)),
        [V] * 2,
        (series.reshape(WIN, WIN), starts.reshape(1, WIN)),
        5 * US,
        1000,
        after=(packed,),
    )

    hops = [k for k in (1, 3, 8, 24) if k < members]
    steps = iter(hops)

    def hop(value, after=None):
        k = next(steps, None)
        if after is not None:
            value = lax.optimization_barrier((value, after))[0]
        return value if k is None else value + over_member(value, k)

    def hop_parts(value, after=None):
        k = next(steps, None)
        if after is not None:
            value = lax.optimization_barrier((value, after))[0]
        return value, jnp.zeros_like(value) if k is None else over_member(value, k)

    every, late = hop_parts(every)
    m24, ecat, every = call(
        lift_kernel,
        (pltpu.VMEM((32, HIDDEN), F32), pltpu.VMEM((4, KCAT, SHARD), BF), pltpu.VMEM((members, WIN), F32)),
        [V] * 7,
        (up, *shards, every, late),
        3 * US,
        1000,
        [pltpu.VMEM((4, 96, SHARD), BF)],
        after=(info,),
    )
    m24_peer = over_tensor(m24, 1)
    mcat_shape = pltpu.VMEM((KCAT, HIDDEN), BF)
    rstd, m_own = call(
        scale_kernel,
        (pltpu.VMEM((PATCHES, WIN, 128), F32), mcat_shape),
        [V] * 3,
        (q, ecat, m24),
        2 * US,
        1000,
    )

    def sums(group):
        rows = (group[1] - group[0]) * WIN
        return pltpu.VMEM((rows, 2 * HIDDEN), BF), pltpu.VMEM((rows, SHARD), BF)

    m_peer, act, send, give_y = call(
        first_away_kernel,
        (mcat_shape, *sums(GROUPS[0]), shard_bf),
        [V] * 6,
        (q, rstd, m_own, m24_peer, down[0], peer_x),
        4 * US,
        1000,
        [pltpu.SemaphoreType.DMA],
    )
    acts, crossed = [act], [over_tensor(send, 2)]
    fed = (q, rstd, m_own, m_peer, down[0], peer_x)
    peer_y = over_tensor(lax.optimization_barrier((give_y, send))[0], 1)
    for g in range(1, 4):
        last_one = g == 3
        out = call(
            functools.partial(counting_kernel if last_one else away_kernel, GROUPS[g]),
            sums(GROUPS[g]) + ((pltpu.VMEM((members, WIN), F32),) if last_one else ()),
            [V] * (8 if last_one else 6),
            fed + ((every, late) if last_one else ()),
            4 * US,
            1000,
            after=() if g == 1 else (crossed[1],) if last_one else (every, crossed[0]),
        )
        act, send = out[:2]
        acts.append(act)
        crossed.append(over_tensor(send, 2))
        if g == 1:
            every = hop(every, send)
            every, late = hop_parts(every)
    every = out[2]
    every, late = hop_parts(every, send)
    homes = (q, ecat, down[0], peer_y)
    (part,) = call(
        home_kernel,
        (pltpu.VMEM((GROUPS[1][1] * WIN, SHARD), F32),),
        [V] * 6,
        (*homes, *acts[:2]),
        US // 10,
        1000,
        after=(send,),
    )
    tail = (GROUPS[3][1] - GROUPS[3][0]) * WIN
    state, last, stats, shares = call(
        functools.partial(state_kernel, members, own),
        (
            pltpu.VMEM((GROUPS[2][1] * WIN, SHARD), F32),
            pltpu.VMEM((tail, SHARD), F32),
            pltpu.VMEM((2 * PATCHES, WIN), F32),
            pltpu.VMEM((8, WIN), F32),
        ),
        [V] * 13,
        (*homes, *acts[2:], part, *crossed[:3], info, every, late),
        5 * US,
        1000,
    )
    last, stats = call(
        last_state_kernel,
        (pltpu.VMEM((tail, SHARD), F32), pltpu.VMEM((2 * PATCHES, WIN), F32)),
        [V] * 3,
        (last, crossed[3], stats),
        US,
        1000,
    )
    features = SHARD
    for k in (1, 2):
        other = over_tensor(stats, k)
        gap = stats[:PATCHES] - other[:PATCHES]
        square = stats[PATCHES:] + other[PATCHES:] + (0.5 * features) * (gap * gap)
        stats = jnp.concatenate([0.5 * (stats[:PATCHES] + other[:PATCHES]), square], axis=0)
        features *= 2
    sent, held = call(
        head_kernel,
        (pltpu.VMEM((56, WIN), F32),) * 2,
        [V] * 6,
        (stats, state, last, heads, packed, shares),
        US,
        1000,
        [pltpu.VMEM((WIN, WIN), F32)],
    )
    total = held + over_tensor(sent, 1)
    total = total + over_tensor(total, 2)
    if members > 4:
        pairs = [(4 * m + t, 4 * (m ^ 4) + (t ^ 2)) for m in range(members) for t in range(4)]
        met = lax.ppermute(total, ("member", "tensor"), pairs)
    else:
        met = jnp.zeros_like(total)
    (total,) = call(weigh_kernel, (pltpu.VMEM((24, WIN), F32),), [V] * 2, (total, met), US, 1000)
    for ring in ((1, 2, 3), (8, 16, 24)):
        if ring[-1] < members:
            got = [over_member(total, k) for k in ring]
            total = total + got[0] + got[1] + got[2]

    levels = tuple(WIN * n // 100 for n in (50, 80, 90, 95))
    return call(
        functools.partial(rank_kernel, levels, own),
        (sds((own, 24), F32), sds((4, 24), F32)),
        [V] * 3,
        (total, info, target),
        US,
        1000,
        [pltpu.VMEM((WIN, WIN), F32), pltpu.VMEM((WIN, WIN), F32), pltpu.VMEM((24, WIN), F32)],
    )


def solution(mesh):
    placed = (
        P(),
        P(),
        P(None, "member"),
        P("member", None, "tensor"),
        P("member", None, "tensor"),
        P("member", "tensor"),
        P("member", None, "tensor"),
        P("member", "tensor", None),
        P("member", "tensor"),
        P("member", None, "tensor", None),
    )
    return jax.shard_map(
        per_device,
        mesh=mesh,
        in_specs=placed,
        out_specs=(P("member", "tensor"), P(None, "tensor")),
        check_vma=False,
    )
```
